256 devices in a mesh: term: 32 (over y, x, core), sec: 8 (over z).
Axes of the slice: x: 4, y: 4, z: 8, core: 2. Of those that a mesh axis runs over, the one named last changes fastest.
Arguments:
- psi: float32 [2, 1024, 1024], P(None, None, 'sec'), may hold values from -6 to 6
- diag: float32 [2, 1024, 1024], P(None, None, 'sec'), may hold values from 0.5 to 40
- block_dims: int32 [2, 2], replicated, may hold values from 512 to 1024, as said below
- left_env: bfloat16 [32, 2, 1024, 1024], P('term'), may hold values from -0.1875 to 0.1875
- right_env: bfloat16 [32, 2, 1024, 1024], P('term'), may hold values from -0.1875 to 0.1875
Outputs:
- new_psi: float32 [2, 1024, 1024], P(None, None, 'sec')
- energy: float32 [], replicated
The draws below stay inside these ranges and needn't reach their ends.
Inputs may be any that keep to these rules, and one draw needn't show every extreme that they name: `block_dims`: sector 0 uses the whole padded block; every other sector uses at least half of the rows and half of the columns.
All inputs are finite; a program needn't handle non-finite values.
Results may differ from the reference program's by a relative error of at most 0.0027.
The reference program's roundings to bfloat16 on the way (of `left`) count: a program that leaves them out, or rounds other values in their place, can miss the bound.
Values may be sent and summed in bfloat16 or wider, within the bound.
No kernel may reach another device: no remote copies, remote signals or barrier semaphores. Data moves between devices by JAX's collectives and lax.ppermute only.
A program may use at most 64 MiB of HBM per device.

```python
import math
import jax
import jax.numpy as jnp
from jax import lax

BLK = 1024
SECTORS = 2
ITERS = 2
TERMS = 32


def draw_block_dims(key, part):
    key = jax.random.fold_in(key, 11)
    sizes_drawn = jax.random.randint(key, (SECTORS, 2), BLK // 2, BLK + 1, dtype=jnp.int32)
    return sizes_drawn.at[0, :].set(BLK)


def column_rise(key, low, high, factor):
    rough = jax.random.uniform(key, (SECTORS, BLK, BLK), jnp.float32, low, high)
    columns = jnp.arange(BLK, dtype=jnp.float32) / BLK
    return rough * jnp.exp(math.log(factor) * columns)[None, None, :]


def draw_diag(key, part):
    key = jax.random.fold_in(key, 23)
    return column_rise(key, 0.5, 4.0, 6.0)


def shard_levels(key, shape, shards, least, largest):
    def one(position, blocks):
        draws = jax.random.uniform(jax.random.fold_in(jax.random.fold_in(key, 6), position), (blocks,), jnp.float32, least / len(shards), largest / len(shards))
        return jnp.repeat(jnp.exp(draws), shape[position] // blocks).reshape((-1,) + (1,) * (len(shape) - position - 1))

    gain = one(*shards[0])
    for cut in shards[1:]:
        gain = gain * one(*cut)
    return gain


def bell_draw(own_key, dims, scale, most, pieces=(), kind=jnp.bfloat16):
    array = scale * jax.random.normal(own_key, dims, jnp.float32)
    if pieces:
        array = array * shard_levels(own_key, dims, pieces, -0.22, 0.18)
    return jnp.clip(array, -most, most).astype(kind)


def setup_inputs(seed: int = 0) -> dict:
    key_of = jax.random.split(jax.random.key(seed), 6)
    psi = bell_draw(key_of[0], (SECTORS, BLK, BLK), 1.0, 6.0, ((2, 8),), jnp.float32)
    diag = draw_diag(jax.random.fold_in(key_of[5], 71), 0)
    block_dims = draw_block_dims(jax.random.fold_in(key_of[5], 71), 0)
    left_env = bell_draw(key_of[3], (TERMS, SECTORS, BLK, BLK), BLK ** -0.5, 0.1875, ((0, 32),))
    right_env = bell_draw(key_of[4], (TERMS, SECTORS, BLK, BLK), BLK ** -0.5, 0.1875, ((0, 32),))
    return {"psi": psi, "diag": diag, "block_dims": block_dims, "left_env": left_env, "right_env": right_env}


def inner(first, second):
    return jnp.sum(first * second) / (BLK * BLK)

def apply_ham(field, left_env, right_env, mask):
    field_low = field.astype(jnp.bfloat16).astype(jnp.float32)

    def one_term(total, envs):
        left_w, right_w = envs
        left = jnp.einsum('sik,skc->sic', left_w.astype(jnp.float32), field_low).astype(jnp.bfloat16)
        total = total + jnp.einsum('sic,sjc->sij', left.astype(jnp.float32), right_w.astype(jnp.float32))
        return (total, None)
    start = jnp.zeros(field.shape, jnp.float32)
    total, _ = lax.scan(one_term, start, (left_env, right_env))
    return total * mask

def reference(psi, diag, block_dims, left_env, right_env):
    positions = jnp.arange(BLK, dtype=jnp.int32)
    row_ok = positions[None, :, None] < block_dims[:, 0][:, None, None]
    col_ok = positions[None, None, :] < block_dims[:, 1][:, None, None]
    mask = (row_ok & col_ok).astype(jnp.float32)
    start = psi * mask
    vector = start / jnp.sqrt(inner(start, start))
    image = apply_ham(vector, left_env, right_env, mask)
    lowest = jnp.float32(0.0)
    for step in range(ITERS):
        theta = inner(vector, image)
        corr = (image - theta * vector) / (1.0 + jnp.abs(diag - theta))
        orth = corr - inner(vector, corr) * vector
        fresh = orth / jnp.sqrt(inner(orth, orth))
        fresh_image = apply_ham(fresh, left_env, right_env, mask)
        cross = 0.5 * (inner(vector, fresh_image) + inner(fresh, image))
        corner = inner(fresh, fresh_image)
        lowest = 0.5 * (theta + corner) - jnp.sqrt((0.5 * (theta - corner)) ** 2 + cross * cross)
        weight_old = corner - lowest
        weight_new = -cross
        scale_sum = jnp.sqrt(weight_old * weight_old + weight_new * weight_new)
        weight_old = weight_old / scale_sum
        weight_new = weight_new / scale_sum
        vector = weight_old * vector + weight_new * fresh
        image = weight_old * image + weight_new * fresh_image
    return (vector, lowest)
```

```python
import jax
import jax.numpy as jnp
from jax import lax
from jax.sharding import Mesh, PartitionSpec as P

ITERS = 2
XY = ("y", "x")
CZ = ("core", "sec")


def pick(array, index, axis=0):
    return lax.dynamic_index_in_dim(array, index, axis, keepdims=False)


def lanes(values, rows, width):
    lane = lax.broadcasted_iota(jnp.int32, (rows, width), 1)
    tile = jnp.zeros((rows, width), jnp.float32)
    for position, value in enumerate(values):
        tile = jnp.where(lane == position, value, tile)
    return tile


def make(n_y, n_x, n_z):
    n_xy = n_y * n_x

    def per_device(psi, diag, block_dims, left_env, right_env):
        _, size, cols = psi.shape
        sub = cols // n_xy
        scale = 1.0 / (size * size)
        core, z = lax.axis_index("core"), lax.axis_index("sec")
        q = lax.axis_index(XY)
        swap = [(0, 1), (1, 0)]

        left_got = lax.ppermute(pick(left_env[0], 1 - core), "core", swap)
        right_got = lax.ppermute(pick(right_env[0], 1 - core), "core", swap)
        lefts = (pick(left_env[0], core), left_got)
        rights = (pick(right_env[0], core), right_got)

        def a2a(array, axes):
            return lax.all_to_all(array, axes, 0, 0, tiled=True)

        def share_mask(dims):
            row = lax.broadcasted_iota(jnp.int32, (size, cols), 0)
            col = lax.broadcasted_iota(jnp.int32, (size, cols), 1) + z * cols
            return (row < dims[0]) & (col < dims[1])

        dims = pick(block_dims, core)
        shard = (n_z, sub, cols)
        shard_row = z * cols + q * sub + lax.broadcasted_iota(jnp.int32, shard, 1)
        shard_col = lax.broadcasted_iota(jnp.int32, shard, 0) * cols + lax.broadcasted_iota(jnp.int32, shard, 2)
        shard_mask = (shard_row < dims[0]) & (shard_col < dims[1])

        total = jnp.float32(0.0)
        for s in range(psi.shape[0]):
            total = total + jnp.sum(jnp.where(share_mask(block_dims[s]), psi[s] * psi[s], 0.0))
        psi_a = jnp.where(share_mask(dims), pick(psi, core), 0.0)
        diag_a = pick(diag, core)

        def own_rows(array):
            return pick(array.reshape(n_z, n_xy, sub, cols), q, 1)

        first = jnp.concatenate(
            [own_rows(psi_a), own_rows(diag_a), jnp.broadcast_to(total * scale, shard)], axis=1
        )
        first = a2a(first, "sec")
        inverse = 1.0 / jnp.sqrt(jnp.sum(first[:, 2 * sub, 0]))
        u_a, u_b = psi_a * inverse, first[:, :sub] * inverse
        diag_b = first[:, sub : 2 * sub]

        def apply_ham(field):
            field = field.astype(jnp.bfloat16)
            parts = [
                jnp.dot(env, field, preferred_element_type=jnp.float32)
                .astype(jnp.bfloat16)
                .reshape(n_z, 1, cols, cols)
                for env in lefts
            ]
            moved = a2a(jnp.concatenate(parts, axis=1), "sec")
            partial = jnp.zeros((cols, size), jnp.float32)
            for w, env in enumerate(rights):
                rows = moved[:, w].transpose(1, 0, 2).reshape(cols, size)
                partial = partial + lax.dot_general(
                    rows, env, (((1,), (1,)), ((), ())), preferred_element_type=jnp.float32
                )
            got = a2a(partial.reshape(n_xy, sub, size), XY)
            image = jnp.sum(got, axis=0).reshape(sub, n_z, cols).transpose(1, 0, 2)
            return jnp.where(shard_mask, image, 0.0)

        def dot_b(first, second):
            return jnp.sum(first * second) * scale

        def gather(image_b, values):
            block = jnp.concatenate(
                [image_b, jnp.broadcast_to(lanes(values, 8, cols)[None], (n_z, 8, cols))], axis=1
            )
            got = a2a(jnp.broadcast_to(block[None], (2,) + block.shape).reshape(2 * n_z, sub + 8, cols), CZ)
            sums = jnp.sum(got[:, sub:], axis=0)
            mine = pick(got.reshape(2, n_z, sub + 8, cols), core)[:, :sub].reshape(n_z * sub, cols)
            block = jnp.concatenate([mine, sums], axis=0)
            got = a2a(jnp.broadcast_to(block[None], (n_xy,) + block.shape), XY)
            sums = jnp.sum(got[:, n_z * sub], axis=0)
            image_a = got[:, : n_z * sub].reshape(n_xy, n_z, sub, cols).transpose(1, 0, 2, 3)
            return image_a.reshape(size, cols), [sums[k] for k in range(len(values))]

        def sum_cz(values):
            tile = lanes(values, 8, cols)
            got = a2a(jnp.broadcast_to(tile[None], (2 * n_z, 8, cols)), CZ)
            sums = jnp.sum(got[:, 0], axis=0)
            return [sums[k] for k in range(len(values))]

        def sum_all(values):
            tile = lanes(values, 8, cols)
            got = a2a(jnp.broadcast_to(tile[None], (2 * n_z, 8, cols)), CZ)
            got = a2a(jnp.broadcast_to(jnp.sum(got, axis=0)[None], (n_xy, 8, cols)), XY)
            sums = jnp.sum(got[:, 0], axis=0)
            return [sums[k] for k in range(len(values))]

        hu_b = apply_ham(u_a)
        hu_a, (theta,) = gather(hu_b, [dot_b(u_b, hu_b)])
        for step in range(ITERS):
            corr_a = (hu_a - theta * u_a) / (1.0 + jnp.abs(diag_a - theta))
            corr_b = (hu_b - theta * u_b) / (1.0 + jnp.abs(diag_b - theta))
            project, size_corr, size_u = sum_cz(
                [dot_b(u_a, corr_a), dot_b(corr_a, corr_a), dot_b(u_a, u_a)]
            )
            inverse = 1.0 / jnp.sqrt(size_corr - project * project * (2.0 - size_u))
            v_a = (corr_a - project * u_a) * inverse
            v_b = (corr_b - project * u_b) * inverse
            if step == ITERS - 1:
                u_far = lax.ppermute(u_a, "core", swap)
                v_far = lax.ppermute(v_a, "core", swap)
            hv_b = apply_ham(v_a)
            sums = [dot_b(u_b, hv_b), dot_b(v_b, hu_b), dot_b(v_b, hv_b)]
            if step < ITERS - 1:
                hv_a, sums = gather(hv_b, sums)
            else:
                sums = sum_all(sums)
            cross, corner = 0.5 * (sums[0] + sums[1]), sums[2]
            lowest = 0.5 * (theta + corner) - jnp.sqrt((0.5 * (theta - corner)) ** 2 + cross * cross)
            x, y = corner - lowest, -cross
            length = jnp.sqrt(x * x + y * y)
            x, y = x / length, y / length
            theta = x * x * theta + 2.0 * x * y * cross + y * y * corner
            u_a = x * u_a + y * v_a
            if step < ITERS - 1:
                u_b = x * u_b + y * v_b
                hu_a, hu_b = x * hu_a + y * hv_a, x * hu_b + y * hv_b
        far = x * u_far + y * v_far
        out = jnp.stack([jnp.where(core == 0, u_a, far), jnp.where(core == 0, far, u_a)])
        return out, lowest

    return per_device


def solution(mesh):
    n_z = mesh.shape["sec"]
    n_y = n_x = int(round((mesh.shape["term"] // 2) ** 0.5))
    fine = Mesh(mesh.devices.reshape(n_y, n_x, 2, n_z), ("y", "x", "core", "sec"))
    term = ("y", "x", "core")
    in_specs = (
        P(None, None, "sec"),
        P(None, None, "sec"),
        P(),
        P(term, None, None, None),
        P(term, None, None, None),
    )
    out_specs = (P(None, None, "sec"), P())
    return jax.shard_map(
        make(n_y, n_x, n_z), mesh=fine, in_specs=in_specs, out_specs=out_specs, check_vma=False
    )
```

```python
import functools

import jax
import jax.numpy as jnp
from jax import lax
from jax.experimental import pallas as pl
from jax.experimental.pallas import tpu as pltpu
from jax.sharding import Mesh, PartitionSpec as P

ITERS = 2
XY = ("y", "x")
CZ = ("core", "sec")
LANES = 128
PIECE = 256
F32 = jnp.float32
BF16 = jnp.bfloat16
SMEM = pl.BlockSpec(memory_space=pltpu.SMEM)
ANY = pl.BlockSpec(memory_space=pl.ANY)
VMEM = pl.BlockSpec(memory_space=pltpu.VMEM)


def call(kernel, outs, ins, scratch=(), flops=0):
    moved = sum(int(a.size) * a.dtype.itemsize for a, _ in ins)
    return pl.pallas_call(
        kernel,
        out_shape=[jax.ShapeDtypeStruct(s, d) for s, d in outs],
        in_specs=[s for _, s in ins],
        out_specs=[VMEM] * len(outs),
        scratch_shapes=list(scratch),
        compiler_params=pltpu.CompilerParams(vmem_limit_bytes=24 * 2**20),
        cost_estimate=pl.CostEstimate(flops=flops, bytes_accessed=moved, transcendentals=0),
    )(*[a for a, _ in ins])


def fold(product):
    parts = [product[:, k : k + LANES] for k in range(0, product.shape[1], LANES)]
    return jnp.sum(functools.reduce(lambda a, b: a + b, parts), axis=0, keepdims=True)


def tile_of(rows):
    return jnp.concatenate(rows + [jnp.zeros((8 - len(rows), LANES), F32)], axis=0)


def scalars(tile, count, scale):
    sums = jnp.sum(tile, axis=1, keepdims=True) * scale
    return [sums[k : k + 1] for k in range(count)]


def make(n_y, n_x, n_z):
    n_xy = n_y * n_x

    def per_device(psi, diag, block_dims, left_env, right_env):
        sectors, size, cols = psi.shape
        sub = cols // n_xy
        shard_rows = n_z * sub
        scale = 1.0 / (size * size)
        core = lax.axis_index("core")
        swap = [(0, 1), (1, 0)]
        ids = jnp.stack([core, lax.axis_index("sec"), lax.axis_index(XY)]).astype(jnp.int32)
        share, shard = (size, cols), (sub, size)

        def a2a(array, axes):
            return lax.all_to_all(array, axes, 0, 0, tiled=True)

        def share_mask(dims_ref, ids_ref, sector):
            row = lax.broadcasted_iota(jnp.int32, share, 0)
            col = lax.broadcasted_iota(jnp.int32, share, 1) + ids_ref[1] * cols
            return (row < dims_ref[sector, 0]) & (col < dims_ref[sector, 1])

        def start_kernel(ids_ref, dims_ref, psi_ref, diag_ref, out_ref):
            total = jnp.zeros((1, LANES), F32)
            for s in range(sectors):
                own = psi_ref[s]
                total = total + fold(jnp.where(share_mask(dims_ref, ids_ref, s), own * own, 0.0))
            c, first = ids_ref[0], pl.multiple_of(ids_ref[2] * sub, sub)
            dims = (dims_ref[c, 0], dims_ref[c, 1])
            col = lax.broadcasted_iota(jnp.int32, (sub, cols), 1) + ids_ref[1] * cols
            row = lax.broadcasted_iota(jnp.int32, (sub, cols), 0) + first
            for k in range(n_z):
                rows = pl.ds(k * cols + first, sub)
                keep = (row + k * cols < dims[0]) & (col < dims[1])
                out_ref[k, :sub] = jnp.where(keep, psi_ref[c, rows], 0.0)
                out_ref[k, sub : 2 * sub] = diag_ref[c, rows]
                out_ref[k, 2 * sub :] = tile_of([total])

        def left_matmul(ids_ref, env_ref, got_ref, field, left_ref, buf, sems, copies):
            for k, copy in enumerate(copies):
                copy.wait()
                w, i = k % 2, k // 2
                rows = jnp.dot(buf[w, pl.ds(i * PIECE, PIECE)], field, preferred_element_type=F32)
                per = PIECE // cols
                left_ref[i * per : (i + 1) * per, w] = rows.astype(BF16).reshape(per, cols, cols)

        def env_copies(ids_ref, env_ref, got_ref, buf, sems):
            copies = []
            for i in range(size // PIECE):
                rows = pl.ds(i * PIECE, PIECE)
                for w, source in enumerate((env_ref.at[0, ids_ref[0]], got_ref)):
                    copy = pltpu.make_async_copy(source.at[rows], buf.at[w, rows], sems.at[w, i])
                    copy.start()
                    copies.append(copy)
            return copies

        def first_kernel(ids_ref, dims_ref, got_ref, psi_ref, env_ref, env2_ref, u_a_ref, u_b_ref, diag_b_ref, left_ref, buf, sems):
            copies = env_copies(ids_ref, env_ref, env2_ref, buf, sems)
            got = got_ref[...]
            (norm,) = scalars(jnp.sum(got[:, 2 * sub :], axis=0), 1, scale)
            inverse = 1.0 / jnp.sqrt(norm)
            u_a = jnp.where(share_mask(dims_ref, ids_ref, ids_ref[0]), psi_ref[ids_ref[0]], 0.0) * inverse
            u_a_ref[...] = u_a
            for k in range(n_z):
                lanes = slice(k * cols, (k + 1) * cols)
                u_b_ref[:, lanes] = got[k, :sub] * inverse
                diag_b_ref[:, lanes] = got[k, sub : 2 * sub]
            left_matmul(ids_ref, env_ref, env2_ref, u_a.astype(BF16), left_ref, buf, sems, copies)

        def fresh_kernel(ids_ref, got_ref, corr_a_ref, u_a_ref, corr_b_ref, u_b_ref, env_ref, env2_ref, v_a_ref, v_b_ref, left_ref, buf, sems):
            copies = env_copies(ids_ref, env_ref, env2_ref, buf, sems)
            project, size_corr, size_u = scalars(jnp.sum(got_ref[...], axis=0), 3, scale)
            inverse = 1.0 / jnp.sqrt(size_corr - project * project * (2.0 - size_u))
            v_a = (corr_a_ref[...] - project * u_a_ref[...]) * inverse
            v_a_ref[...] = v_a
            v_b_ref[...] = (corr_b_ref[...] - project * u_b_ref[...]) * inverse
            left_matmul(ids_ref, env_ref, env2_ref, v_a.astype(BF16), left_ref, buf, sems, copies)

        def right_kernel(ids_ref, moved_ref, env_ref, got_ref, out_ref, buf, sems):
            copies = env_copies(ids_ref, env_ref, got_ref, buf, sems)
            fields = [
                jnp.concatenate([moved_ref[k, w] for k in range(n_z)], axis=1) for w in range(2)
            ]
            for i in range(size // PIECE):
                rows = pl.ds(i * PIECE, PIECE)
                total = None
                for w in range(2):
                    copies[2 * i + w].wait()
                    part = lax.dot_general(
                        fields[w], buf[w, rows], (((1,), (1,)), ((), ())), preferred_element_type=F32
                    )
                    total = part if total is None else total + part
                out_ref[:, :, rows] = total.reshape(n_xy, sub, PIECE)

        def image_of(ids_ref, dims_ref, got_ref):
            c = ids_ref[0]
            image = jnp.sum(got_ref[...], axis=0)
            row = lax.broadcasted_iota(jnp.int32, shard, 0) + (ids_ref[1] * cols + ids_ref[2] * sub)
            col = lax.broadcasted_iota(jnp.int32, shard, 1)
            return jnp.where((row < dims_ref[c, 0]) & (col < dims_ref[c, 1]), image, 0.0)

        def dots_tile(image, u_b_ref, more):
            rows = [fold(u_b_ref[...] * image)]
            if more:
                rows += [fold(more[0][...] * more[1][...]), fold(more[0][...] * image)]
            return tile_of(rows)

        def image_kernel(ids_ref, dims_ref, got_ref, u_b_ref, *refs):
            *more, image_ref, out_ref = refs
            image = image_of(ids_ref, dims_ref, got_ref)
            image_ref[...] = image
            tile = dots_tile(image, u_b_ref, more)
            for k in range(n_z):
                for c in range(2):
                    out_ref[c * n_z + k, :sub] = image[:, k * cols : (k + 1) * cols]
                    out_ref[c * n_z + k, sub:] = tile

        def last_image_kernel(ids_ref, dims_ref, got_ref, u_b_ref, v_b_ref, hu_b_ref, out_ref):
            image = image_of(ids_ref, dims_ref, got_ref)
            tile = dots_tile(image, u_b_ref, (v_b_ref, hu_b_ref))
            out_ref[...] = jnp.broadcast_to(tile[None], out_ref.shape)

        def spread_kernel(ids_ref, got_ref, out_ref):
            first = ids_ref[0] * n_z
            tile = jnp.sum(got_ref[:, sub:], axis=0)
            for k in range(n_z):
                rows = got_ref[first + k, :sub]
                for j in range(n_xy):
                    out_ref[j, k * sub : (k + 1) * sub] = rows
            for j in range(n_xy):
                out_ref[j, shard_rows:] = tile

        def sums_kernel(got_ref, out_ref):
            tile = jnp.sum(got_ref[...], axis=0)
            out_ref[...] = jnp.broadcast_to(tile[None], out_ref.shape)

        def projected(theta, tile):
            one, two, corner = scalars(tile, 3, scale)
            cross = 0.5 * (one + two)
            half = 0.5 * (theta - corner)
            lowest = 0.5 * (theta + corner) - jnp.sqrt(half * half + cross * cross)
            x, y = corner - lowest, -cross
            length = jnp.sqrt(x * x + y * y)
            x, y = x / length, y / length
            theta = x * x * theta + 2.0 * x * y * cross + y * y * corner
            return x, y, theta, lowest

        def corr_out(theta, hu_a, u_a, diag_a, hu_b, u_b, diag_b, corr_a_ref, corr_b_ref, theta_ref, out_ref):
            corr_a = (hu_a - theta * u_a) / (1.0 + jnp.abs(diag_a - theta))
            corr_a_ref[...] = corr_a
            corr_b_ref[...] = (hu_b - theta * u_b) / (1.0 + jnp.abs(diag_b - theta))
            theta_ref[...] = jnp.broadcast_to(theta, theta_ref.shape)
            tile = tile_of([fold(u_a * corr_a), fold(corr_a * corr_a), fold(u_a * u_a)])
            out_ref[...] = jnp.broadcast_to(tile[None], out_ref.shape)

        def share_of(got_ref):
            got = got_ref[:, :shard_rows].reshape(n_xy, n_z, sub, cols)
            return jnp.transpose(got, (1, 0, 2, 3)).reshape(share)

        def begin_kernel(ids_ref, got_ref, u_a_ref, u_b_ref, hu_b_ref, diag_ref, diag_b_ref, hu_a_ref, corr_a_ref, corr_b_ref, theta_ref, out_ref):
            (theta,) = scalars(jnp.sum(got_ref[:, shard_rows:], axis=0), 1, scale)
            hu_a = share_of(got_ref)
            hu_a_ref[...] = hu_a
            corr_out(theta, hu_a, u_a_ref[...], diag_ref[ids_ref[0]], hu_b_ref[...], u_b_ref[...], diag_b_ref[...], corr_a_ref, corr_b_ref, theta_ref, out_ref)

        def update_kernel(ids_ref, got_ref, old_theta_ref, u_a_ref, v_a_ref, hu_a_ref, u_b_ref, v_b_ref, hu_b_ref, hv_b_ref, diag_ref, diag_b_ref, u_a_out, hu_a_out, u_b_out, hu_b_out, corr_a_ref, corr_b_ref, theta_ref, out_ref):
            tile = jnp.sum(got_ref[:, shard_rows:], axis=0)
            x, y, theta, _ = projected(old_theta_ref[0:1, 0:1], tile)
            u_a = x * u_a_ref[...] + y * v_a_ref[...]
            hu_a = x * hu_a_ref[...] + y * share_of(got_ref)
            u_b = x * u_b_ref[...] + y * v_b_ref[...]
            hu_b = x * hu_b_ref[...] + y * hv_b_ref[...]
            u_a_out[...], hu_a_out[...] = u_a, hu_a
            u_b_out[...], hu_b_out[...] = u_b, hu_b
            corr_out(theta, hu_a, u_a, diag_ref[ids_ref[0]], hu_b, u_b, diag_b_ref[...], corr_a_ref, corr_b_ref, theta_ref, out_ref)

        def last_kernel(ids_ref, got_ref, theta_ref, u_a_ref, v_a_ref, u_far_ref, v_far_ref, out_ref, energy_ref):
            tile = jnp.sum(got_ref[...], axis=0)
            x, y, _, lowest = projected(theta_ref[0:1, 0:1], tile)
            c = ids_ref[0]
            out_ref[c] = x * u_a_ref[...] + y * v_a_ref[...]
            out_ref[1 - c] = x * u_far_ref[...] + y * v_far_ref[...]
            energy_ref[...] = jnp.broadcast_to(lowest, energy_ref.shape)

        def v(*arrays):
            return [(a, VMEM) for a in arrays]

        i_ids, i_dims = (ids, SMEM), (block_dims, SMEM)
        env_scratch = [pltpu.VMEM((2, size, size), BF16), pltpu.SemaphoreType.DMA((2, size // PIECE))]
        left_out = ((n_z, 2, cols, cols), BF16)
        small = ((2 * n_z, 8, cols), F32)
        tile_out = ((8, cols), F32)
        work = 4 * size * size * cols

        (first,) = call(start_kernel, [((n_z, 2 * sub + 8, cols), F32)], [i_ids, i_dims] + v(psi, diag))
        first, left_env, right_env = lax.optimization_barrier((first, left_env, right_env))
        other = lax.dynamic_index_in_dim(left_env[0], 1 - core, 0, keepdims=False)
        left_got = lax.ppermute(other, "core", swap)
        other = lax.dynamic_index_in_dim(right_env[0], 1 - core, 0, keepdims=False)
        right_got = lax.ppermute(other, "core", swap)
        first = a2a(first, "sec")
        i_lefts = [(left_env, ANY), (left_got, ANY)]
        i_rights = [(right_env, ANY), (right_got, ANY)]

        def apply_right(left):
            moved = a2a(left, "sec")
            (partial,) = call(right_kernel, [((n_xy, sub, size), F32)], [i_ids] + v(moved) + i_rights, env_scratch, work)
            return a2a(partial, XY)

        def gather(payload):
            payload = a2a(payload, CZ)
            (payload,) = call(spread_kernel, [((n_xy, shard_rows + 8, cols), F32)], [i_ids] + v(payload))
            return a2a(payload, XY)

        payload_out = ((2 * n_z, sub + 8, cols), F32)
        u_a, u_b, diag_b, left = call(
            first_kernel, [(share, F32), (shard, F32), (shard, F32), left_out],
            [i_ids, i_dims] + v(first, psi) + i_lefts, env_scratch, work,
        )
        got = apply_right(left)
        hu_b, payload = call(image_kernel, [(shard, F32), payload_out], [i_ids, i_dims] + v(got, u_b))
        got = gather(payload)
        hu_a, corr_a, corr_b, theta, sums = call(
            begin_kernel, [(share, F32), (share, F32), (shard, F32), tile_out, small],
            [i_ids] + v(got, u_a, u_b, hu_b, diag, diag_b),
        )
        for step in range(ITERS):
            sums = a2a(sums, CZ)
            v_a, v_b, left = call(
                fresh_kernel, [(share, F32), (shard, F32), left_out],
                [i_ids] + v(sums, corr_a, u_a, corr_b, u_b) + i_lefts, env_scratch, work,
            )
            got = apply_right(left)
            if step == ITERS - 1:
                break
            hv_b, payload = call(
                image_kernel, [(shard, F32), payload_out], [i_ids, i_dims] + v(got, u_b, v_b, hu_b)
            )
            got = gather(payload)
            u_a, hu_a, u_b, hu_b, corr_a, corr_b, theta, sums = call(
                update_kernel,
                [(share, F32), (share, F32), (shard, F32), (shard, F32), (share, F32), (shard, F32), tile_out, small],
                [i_ids] + v(got, theta, u_a, v_a, hu_a, u_b, v_b, hu_b, hv_b, diag, diag_b),
            )
        u_far = lax.ppermute(u_a, "core", swap)
        v_far = lax.ppermute(v_a, "core", swap)
        (sums,) = call(last_image_kernel, [small], [i_ids, i_dims] + v(got, u_b, v_b, hu_b))
        sums = a2a(sums, CZ)
        (sums,) = call(sums_kernel, [((n_xy, 8, cols), F32)], v(sums))
        sums = a2a(sums, XY)
        out, energy = call(
            last_kernel, [(psi.shape, F32), tile_out], [i_ids] + v(sums, theta, u_a, v_a, u_far, v_far)
        )
        return out, energy[0, 0]

    return per_device


def solution(mesh):
    n_z = mesh.shape["sec"]
    n_y = n_x = int(round((mesh.shape["term"] // 2) ** 0.5))
    fine = Mesh(mesh.devices.reshape(n_y, n_x, 2, n_z), ("y", "x", "core", "sec"))
    term = ("y", "x", "core")
    in_specs = (
        P(None, None, "sec"),
        P(None, None, "sec"),
        P(),
        P(term, None, None, None),
        P(term, None, None, None),
    )
    out_specs = (P(None, None, "sec"), P())
    return jax.shard_map(
        make(n_y, n_x, n_z), mesh=fine, in_specs=in_specs, out_specs=out_specs, check_vma=False
    )
```

```python
import functools

import jax
import jax.numpy as jnp
from jax import lax
from jax.experimental import pallas as pl
from jax.experimental.pallas import tpu as pltpu
from jax.sharding import Mesh, PartitionSpec as P

ITERS = 2
XY = ("y", "x")
CZ = ("core", "sec")
ALL = ("y", "x", "core", "sec")
LANES = 128
PIECE = 256
F32 = jnp.float32
BF16 = jnp.bfloat16
SMEM = pl.BlockSpec(memory_space=pltpu.SMEM)
HBM = pl.BlockSpec(memory_space=pltpu.HBM)
VMEM = pl.BlockSpec(memory_space=pltpu.VMEM)


def call(kernel, outs, ins, scratch=(), flops=0):
    moved = sum(int(a.size) * a.dtype.itemsize for a, _ in ins)
    return pl.pallas_call(
        kernel,
        out_shape=[jax.ShapeDtypeStruct(s, d) for s, d in outs],
        in_specs=[s for _, s in ins],
        out_specs=[VMEM] * len(outs),
        scratch_shapes=list(scratch),
        compiler_params=pltpu.CompilerParams(vmem_limit_bytes=24 * 2**20),
        cost_estimate=pl.CostEstimate(flops=flops, bytes_accessed=moved, transcendentals=0),
    )(*[a for a, _ in ins])


def fold(product):
    parts = [product[:, k : k + LANES] for k in range(0, product.shape[1], LANES)]
    return jnp.sum(functools.reduce(lambda a, b: a + b, parts), axis=0, keepdims=True)


def tile_of(rows):
    return jnp.concatenate(rows + [jnp.zeros((8 - len(rows), LANES), F32)], axis=0)


def make(n_y, n_x, n_z):
    n_xy = n_y * n_x

    def per_device(psi, diag, block_dims, left_env, right_env):
        sectors, size, cols = psi.shape
        sub = cols // n_xy
        shard_rows = n_z * sub
        scale = 1.0 / (size * size)
        core = lax.axis_index("core")
        swap = [(0, 1), (1, 0)]
        meta = jnp.stack(
            [core, lax.axis_index("sec"), lax.axis_index(XY)]
            + [block_dims[s, k] for s in range(sectors) for k in range(2)]
        ).astype(jnp.int32)
        share, shard = (size, cols), (sub, size)

        def a2a(array, axes):
            return lax.all_to_all(array, axes, 0, 0, tiled=True)

        def dims_of(meta_ref, sector):
            return meta_ref[3 + 2 * sector], meta_ref[4 + 2 * sector]

        def share_mask(meta_ref, sector):
            row = lax.broadcasted_iota(jnp.int32, share, 0)
            col = lax.broadcasted_iota(jnp.int32, share, 1) + meta_ref[1] * cols
            rows, columns = dims_of(meta_ref, sector)
            return (row < rows) & (col < columns)

        def start_kernel(meta_ref, psi_ref, diag_ref, out_ref, psi_a_ref, buf, sems):
            core, q = meta_ref[0], meta_ref[2]
            copies = [
                pltpu.make_async_copy(psi_ref.at[s], buf.at[s], sems.at[s]) for s in range(sectors)
            ]
            copies.append(
                pltpu.make_async_copy(diag_ref.at[core, :, q], out_ref.at[:, pl.ds(sub, sub)], sems.at[sectors])
            )
            for copy in copies:
                copy.start()
            total = jnp.zeros((1, LANES), F32)
            for s in range(sectors):
                copies[s].wait()
                own = jnp.where(share_mask(meta_ref, s), buf[s], 0.0)
                total = total + fold(own * own)

                @pl.when(core == s)
                def _():
                    psi_a_ref[...] = own

            first = pl.multiple_of(q * sub, sub)
            for k in range(n_z):
                out_ref[k, :sub] = psi_a_ref[pl.ds(k * cols + first, sub)]
                out_ref[k, 2 * sub :] = tile_of([total])
            copies[sectors].wait()

        def left_matmul(meta_ref, env_ref, got_ref, field, left_ref):
            core, per = meta_ref[0], PIECE // cols
            for i in range(size // PIECE):
                rows = pl.ds(i * PIECE, PIECE)
                for w in range(2):
                    env = env_ref[0, core, rows] if w == 0 else got_ref[rows]
                    part = jnp.dot(env, field, preferred_element_type=F32)
                    left_ref[i * per : (i + 1) * per, w] = part.astype(BF16).reshape(per, cols, cols)

        def first_kernel(meta_ref, got_ref, psi_a_ref, env_ref, env2_ref, u_a_ref, u_b_ref, diag_b_ref, left_ref):
            got = got_ref[...]
            norm = jnp.sum(jnp.sum(got[:, 2 * sub :], axis=0), axis=(0, 1), keepdims=True) * scale
            inverse = 1.0 / jnp.sqrt(norm)
            u_a = psi_a_ref[...] * inverse
            u_a_ref[...] = u_a
            for k in range(n_z):
                lanes = slice(k * cols, (k + 1) * cols)
                u_b_ref[:, lanes] = got[k, :sub] * inverse
                diag_b_ref[:, lanes] = got[k, sub : 2 * sub]
            left_matmul(meta_ref, env_ref, env2_ref, u_a.astype(BF16), left_ref)

        def right_kernel(meta_ref, moved_ref, env_ref, got_ref, out_ref):
            core = meta_ref[0]
            fields = [
                jnp.concatenate([moved_ref[k, w] for k in range(n_z)], axis=1) for w in range(2)
            ]
            for i in range(size // PIECE):
                rows = pl.ds(i * PIECE, PIECE)
                total = None
                for w in range(2):
                    env = env_ref[0, core, rows] if w == 0 else got_ref[rows]
                    part = lax.dot_general(
                        fields[w], env, (((1,), (1,)), ((), ())), preferred_element_type=F32
                    )
                    total = part if total is None else total + part
                out_ref[:, :, rows] = total.reshape(n_xy, sub, PIECE).astype(out_ref.dtype)

        def image_of(meta_ref, got_ref):
            image = jnp.sum(got_ref[...].astype(F32), axis=0)
            row = lax.broadcasted_iota(jnp.int32, shard, 0) + (meta_ref[1] * cols + meta_ref[2] * sub)
            col = lax.broadcasted_iota(jnp.int32, shard, 1)
            rows, columns = dims_of(meta_ref, meta_ref[0])
            return jnp.where((row < rows) & (col < columns), image, 0.0)

        def dots_tile(image, u_b_ref, more):
            u = u_b_ref[...]
            if not more:
                return tile_of([fold(u * image)])
            corr, hu = more[0][...], more[1][...]
            pairs = [(u, image), (corr, hu), (corr, image), (u, corr), (corr, corr), (u, u)]
            return tile_of([fold(a * b) for a, b in pairs])

        def image_kernel(meta_ref, got_ref, u_b_ref, *refs):
            *more, image_ref, out_ref = refs
            image = image_of(meta_ref, got_ref)
            image_ref[...] = image
            tile = dots_tile(image, u_b_ref, more)
            for k in range(n_z):
                for c in range(2):
                    out_ref[c * n_z + k, :sub] = image[:, k * cols : (k + 1) * cols]
                    out_ref[c * n_z + k, sub:] = tile

        def last_image_kernel(meta_ref, got_ref, u_b_ref, corr_b_ref, hu_b_ref, out_ref):
            image = image_of(meta_ref, got_ref)
            tile = dots_tile(image, u_b_ref, (corr_b_ref, hu_b_ref))
            sums = jnp.sum(tile, axis=1, keepdims=True)
            row = lax.broadcasted_iota(jnp.int32, tile.shape, 0)
            lane = lax.broadcasted_iota(jnp.int32, tile.shape, 1)
            line = jnp.sum(jnp.where(row == lane, sums, 0.0), axis=0, keepdims=True)
            out_ref[...] = jnp.broadcast_to(line, out_ref.shape)

        def spread_kernel(meta_ref, got_ref, out_ref):
            first = meta_ref[0] * n_z
            tile = jnp.sum(got_ref[:, sub:], axis=0)
            for k in range(n_z):
                rows = got_ref[first + k, :sub]
                for j in range(n_xy):
                    out_ref[j, k * sub : (k + 1) * sub] = rows
            for j in range(n_xy):
                out_ref[j, shard_rows:] = tile

        def projected(theta, sums):
            u_image, corr_hu, corr_image, project, size_corr, size_u = sums
            inverse = 1.0 / jnp.sqrt(size_corr - project * project * (2.0 - size_u))
            cross = 0.5 * ((u_image - project * theta) + (corr_hu - project * theta)) * inverse
            corner = corr_image - project * (corr_hu + u_image) + project * project * theta
            corner = corner * inverse * inverse
            half = 0.5 * (theta - corner)
            lowest = 0.5 * (theta + corner) - jnp.sqrt(half * half + cross * cross)
            x, y = corner - lowest, -cross
            length = jnp.sqrt(x * x + y * y)
            x, y = x / length, y / length
            theta = x * x * theta + 2.0 * x * y * cross + y * y * corner
            return x - y * project * inverse, y * inverse, theta, lowest

        def sums_of(got_ref, count):
            tile = jnp.sum(got_ref[:, shard_rows:], axis=0)
            sums = jnp.sum(tile, axis=1, keepdims=True) * scale
            return [sums[k : k + 1] for k in range(count)]

        def correction(theta, image, vector, diagonal):
            return (image - theta * vector) / (1.0 + jnp.abs(diagonal - theta))

        def share_of(got_ref):
            got = got_ref[:, :shard_rows].reshape(n_xy, n_z, sub, cols)
            return jnp.transpose(got, (1, 0, 2, 3)).reshape(share)

        def begin_kernel(meta_ref, got_ref, u_a_ref, u_b_ref, hu_b_ref, diag_ref, diag_b_ref, env_ref, env2_ref, hu_a_ref, corr_a_ref, corr_b_ref, theta_ref, left_ref):
            (theta,) = sums_of(got_ref, 1)
            theta_ref[...] = jnp.broadcast_to(theta, theta_ref.shape)
            hu_a = share_of(got_ref)
            hu_a_ref[...] = hu_a
            corr_a = correction(theta, hu_a, u_a_ref[...], diag_ref[meta_ref[0]])
            corr_a_ref[...] = corr_a
            corr_b_ref[...] = correction(theta, hu_b_ref[...], u_b_ref[...], diag_b_ref[...])
            left_matmul(meta_ref, env_ref, env2_ref, corr_a.astype(BF16), left_ref)

        def update_kernel(meta_ref, got_ref, old_theta_ref, u_a_ref, corr_a_ref, hu_a_ref, u_b_ref, corr_b_ref, hu_b_ref, hc_b_ref, diag_ref, diag_b_ref, env_ref, env2_ref, u_a_out, corr_a_out, hu_a_out, u_b_out, corr_b_out, hu_b_out, theta_ref, left_ref):
            one, two, theta, _ = projected(old_theta_ref[0:1, 0:1], sums_of(got_ref, 6))
            theta_ref[...] = jnp.broadcast_to(theta, theta_ref.shape)
            u_a = one * u_a_ref[...] + two * corr_a_ref[...]
            hu_a = one * hu_a_ref[...] + two * share_of(got_ref)
            corr_a = correction(theta, hu_a, u_a, diag_ref[meta_ref[0]])
            u_a_out[...], hu_a_out[...], corr_a_out[...] = u_a, hu_a, corr_a
            u_b = one * u_b_ref[...] + two * corr_b_ref[...]
            hu_b = one * hu_b_ref[...] + two * hc_b_ref[...]
            u_b_out[...], hu_b_out[...] = u_b, hu_b
            corr_b_out[...] = correction(theta, hu_b, u_b, diag_b_ref[...])
            left_matmul(meta_ref, env_ref, env2_ref, corr_a.astype(BF16), left_ref)

        def last_kernel(meta_ref, got_ref, theta_ref, u_a_ref, corr_a_ref, u_far_ref, corr_far_ref, out_ref, energy_ref):
            line = jnp.sum(got_ref[...], axis=0, keepdims=True) * scale
            sums = [line[:, k : k + 1] for k in range(6)]
            one, two, _, lowest = projected(theta_ref[0:1, 0:1], sums)
            c = meta_ref[0]
            out_ref[c] = one * u_a_ref[...] + two * corr_a_ref[...]
            out_ref[1 - c] = one * u_far_ref[...] + two * corr_far_ref[...]
            energy_ref[...] = lowest

        def v(*arrays):
            return [(a, VMEM) for a in arrays]

        i_meta = [(meta, SMEM)]
        left_out = ((n_z, 2, cols, cols), BF16)
        tile_out, a_out, b_out = ((8, cols), F32), (share, F32), (shard, F32)
        work = 4 * size * size * cols

        first, psi_a = call(
            start_kernel,
            [((n_z, 2 * sub + 8, cols), F32), a_out],
            i_meta + [(psi, HBM), (diag.reshape(sectors, n_z, n_xy, sub, cols), HBM)],
            [pltpu.VMEM(psi.shape, F32), pltpu.SemaphoreType.DMA((sectors + 1,))],
        )

        def swapped(env):
            other = lax.dynamic_index_in_dim(env[0], 1 - core, 0, keepdims=False)
            return lax.ppermute(other, "core", swap)

        first, left_env = lax.optimization_barrier((first, left_env))
        lefts = v(left_env, swapped(left_env))
        first = a2a(first, "sec")
        u_a, u_b, diag_b, left = call(
            first_kernel, [a_out, b_out, b_out, left_out], i_meta + v(first, psi_a) + lefts, (), work
        )
        left, right_env = lax.optimization_barrier((left, right_env))
        rights = v(right_env, swapped(right_env))

        def apply_right(left, kind):
            moved = a2a(left, "sec")
            (partial,) = call(
                right_kernel, [((n_xy, sub, size), kind)], i_meta + v(moved) + rights, (), work
            )
            return a2a(partial, XY)

        def gather(payload):
            payload = a2a(payload, CZ)
            (payload,) = call(spread_kernel, [((n_xy, shard_rows + 8, cols), F32)], i_meta + v(payload))
            return a2a(payload, XY)

        payload_out = ((2 * n_z, sub + 8, cols), F32)
        got = apply_right(left, F32)
        hu_b, payload = call(image_kernel, [b_out, payload_out], i_meta + v(got, u_b))
        got = gather(payload)
        hu_a, corr_a, corr_b, theta, left = call(
            begin_kernel,
            [a_out, a_out, b_out, tile_out, left_out],
            i_meta + v(got, u_a, u_b, hu_b, diag, diag_b) + lefts, (), work,
        )
        for _ in range(ITERS - 1):
            got = apply_right(left, F32)
            hc_b, payload = call(
                image_kernel, [b_out, payload_out], i_meta + v(got, u_b, corr_b, hu_b)
            )
            got = gather(payload)
            u_a, corr_a, hu_a, u_b, corr_b, hu_b, theta, left = call(
                update_kernel,
                [a_out, a_out, a_out, b_out, b_out, b_out, tile_out, left_out],
                i_meta + v(got, theta, u_a, corr_a, hu_a, u_b, corr_b, hu_b, hc_b, diag, diag_b) + lefts,
                (), work,
            )
        u_far = lax.ppermute(u_a, "core", swap)
        corr_far = lax.ppermute(corr_a, "core", swap)
        got = apply_right(left, BF16)
        (sums,) = call(
            last_image_kernel, [((2 * n_z * n_xy, cols), F32)], i_meta + v(got, u_b, corr_b, hu_b)
        )
        sums = a2a(sums, ALL)
        out, energy = call(
            last_kernel, [(psi.shape, F32), ((1, 1), F32)],
            i_meta + v(sums, theta, u_a, corr_a, u_far, corr_far),
        )
        return out, energy.reshape(())

    return per_device


def solution(mesh):
    n_z = mesh.shape["sec"]
    n_y = n_x = int(round((mesh.shape["term"] // 2) ** 0.5))
    fine = Mesh(mesh.devices.reshape(n_y, n_x, 2, n_z), ("y", "x", "core", "sec"))
    term = ("y", "x", "core")
    in_specs = (
        P(None, None, "sec"),
        P(None, None, "sec"),
        P(),
        P(term, None, None, None),
        P(term, None, None, None),
    )
    out_specs = (P(None, None, "sec"), P())
    return jax.shard_map(
        make(n_y, n_x, n_z), mesh=fine, in_specs=in_specs, out_specs=out_specs, check_vma=False
    )
```

```python
import functools

import jax
import jax.numpy as jnp
from jax import lax
from jax.experimental import pallas as pl
from jax.experimental.pallas import tpu as pltpu
from jax.sharding import Mesh, PartitionSpec as P

ITERS = 2
XY = ("y", "x")
CZ = ("core", "sec")
ALL = ("y", "x", "core", "sec")
LANES = 128
PIECE = 256
LIMIT = 24
START = 4 * 10**9
F32 = jnp.float32
BF16 = jnp.bfloat16
SMEM = pl.BlockSpec(memory_space=pltpu.SMEM)
VMEM = pl.BlockSpec(memory_space=pltpu.VMEM)


def call(kernel, outs, ins, scratch=(), flops=0):
    moved = sum(int(a.size) * a.dtype.itemsize for a, _ in ins)
    return pl.pallas_call(
        kernel,
        out_shape=[jax.ShapeDtypeStruct(s, d) for s, d in outs],
        in_specs=[s for _, s in ins],
        out_specs=[VMEM] * len(outs),
        scratch_shapes=list(scratch),
        compiler_params=pltpu.CompilerParams(vmem_limit_bytes=LIMIT * 2**20),
        cost_estimate=pl.CostEstimate(flops=flops, bytes_accessed=moved, transcendentals=0),
    )(*[a for a, _ in ins])


def fold(product):
    parts = [product[:, k : k + LANES] for k in range(0, product.shape[1], LANES)]
    return jnp.sum(functools.reduce(lambda a, b: a + b, parts), axis=0, keepdims=True)


def tile_of(rows):
    return jnp.concatenate(rows + [jnp.zeros((8 - len(rows), LANES), F32)], axis=0)


def make(n_y, n_x, n_z):
    n_xy = n_y * n_x

    def per_device(psi, diag, block_dims, left_env, right_env):
        sectors, size, cols = psi.shape
        sub = cols // n_xy
        shard_rows = n_z * sub
        scale = 1.0 / (size * size)
        core = lax.axis_index("core")
        swap = [(0, 1), (1, 0)]
        row = lax.broadcasted_iota(jnp.int32, (sectors + 2, 2), 0) - sectors
        col = lax.broadcasted_iota(jnp.int32, (sectors + 2, 2), 1)
        meta = jnp.where(
            row < 0,
            jnp.pad(block_dims, ((0, 2), (0, 0))),
            jnp.where(row > 0, lax.axis_index(XY), jnp.where(col == 0, core, lax.axis_index("sec"))),
        )
        share, shard = (size, cols), (sub, size)

        def a2a(array, axes):
            return lax.all_to_all(array, axes, 0, 0, tiled=True)

        def dims_of(meta_ref, sector):
            return meta_ref[sector, 0], meta_ref[sector, 1]

        def place(meta_ref):
            return meta_ref[sectors, 0], meta_ref[sectors, 1], meta_ref[sectors + 1, 0]

        def share_mask(meta_ref, sector):
            row = lax.broadcasted_iota(jnp.int32, share, 0)
            col = lax.broadcasted_iota(jnp.int32, share, 1) + place(meta_ref)[1] * cols
            rows, columns = dims_of(meta_ref, sector)
            return (row < rows) & (col < columns)

        def own_rows(meta_ref, k):
            return pl.ds(pl.multiple_of(k * cols + place(meta_ref)[2] * sub, sub), sub)

        def start_kernel(meta_ref, psi_ref, out_ref, psi_a_ref):
            total = jnp.zeros((1, LANES), F32)
            for s in range(sectors):
                own = jnp.where(share_mask(meta_ref, s), psi_ref[s], 0.0)
                total = total + fold(own * own)

                @pl.when(place(meta_ref)[0] == s)
                def _():
                    psi_a_ref[...] = own

            for k in range(n_z):
                out_ref[k, :sub] = psi_a_ref[own_rows(meta_ref, k)]
                out_ref[k, sub:] = tile_of([total])

        def left_matmul(meta_ref, env_ref, got_ref, field, left_ref):
            core, per = place(meta_ref)[0], PIECE // cols
            for i in range(size // PIECE):
                rows = pl.ds(i * PIECE, PIECE)
                for w in range(2):
                    env = env_ref[0, core, rows] if w == 0 else got_ref[rows]
                    part = jnp.dot(env, field, preferred_element_type=F32)
                    left_ref[i * per : (i + 1) * per, w] = part.astype(BF16).reshape(per, cols, cols)

        def first_kernel(meta_ref, got_ref, psi_a_ref, env_ref, env2_ref, u_a_ref, u_b_ref, left_ref):
            got = got_ref[...]
            norm = jnp.sum(jnp.sum(got[:, sub:], axis=0), axis=(0, 1), keepdims=True) * scale
            inverse = 1.0 / jnp.sqrt(norm)
            u_a = psi_a_ref[...] * inverse
            u_a_ref[...] = u_a
            for k in range(n_z):
                lanes = slice(k * cols, (k + 1) * cols)
                u_b_ref[:, lanes] = got[k, :sub] * inverse
            left_matmul(meta_ref, env_ref, env2_ref, u_a.astype(BF16), left_ref)

        def right_pieces(meta_ref, moved_ref, env_ref, got_ref):
            core = place(meta_ref)[0]
            fields = [
                jnp.concatenate([moved_ref[k, w] for k in range(n_z)], axis=1) for w in range(2)
            ]
            for i in range(size // PIECE):
                rows = pl.ds(i * PIECE, PIECE)
                total = None
                for w in range(2):
                    env = env_ref[0, core, rows] if w == 0 else got_ref[rows]
                    part = lax.dot_general(
                        fields[w], env, (((1,), (1,)), ((), ())), preferred_element_type=F32
                    )
                    total = part if total is None else total + part
                yield rows, total

        def right_kernel(meta_ref, moved_ref, env_ref, got_ref, out_ref):
            for rows, total in right_pieces(meta_ref, moved_ref, env_ref, got_ref):
                out_ref[:, :, rows] = total.reshape(n_xy, sub, PIECE).astype(out_ref.dtype)

        def image_of(meta_ref, got_ref):
            core, z, q = place(meta_ref)
            image = jnp.sum(got_ref[...].astype(F32), axis=0)
            row = lax.broadcasted_iota(jnp.int32, shard, 0) + (z * cols + q * sub)
            col = lax.broadcasted_iota(jnp.int32, shard, 1)
            rows, columns = dims_of(meta_ref, core)
            return jnp.where((row < rows) & (col < columns), image, 0.0)

        def dots_tile(image, u_b_ref, more):
            u = u_b_ref[...]
            if not more:
                return tile_of([fold(u * image)])
            corr, hu = more[0][...], more[1][...]
            pairs = [(u, image), (corr, hu), (corr, image), (u, corr), (corr, corr), (u, u)]
            return tile_of([fold(a * b) for a, b in pairs])

        def put_image(meta_ref, got_ref, u_b_ref, more, image_ref, out_ref):
            image = image_of(meta_ref, got_ref)
            image_ref[...] = image
            tile = dots_tile(image, u_b_ref, more)
            for k in range(n_z):
                for c in range(2):
                    out_ref[c * n_z + k, :sub] = image[:, k * cols : (k + 1) * cols]
                    out_ref[c * n_z + k, sub : sub + 8] = tile

        def first_image_kernel(meta_ref, got_ref, u_b_ref, diag_ref, image_ref, out_ref):
            put_image(meta_ref, got_ref, u_b_ref, (), image_ref, out_ref)
            core = place(meta_ref)[0]
            for k in range(n_z):
                out_ref[core * n_z + k, sub + 8 :] = diag_ref[core, own_rows(meta_ref, k)]
                out_ref[(1 - core) * n_z + k, sub + 8 :] = jnp.zeros((sub, cols), F32)

        def image_kernel(meta_ref, got_ref, u_b_ref, corr_b_ref, hu_b_ref, image_ref, out_ref):
            put_image(meta_ref, got_ref, u_b_ref, (corr_b_ref, hu_b_ref), image_ref, out_ref)

        def last_image_kernel(meta_ref, got_ref, u_b_ref, corr_b_ref, hu_b_ref, out_ref):
            image = image_of(meta_ref, got_ref)
            tile = dots_tile(image, u_b_ref, (corr_b_ref, hu_b_ref))
            sums = jnp.sum(tile, axis=1, keepdims=True)
            row = lax.broadcasted_iota(jnp.int32, tile.shape, 0)
            lane = lax.broadcasted_iota(jnp.int32, tile.shape, 1)
            line = jnp.sum(jnp.where(row == lane, sums, 0.0), axis=0, keepdims=True)
            out_ref[...] = jnp.broadcast_to(line, out_ref.shape)

        def spread_kernel(meta_ref, got_ref, out_ref, *diag_b_ref):
            first = place(meta_ref)[0] * n_z
            tile = jnp.sum(got_ref[:, sub : sub + 8], axis=0)
            for k in range(n_z):
                rows = got_ref[first + k, :sub]
                for j in range(n_xy):
                    out_ref[j, k * sub : (k + 1) * sub] = rows
                for ref in diag_b_ref:
                    ref[:, k * cols : (k + 1) * cols] = got_ref[first + k, sub + 8 :]
            for j in range(n_xy):
                out_ref[j, shard_rows:] = tile

        def projected(theta, sums):
            u_image, corr_hu, corr_image, project, size_corr, size_u = sums
            inverse = 1.0 / jnp.sqrt(size_corr - project * project * (2.0 - size_u))
            cross = 0.5 * ((u_image - project * theta) + (corr_hu - project * theta)) * inverse
            corner = corr_image - project * (corr_hu + u_image) + project * project * theta
            corner = corner * inverse * inverse
            half = 0.5 * (theta - corner)
            lowest = 0.5 * (theta + corner) - jnp.sqrt(half * half + cross * cross)
            x, y = corner - lowest, -cross
            length = jnp.sqrt(x * x + y * y)
            x, y = x / length, y / length
            theta = x * x * theta + 2.0 * x * y * cross + y * y * corner
            return x - y * project * inverse, y * inverse, theta, lowest

        def sums_of(got_ref, count):
            tile = jnp.sum(got_ref[:, shard_rows:], axis=0)
            sums = jnp.sum(tile, axis=1, keepdims=True) * scale
            return [sums[k : k + 1] for k in range(count)]

        def correction(theta, image, vector, diagonal):
            return (image - theta * vector) / (1.0 + jnp.abs(diagonal - theta))

        def share_of(got_ref):
            got = got_ref[:, :shard_rows].reshape(n_xy, n_z, sub, cols)
            return jnp.transpose(got, (1, 0, 2, 3)).reshape(share)

        def begin_kernel(meta_ref, got_ref, u_a_ref, u_b_ref, hu_b_ref, diag_ref, diag_b_ref, env_ref, env2_ref, hu_a_ref, corr_a_ref, corr_b_ref, theta_ref, left_ref):
            (theta,) = sums_of(got_ref, 1)
            theta_ref[...] = jnp.broadcast_to(theta, theta_ref.shape)
            hu_a = share_of(got_ref)
            hu_a_ref[...] = hu_a
            corr_a = correction(theta, hu_a, u_a_ref[...], diag_ref[place(meta_ref)[0]])
            corr_a_ref[...] = corr_a
            corr_b_ref[...] = correction(theta, hu_b_ref[...], u_b_ref[...], diag_b_ref[...])
            left_matmul(meta_ref, env_ref, env2_ref, corr_a.astype(BF16), left_ref)

        def update_kernel(meta_ref, got_ref, old_theta_ref, u_a_ref, corr_a_ref, hu_a_ref, u_b_ref, corr_b_ref, hu_b_ref, hc_b_ref, diag_ref, diag_b_ref, env_ref, env2_ref, u_a_out, corr_a_out, hu_a_out, u_b_out, corr_b_out, hu_b_out, theta_ref, left_ref):
            one, two, theta, _ = projected(old_theta_ref[0:1, 0:1], sums_of(got_ref, 6))
            theta_ref[...] = jnp.broadcast_to(theta, theta_ref.shape)
            u_a = one * u_a_ref[...] + two * corr_a_ref[...]
            hu_a = one * hu_a_ref[...] + two * share_of(got_ref)
            corr_a = correction(theta, hu_a, u_a, diag_ref[place(meta_ref)[0]])
            u_a_out[...], hu_a_out[...], corr_a_out[...] = u_a, hu_a, corr_a
            u_b = one * u_b_ref[...] + two * corr_b_ref[...]
            hu_b = one * hu_b_ref[...] + two * hc_b_ref[...]
            u_b_out[...], hu_b_out[...] = u_b, hu_b
            corr_b_out[...] = correction(theta, hu_b, u_b, diag_b_ref[...])
            left_matmul(meta_ref, env_ref, env2_ref, corr_a.astype(BF16), left_ref)

        def last_kernel(meta_ref, got_ref, theta_ref, u_a_ref, corr_a_ref, u_far_ref, corr_far_ref, out_ref, energy_ref):
            line = jnp.sum(got_ref[...], axis=0, keepdims=True) * scale
            sums = [line[:, k : k + 1] for k in range(6)]
            one, two, _, lowest = projected(theta_ref[0:1, 0:1], sums)
            c = place(meta_ref)[0]
            out_ref[c] = one * u_a_ref[...] + two * corr_a_ref[...]
            out_ref[1 - c] = one * u_far_ref[...] + two * corr_far_ref[...]
            energy_ref[...] = lowest

        def v(*arrays):
            return [(a, VMEM) for a in arrays]

        i_meta = [(meta, SMEM)]
        left_out = ((n_z, 2, cols, cols), BF16)
        tile_out, a_out, b_out = ((8, cols), F32), (share, F32), (shard, F32)
        work = 4 * size * size * cols

        first, psi_a = call(
            start_kernel, [((n_z, sub + 8, cols), F32), a_out], i_meta + v(psi), (), START
        )

        def swapped(env, other):
            give = lax.dynamic_slice(
                env, (0, other, 0, 0), (1, 1, size, size), allow_negative_indices=False
            )
            return lax.ppermute(give.reshape(size, size), "core", swap)

        first, left_env, other = lax.optimization_barrier((first, left_env, 1 - core))
        lefts = v(left_env, swapped(left_env, other))
        first = a2a(first, "sec")
        u_a, u_b, left = call(
            first_kernel, [a_out, b_out, left_out], i_meta + v(first, psi_a) + lefts, (), work
        )
        left, right_env = lax.optimization_barrier((left, right_env))
        rights = v(right_env, swapped(right_env, other))

        def apply_right(left, kind=F32):
            moved = a2a(left, "sec")
            (partial,) = call(
                right_kernel, [((n_xy, sub, size), kind)], i_meta + v(moved) + rights, (), work
            )
            return a2a(partial, XY)

        def gather(payload, *more):
            payload = a2a(payload, CZ)
            payload, *more = call(
                spread_kernel, [((n_xy, shard_rows + 8, cols), F32), *more], i_meta + v(payload)
            )
            return [a2a(payload, XY), *more]

        payload_out = ((2 * n_z, sub + 8, cols), F32)
        got = apply_right(left)
        hu_b, payload = call(
            first_image_kernel,
            [b_out, ((2 * n_z, 2 * sub + 8, cols), F32)],
            i_meta + v(got, u_b, diag),
        )
        got, diag_b = gather(payload, b_out)
        hu_a, corr_a, corr_b, theta, left = call(
            begin_kernel,
            [a_out, a_out, b_out, tile_out, left_out],
            i_meta + v(got, u_a, u_b, hu_b, diag, diag_b) + lefts, (), work,
        )
        for _ in range(ITERS - 1):
            got = apply_right(left)
            hc_b, payload = call(
                image_kernel, [b_out, payload_out], i_meta + v(got, u_b, corr_b, hu_b)
            )
            (got,) = gather(payload)
            u_a, corr_a, hu_a, u_b, corr_b, hu_b, theta, left = call(
                update_kernel,
                [a_out, a_out, a_out, b_out, b_out, b_out, tile_out, left_out],
                i_meta + v(got, theta, u_a, corr_a, hu_a, u_b, corr_b, hu_b, hc_b, diag, diag_b) + lefts,
                (), work,
            )
        got = apply_right(left, BF16)
        got, u_send, corr_send = lax.optimization_barrier((got, u_a, corr_a))
        u_far = lax.ppermute(u_send, "core", swap)
        corr_far = lax.ppermute(corr_send, "core", swap)
        (sums,) = call(
            last_image_kernel, [((2 * n_z * n_xy, cols), F32)], i_meta + v(got, u_b, corr_b, hu_b)
        )
        sums = a2a(sums, ALL)
        out, energy = call(
            last_kernel, [(psi.shape, F32), ((1, 1), F32)],
            i_meta + v(sums, theta, u_a, corr_a, u_far, corr_far),
        )
        return out, energy.reshape(())

    return per_device


def solution(mesh):
    n_z = mesh.shape["sec"]
    n_y = n_x = int(round((mesh.shape["term"] // 2) ** 0.5))
    fine = Mesh(mesh.devices.reshape(n_y, n_x, 2, n_z), ("y", "x", "core", "sec"))
    term = ("y", "x", "core")
    in_specs = (
        P(None, None, "sec"),
        P(None, None, "sec"),
        P(),
        P(term, None, None, None),
        P(term, None, None, None),
    )
    out_specs = (P(None, None, "sec"), P())
    return jax.shard_map(
        make(n_y, n_x, n_z), mesh=fine, in_specs=in_specs, out_specs=out_specs, check_vma=False
    )
```

```python
import functools

import jax
import jax.numpy as jnp
from jax import lax
from jax.experimental import pallas as pl
from jax.experimental.pallas import tpu as pltpu
from jax.sharding import Mesh, PartitionSpec as P

ITERS = 2
XY = ("y", "x")
CZ = ("core", "sec")
ALL = ("y", "x", "core", "sec")
LANES = 128
PIECE = 256
LIMIT = 24
START = 4 * 10**9
F32 = jnp.float32
BF16 = jnp.bfloat16
SMEM = pl.BlockSpec(memory_space=pltpu.SMEM)
VMEM = pl.BlockSpec(memory_space=pltpu.VMEM)


def call(kernel, outs, ins, scratch=(), flops=0):
    moved = sum(int(a.size) * a.dtype.itemsize for a, _ in ins)
    return pl.pallas_call(
        kernel,
        out_shape=[jax.ShapeDtypeStruct(s, d) for s, d in outs],
        in_specs=[s for _, s in ins],
        out_specs=[VMEM] * len(outs),
        scratch_shapes=list(scratch),
        compiler_params=pltpu.CompilerParams(vmem_limit_bytes=LIMIT * 2**20),
        cost_estimate=pl.CostEstimate(flops=flops, bytes_accessed=moved, transcendentals=0),
    )(*[a for a, _ in ins])


def fold(product):
    parts = [product[:, k : k + LANES] for k in range(0, product.shape[1], LANES)]
    return jnp.sum(functools.reduce(lambda a, b: a + b, parts), axis=0, keepdims=True)


def line_of(rows):
    tile = jnp.concatenate(rows + [jnp.zeros((8 - len(rows), LANES), F32)], axis=0)
    sums = jnp.sum(tile, axis=1, keepdims=True)
    row = lax.broadcasted_iota(jnp.int32, tile.shape, 0)
    lane = lax.broadcasted_iota(jnp.int32, tile.shape, 1)
    return jnp.sum(jnp.where(row == lane, sums, 0.0), axis=0, keepdims=True)


def add_rows(ref, start, step, count):
    return functools.reduce(lambda a, b: a + b, [ref[pl.ds(start + step * k, 1)] for k in range(count)])


def make(n_y, n_x, n_z):
    n_xy = n_y * n_x

    def per_device(psi, diag, block_dims, left_env, right_env):
        sectors, size, cols = psi.shape
        sub = cols // n_xy
        shard_rows = n_z * sub
        one, two = sub + 1, 2 * sub + 1
        scale = 1.0 / (size * size)
        core = lax.axis_index("core")
        swap = [(0, 1), (1, 0)]
        row = lax.broadcasted_iota(jnp.int32, (sectors + 2, 2), 0) - sectors
        col = lax.broadcasted_iota(jnp.int32, (sectors + 2, 2), 1)
        meta = jnp.where(
            row < 0,
            jnp.pad(block_dims, ((0, 2), (0, 0))),
            jnp.where(row > 0, lax.axis_index(XY), jnp.where(col == 0, core, lax.axis_index("sec"))),
        )
        share, shard = (size, cols), (sub, size)

        def a2a(array, axes):
            return lax.all_to_all(array, axes, 0, 0, tiled=True)

        def a2a_rows(array, parts, axes):
            blocks = array.reshape(parts, array.shape[0] // parts, 1, cols)
            return a2a(blocks, axes).reshape(array.shape)

        def dims_of(meta_ref, sector):
            return meta_ref[sector, 0], meta_ref[sector, 1]

        def place(meta_ref):
            return meta_ref[sectors, 0], meta_ref[sectors, 1], meta_ref[sectors + 1, 0]

        def share_mask(meta_ref, sector):
            row = lax.broadcasted_iota(jnp.int32, share, 0)
            col = lax.broadcasted_iota(jnp.int32, share, 1) + place(meta_ref)[1] * cols
            rows, columns = dims_of(meta_ref, sector)
            return (row < rows) & (col < columns)

        def own_rows(meta_ref, k):
            return pl.ds(pl.multiple_of(k * cols + place(meta_ref)[2] * sub, sub), sub)

        def start_kernel(meta_ref, psi_ref, out_ref, psi_a_ref):
            total = jnp.zeros((1, LANES), F32)
            for s in range(sectors):
                own = jnp.where(share_mask(meta_ref, s), psi_ref[s], 0.0)
                total = total + fold(own * own)

                @pl.when(place(meta_ref)[0] == s)
                def _():
                    psi_a_ref[...] = own

            for k in range(n_z):
                out_ref[pl.ds(k * one, sub)] = psi_a_ref[own_rows(meta_ref, k)]
                out_ref[pl.ds(k * one + sub, 1)] = total

        def left_matmul(meta_ref, env_ref, got_ref, field, left_ref):
            core, per = place(meta_ref)[0], PIECE // cols
            for i in range(size // PIECE):
                rows = pl.ds(i * PIECE, PIECE)
                for w in range(2):
                    env = env_ref[0, core, rows] if w == 0 else got_ref[rows]
                    part = jnp.dot(env, field, preferred_element_type=F32)
                    left_ref[i * per : (i + 1) * per, w] = part.astype(BF16).reshape(per, cols, cols)

        def first_kernel(meta_ref, got_ref, psi_a_ref, env_ref, env2_ref, u_a_ref, u_b_ref, left_ref):
            norm = jnp.sum(add_rows(got_ref, sub, one, n_z), axis=1, keepdims=True) * scale
            inverse = 1.0 / jnp.sqrt(norm)
            u_a = psi_a_ref[...] * inverse
            u_a_ref[...] = u_a
            for k in range(n_z):
                lanes = slice(k * cols, (k + 1) * cols)
                u_b_ref[:, lanes] = got_ref[pl.ds(k * one, sub)] * inverse
            left_matmul(meta_ref, env_ref, env2_ref, u_a.astype(BF16), left_ref)

        def right_pieces(meta_ref, moved_ref, env_ref, got_ref):
            core = place(meta_ref)[0]
            fields = [
                jnp.concatenate([moved_ref[k, w] for k in range(n_z)], axis=1) for w in range(2)
            ]
            for i in range(size // PIECE):
                rows = pl.ds(i * PIECE, PIECE)
                total = None
                for w in range(2):
                    env = env_ref[0, core, rows] if w == 0 else got_ref[rows]
                    part = lax.dot_general(
                        fields[w], env, (((1,), (1,)), ((), ())), preferred_element_type=F32
                    )
                    total = part if total is None else total + part
                yield rows, total

        def right_kernel(meta_ref, moved_ref, env_ref, got_ref, out_ref):
            for rows, total in right_pieces(meta_ref, moved_ref, env_ref, got_ref):
                out_ref[:, :, rows] = total.reshape(n_xy, sub, PIECE).astype(out_ref.dtype)

        def image_of(meta_ref, got_ref):
            core, z, q = place(meta_ref)
            image = jnp.sum(got_ref[...].astype(F32), axis=0)
            row = lax.broadcasted_iota(jnp.int32, shard, 0) + (z * cols + q * sub)
            col = lax.broadcasted_iota(jnp.int32, shard, 1)
            rows, columns = dims_of(meta_ref, core)
            return jnp.where((row < rows) & (col < columns), image, 0.0)

        def dots_line(image, u_b_ref, more):
            u = u_b_ref[...]
            if not more:
                return line_of([fold(u * image)])
            corr, hu = more[0][...], more[1][...]
            pairs = [(u, image), (corr, hu), (corr, image), (u, corr), (corr, corr), (u, u)]
            return line_of([fold(a * b) for a, b in pairs])

        def put_image(meta_ref, got_ref, u_b_ref, more, image_ref, out_ref, step):
            image = image_of(meta_ref, got_ref)
            image_ref[...] = image
            line = dots_line(image, u_b_ref, more)
            for k in range(n_z):
                for c in range(2):
                    first = (c * n_z + k) * step
                    out_ref[pl.ds(first, sub)] = image[:, k * cols : (k + 1) * cols]
                    out_ref[pl.ds(first + sub, 1)] = line

        def first_image_kernel(meta_ref, got_ref, u_b_ref, diag_ref, image_ref, out_ref):
            put_image(meta_ref, got_ref, u_b_ref, (), image_ref, out_ref, two)
            core = place(meta_ref)[0]
            for k in range(n_z):
                rows = diag_ref[core, own_rows(meta_ref, k)]
                for c in range(2):
                    out_ref[pl.ds((c * n_z + k) * two + one, sub)] = rows

        def image_kernel(meta_ref, got_ref, u_b_ref, corr_b_ref, hu_b_ref, image_ref, out_ref):
            put_image(meta_ref, got_ref, u_b_ref, (corr_b_ref, hu_b_ref), image_ref, out_ref, one)

        def last_image_kernel(meta_ref, got_ref, u_b_ref, corr_b_ref, hu_b_ref, out_ref):
            image = image_of(meta_ref, got_ref)
            line = dots_line(image, u_b_ref, (corr_b_ref, hu_b_ref))
            out_ref[...] = jnp.broadcast_to(line, out_ref.shape)

        def spread_kernel(meta_ref, got_ref, out_ref, *diag_b_ref):
            core = place(meta_ref)[0]
            step = two if diag_b_ref else one
            full = shard_rows + 1

            def mine(k, start):
                rows = [got_ref[pl.ds((c * n_z + k) * step + start, sub)] for c in range(2)]
                return jnp.where(core == 0, rows[0], rows[1])

            line = add_rows(got_ref, sub, step, 2 * n_z)
            for k in range(n_z):
                rows = mine(k, 0)
                for j in range(n_xy):
                    out_ref[pl.ds(j * full + k * sub, sub)] = rows
                for ref in diag_b_ref:
                    ref[:, k * cols : (k + 1) * cols] = mine(k, one)
            for j in range(n_xy):
                out_ref[pl.ds(j * full + shard_rows, 1)] = line

        def projected(theta, sums):
            u_image, corr_hu, corr_image, project, size_corr, size_u = sums
            inverse = 1.0 / jnp.sqrt(size_corr - project * project * (2.0 - size_u))
            cross = 0.5 * ((u_image - project * theta) + (corr_hu - project * theta)) * inverse
            corner = corr_image - project * (corr_hu + u_image) + project * project * theta
            corner = corner * inverse * inverse
            half = 0.5 * (theta - corner)
            lowest = 0.5 * (theta + corner) - jnp.sqrt(half * half + cross * cross)
            x, y = corner - lowest, -cross
            length = jnp.sqrt(x * x + y * y)
            x, y = x / length, y / length
            theta = x * x * theta + 2.0 * x * y * cross + y * y * corner
            return x - y * project * inverse, y * inverse, theta, lowest

        def sums_of(got_ref, count):
            line = add_rows(got_ref, shard_rows, shard_rows + 1, n_xy) * scale
            return [line[:, k : k + 1] for k in range(count)]

        def correction(theta, image, vector, diagonal):
            return (image - theta * vector) / (1.0 + jnp.abs(diagonal - theta))

        def share_of(got_ref):
            parts = [
                got_ref[pl.ds(j * (shard_rows + 1), shard_rows)].reshape(n_z, 1, sub, cols)
                for j in range(n_xy)
            ]
            return jnp.concatenate(parts, axis=1).reshape(share)

        def begin_kernel(meta_ref, got_ref, u_a_ref, u_b_ref, hu_b_ref, diag_ref, diag_b_ref, env_ref, env2_ref, hu_a_ref, corr_a_ref, corr_b_ref, theta_ref, left_ref):
            (theta,) = sums_of(got_ref, 1)
            theta_ref[...] = jnp.broadcast_to(theta, theta_ref.shape)
            hu_a = share_of(got_ref)
            hu_a_ref[...] = hu_a
            corr_a = correction(theta, hu_a, u_a_ref[...], diag_ref[place(meta_ref)[0]])
            corr_a_ref[...] = corr_a
            corr_b_ref[...] = correction(theta, hu_b_ref[...], u_b_ref[...], diag_b_ref[...])
            left_matmul(meta_ref, env_ref, env2_ref, corr_a.astype(BF16), left_ref)

        def update_kernel(meta_ref, got_ref, old_theta_ref, u_a_ref, corr_a_ref, hu_a_ref, u_b_ref, corr_b_ref, hu_b_ref, hc_b_ref, diag_ref, diag_b_ref, env_ref, env2_ref, u_a_out, corr_a_out, hu_a_out, u_b_out, corr_b_out, hu_b_out, theta_ref, left_ref):
            old, new, theta, _ = projected(old_theta_ref[0:1, 0:1], sums_of(got_ref, 6))
            theta_ref[...] = jnp.broadcast_to(theta, theta_ref.shape)
            u_a = old * u_a_ref[...] + new * corr_a_ref[...]
            hu_a = old * hu_a_ref[...] + new * share_of(got_ref)
            corr_a = correction(theta, hu_a, u_a, diag_ref[place(meta_ref)[0]])
            u_a_out[...], hu_a_out[...], corr_a_out[...] = u_a, hu_a, corr_a
            u_b = old * u_b_ref[...] + new * corr_b_ref[...]
            hu_b = old * hu_b_ref[...] + new * hc_b_ref[...]
            u_b_out[...], hu_b_out[...] = u_b, hu_b
            corr_b_out[...] = correction(theta, hu_b, u_b, diag_b_ref[...])
            left_matmul(meta_ref, env_ref, env2_ref, corr_a.astype(BF16), left_ref)

        def last_kernel(meta_ref, got_ref, theta_ref, u_a_ref, corr_a_ref, u_far_ref, corr_far_ref, out_ref, energy_ref):
            line = jnp.sum(got_ref[...], axis=0, keepdims=True) * scale
            sums = [line[:, k : k + 1] for k in range(6)]
            old, new, _, lowest = projected(theta_ref[0:1, 0:1], sums)
            c = place(meta_ref)[0]
            out_ref[c] = old * u_a_ref[...] + new * corr_a_ref[...]
            out_ref[1 - c] = old * u_far_ref[...] + new * corr_far_ref[...]
            energy_ref[...] = lowest

        def v(*arrays):
            return [(a, VMEM) for a in arrays]

        i_meta = [(meta, SMEM)]
        left_out = ((n_z, 2, cols, cols), BF16)
        tile_out, a_out, b_out = ((8, cols), F32), (share, F32), (shard, F32)
        work = 4 * size * size * cols

        first, psi_a = call(
            start_kernel, [((n_z * one, cols), F32), a_out], i_meta + v(psi), (), START
        )

        def swapped(env, other):
            give = lax.dynamic_slice(
                env, (0, other, 0, 0), (1, 1, size, size), allow_negative_indices=False
            )
            return lax.ppermute(give.reshape(size, size), "core", swap)

        first, left_env, other = lax.optimization_barrier((first, left_env, 1 - core))
        lefts = v(left_env, swapped(left_env, other))
        first = a2a_rows(first, n_z, "sec")
        u_a, u_b, left = call(
            first_kernel, [a_out, b_out, left_out], i_meta + v(first, psi_a) + lefts, (), work
        )
        left, right_env = lax.optimization_barrier((left, right_env))
        rights = v(right_env, swapped(right_env, other))

        def apply_right(left, kind=F32):
            moved = a2a(left, "sec")
            (partial,) = call(
                right_kernel, [((n_xy, sub, size), kind)], i_meta + v(moved) + rights, (), work
            )
            return a2a(partial, XY)

        def gather(payload, *more):
            payload = a2a_rows(payload, 2 * n_z, CZ)
            payload, *more = call(
                spread_kernel, [((n_xy * (shard_rows + 1), cols), F32), *more], i_meta + v(payload)
            )
            return [a2a_rows(payload, n_xy, XY), *more]

        payload_out = ((2 * n_z * one, cols), F32)
        got = apply_right(left)
        hu_b, payload = call(
            first_image_kernel,
            [b_out, ((2 * n_z * two, cols), F32)],
            i_meta + v(got, u_b, diag),
        )
        got, diag_b = gather(payload, b_out)
        hu_a, corr_a, corr_b, theta, left = call(
            begin_kernel,
            [a_out, a_out, b_out, tile_out, left_out],
            i_meta + v(got, u_a, u_b, hu_b, diag, diag_b) + lefts, (), work,
        )
        for _ in range(ITERS - 1):
            got = apply_right(left)
            hc_b, payload = call(
                image_kernel, [b_out, payload_out], i_meta + v(got, u_b, corr_b, hu_b)
            )
            (got,) = gather(payload)
            u_a, corr_a, hu_a, u_b, corr_b, hu_b, theta, left = call(
                update_kernel,
                [a_out, a_out, a_out, b_out, b_out, b_out, tile_out, left_out],
                i_meta + v(got, theta, u_a, corr_a, hu_a, u_b, corr_b, hu_b, hc_b, diag, diag_b) + lefts,
                (), work,
            )
        got = apply_right(left, BF16)
        got, u_send, corr_send = lax.optimization_barrier((got, u_a, corr_a))
        u_far = lax.ppermute(u_send, "core", swap)
        corr_far = lax.ppermute(corr_send, "core", swap)
        (sums,) = call(
            last_image_kernel, [((2 * n_z * n_xy, cols), F32)], i_meta + v(got, u_b, corr_b, hu_b)
        )
        sums = a2a(sums, ALL)
        out, energy = call(
            last_kernel, [(psi.shape, F32), ((1, 1), F32)],
            i_meta + v(sums, theta, u_a, corr_a, u_far, corr_far),
        )
        return out, energy.reshape(())

    return per_device


def solution(mesh):
    n_z = mesh.shape["sec"]
    n_y = n_x = int(round((mesh.shape["term"] // 2) ** 0.5))
    fine = Mesh(mesh.devices.reshape(n_y, n_x, 2, n_z), ("y", "x", "core", "sec"))
    term = ("y", "x", "core")
    in_specs = (
        P(None, None, "sec"),
        P(None, None, "sec"),
        P(),
        P(term, None, None, None),
        P(term, None, None, None),
    )
    out_specs = (P(None, None, "sec"), P())
    return jax.shard_map(
        make(n_y, n_x, n_z), mesh=fine, in_specs=in_specs, out_specs=out_specs, check_vma=False
    )
```

```python
import functools

import jax
import jax.numpy as jnp
from jax import lax
from jax.experimental import pallas as pl
from jax.experimental.pallas import tpu as pltpu
from jax.sharding import Mesh, PartitionSpec as P

ITERS = 2
XY = ("y", "x")
CZ = ("core", "sec")
ALL = ("y", "x", "core", "sec")
LANES = 128
PIECE = 1024
BROWS = 16
LIMIT = 24
START = 4 * 10**9
F32 = jnp.float32
BF16 = jnp.bfloat16
SMEM = pl.BlockSpec(memory_space=pltpu.SMEM)
VMEM = pl.BlockSpec(memory_space=pltpu.VMEM)


def call(kernel, outs, ins, scratch=(), flops=0):
    moved = sum(int(a.size) * a.dtype.itemsize for a, _ in ins)
    return pl.pallas_call(
        kernel,
        out_shape=[jax.ShapeDtypeStruct(s, d) for s, d in outs],
        in_specs=[s for _, s in ins],
        out_specs=[VMEM] * len(outs),
        scratch_shapes=list(scratch),
        compiler_params=pltpu.CompilerParams(vmem_limit_bytes=LIMIT * 2**20),
        cost_estimate=pl.CostEstimate(flops=flops, bytes_accessed=moved, transcendentals=0),
    )(*[a for a, _ in ins])


def fold(product):
    parts = [product[:, k : k + LANES] for k in range(0, product.shape[1], LANES)]
    return jnp.sum(functools.reduce(lambda a, b: a + b, parts), axis=0, keepdims=True)


def line_of(rows):
    tile = jnp.concatenate(rows + [jnp.zeros((8 - len(rows), LANES), F32)], axis=0)
    sums = jnp.sum(tile, axis=1, keepdims=True)
    row = lax.broadcasted_iota(jnp.int32, tile.shape, 0)
    lane = lax.broadcasted_iota(jnp.int32, tile.shape, 1)
    return jnp.sum(jnp.where(row == lane, sums, 0.0), axis=0, keepdims=True)


def add_rows(ref, start, step, count):
    return functools.reduce(lambda a, b: a + b, [ref[pl.ds(start + step * k, 1)] for k in range(count)])


def make(n_y, n_x, n_z):
    n_xy = n_y * n_x

    def per_device(psi, diag, block_dims, left_env, right_env):
        sectors, size, cols = psi.shape
        sub = cols // n_xy
        shard_rows = n_z * sub
        one, two = sub + 1, 2 * sub + 1
        scale = 1.0 / (size * size)
        core = lax.axis_index("core")
        swap = [(0, 1), (1, 0)]
        row = lax.broadcasted_iota(jnp.int32, (sectors + 2, 2), 0) - sectors
        col = lax.broadcasted_iota(jnp.int32, (sectors + 2, 2), 1)
        meta = jnp.where(
            row < 0,
            jnp.pad(block_dims, ((0, 2), (0, 0))),
            jnp.where(row > 0, lax.axis_index(XY), jnp.where(col == 0, core, lax.axis_index("sec"))),
        )
        share, shard = (size, cols), (sub, size)

        def a2a(array, axes):
            return lax.all_to_all(array, axes, 0, 0, tiled=True)

        def a2a_rows(array, parts, axes):
            blocks = array.reshape(parts, array.shape[0] // parts, 1, cols)
            return a2a(blocks, axes).reshape(array.shape)

        def dims_of(meta_ref, sector):
            return meta_ref[sector, 0], meta_ref[sector, 1]

        def place(meta_ref):
            return meta_ref[sectors, 0], meta_ref[sectors, 1], meta_ref[sectors + 1, 0]

        def share_mask(meta_ref, sector):
            row = lax.broadcasted_iota(jnp.int32, share, 0)
            col = lax.broadcasted_iota(jnp.int32, share, 1) + place(meta_ref)[1] * cols
            rows, columns = dims_of(meta_ref, sector)
            return (row < rows) & (col < columns)

        def own_rows(meta_ref, k):
            return pl.ds(pl.multiple_of(k * cols + place(meta_ref)[2] * sub, sub), sub)

        def start_kernel(meta_ref, psi_ref, out_ref, psi_a_ref):
            total = jnp.zeros((1, LANES), F32)
            for s in range(sectors):
                own = jnp.where(share_mask(meta_ref, s), psi_ref[s], 0.0)
                total = total + fold(own * own)

                @pl.when(place(meta_ref)[0] == s)
                def _():
                    psi_a_ref[...] = own

            for k in range(n_z):
                out_ref[pl.ds(k * one, sub)] = psi_a_ref[own_rows(meta_ref, k)]
                out_ref[pl.ds(k * one + sub, 1)] = total

        def left_matmul(meta_ref, env_ref, got_ref, field, left_ref):
            core, per = place(meta_ref)[0], PIECE // cols
            for i in range(size // PIECE):
                rows = pl.ds(i * PIECE, PIECE)
                for w in range(2):
                    env = env_ref[0, core, rows] if w == 0 else got_ref[rows]
                    part = jnp.dot(env, field, preferred_element_type=F32)
                    left_ref[i * per : (i + 1) * per, w] = part.astype(BF16).reshape(per, cols, cols)

        def first_kernel(meta_ref, got_ref, psi_a_ref, env_ref, env2_ref, u_a_ref, u_b_ref, left_ref):
            norm = jnp.sum(add_rows(got_ref, sub, one, n_z), axis=1, keepdims=True) * scale
            inverse = 1.0 / jnp.sqrt(norm)
            u_a = psi_a_ref[...] * inverse
            u_a_ref[...] = u_a
            for k in range(n_z):
                lanes = slice(k * cols, (k + 1) * cols)
                u_b_ref[:, lanes] = got_ref[pl.ds(k * one, sub)] * inverse
            left_matmul(meta_ref, env_ref, env2_ref, u_a.astype(BF16), left_ref)

        def right_pieces(meta_ref, moved_ref, env_ref, got_ref):
            core = place(meta_ref)[0]
            fields = [
                jnp.concatenate([moved_ref[k, w] for k in range(n_z)], axis=1) for w in range(2)
            ]
            for i in range(size // PIECE):
                rows = pl.ds(i * PIECE, PIECE)
                total = None
                for w in range(2):
                    env = env_ref[0, core, rows] if w == 0 else got_ref[rows]
                    part = lax.dot_general(
                        fields[w], env, (((1,), (1,)), ((), ())), preferred_element_type=F32
                    )
                    total = part if total is None else total + part
                yield rows, total

        def right_kernel(meta_ref, moved_ref, env_ref, got_ref, out_ref):
            for rows, total in right_pieces(meta_ref, moved_ref, env_ref, got_ref):
                out_ref[:, :, rows] = total.reshape(n_xy, sub, PIECE).astype(out_ref.dtype)

        def image_of(meta_ref, got_ref):
            core, z, q = place(meta_ref)
            image = jnp.sum(got_ref[...].astype(F32), axis=0)
            row = lax.broadcasted_iota(jnp.int32, shard, 0) + (z * cols + q * sub)
            col = lax.broadcasted_iota(jnp.int32, shard, 1)
            rows, columns = dims_of(meta_ref, core)
            return jnp.where((row < rows) & (col < columns), image, 0.0)

        def dots_line(image, u_b_ref, more):
            u = u_b_ref[...]
            if not more:
                return line_of([fold(u * image)])
            corr, hu = more[0][...], more[1][...]
            pairs = [(u, image), (corr, hu), (corr, image), (u, corr), (corr, corr), (u, u)]
            return line_of([fold(a * b) for a, b in pairs])

        def put_image(meta_ref, got_ref, u_b_ref, more, image_ref, out_ref, step):
            image = image_of(meta_ref, got_ref)
            image_ref[...] = image
            line = dots_line(image, u_b_ref, more)
            for k in range(n_z):
                for c in range(2):
                    first = (c * n_z + k) * step
                    out_ref[pl.ds(first, sub)] = image[:, k * cols : (k + 1) * cols]
                    out_ref[pl.ds(first + sub, 1)] = line

        def first_image_kernel(meta_ref, got_ref, u_b_ref, diag_ref, image_ref, out_ref):
            put_image(meta_ref, got_ref, u_b_ref, (), image_ref, out_ref, two)
            core = place(meta_ref)[0]
            for k in range(n_z):
                rows = diag_ref[core, own_rows(meta_ref, k)]
                for c in range(2):
                    out_ref[pl.ds((c * n_z + k) * two + one, sub)] = rows

        def image_kernel(meta_ref, got_ref, u_b_ref, corr_b_ref, hu_b_ref, image_ref, out_ref):
            put_image(meta_ref, got_ref, u_b_ref, (corr_b_ref, hu_b_ref), image_ref, out_ref, one)

        def last_image_kernel(meta_ref, got_ref, u_b_ref, corr_b_ref, hu_b_ref, out_ref):
            image = image_of(meta_ref, got_ref)
            line = dots_line(image, u_b_ref, (corr_b_ref, hu_b_ref))
            out_ref[...] = jnp.broadcast_to(line, out_ref.shape)

        def mine(meta_ref, got_ref, k, step, start):
            rows = [got_ref[pl.ds((c * n_z + k) * step + start, sub)] for c in range(2)]
            return jnp.where(place(meta_ref)[0] == 0, rows[0], rows[1])

        def first_spread_kernel(meta_ref, got_ref, out_ref, diag_b_ref):
            full = shard_rows + 1
            line = add_rows(got_ref, sub, two, 2 * n_z)
            for k in range(n_z):
                rows = mine(meta_ref, got_ref, k, two, 0)
                for j in range(n_xy):
                    out_ref[pl.ds(j * full + k * sub, sub)] = rows
                diag_b_ref[:, k * cols : (k + 1) * cols] = mine(meta_ref, got_ref, k, two, one)
            for j in range(n_xy):
                out_ref[pl.ds(j * full + shard_rows, 1)] = line

        def spread_kernel(meta_ref, got_ref, out_ref):
            line = add_rows(got_ref, sub, one, 2 * n_z)
            pieces = []
            for _ in range(3):
                pieces.append(line.astype(BF16).astype(F32))
                line = line - pieces[-1]
            pieces.append(jnp.zeros((BROWS - 3, cols), F32))
            rows = [mine(meta_ref, got_ref, k, one, 0) for k in range(n_z)]
            block = jnp.concatenate(rows + pieces, axis=0).astype(BF16)
            out_ref[...] = jnp.broadcast_to(block[None], out_ref.shape)

        def projected(theta, sums):
            u_image, corr_hu, corr_image, project, size_corr, size_u = sums
            inverse = 1.0 / jnp.sqrt(size_corr - project * project * (2.0 - size_u))
            cross = 0.5 * ((u_image - project * theta) + (corr_hu - project * theta)) * inverse
            corner = corr_image - project * (corr_hu + u_image) + project * project * theta
            corner = corner * inverse * inverse
            half = 0.5 * (theta - corner)
            lowest = 0.5 * (theta + corner) - jnp.sqrt(half * half + cross * cross)
            x, y = corner - lowest, -cross
            length = jnp.sqrt(x * x + y * y)
            x, y = x / length, y / length
            theta = x * x * theta + 2.0 * x * y * cross + y * y * corner
            return x - y * project * inverse, y * inverse, theta, lowest

        def correction(theta, image, vector, diagonal):
            return (image - theta * vector) / (1.0 + jnp.abs(diagonal - theta))

        def share_of(parts):
            parts = [part.reshape(n_z, 1, sub, cols) for part in parts]
            return jnp.concatenate(parts, axis=1).reshape(share)

        def begin_kernel(meta_ref, got_ref, u_a_ref, u_b_ref, hu_b_ref, diag_ref, diag_b_ref, env_ref, env2_ref, hu_a_ref, corr_a_ref, corr_b_ref, theta_ref, left_ref):
            full = shard_rows + 1
            theta = add_rows(got_ref, shard_rows, full, n_xy)[:, :1] * scale
            theta_ref[...] = jnp.broadcast_to(theta, theta_ref.shape)
            hu_a = share_of([got_ref[pl.ds(j * full, shard_rows)] for j in range(n_xy)])
            hu_a_ref[...] = hu_a
            corr_a = correction(theta, hu_a, u_a_ref[...], diag_ref[place(meta_ref)[0]])
            corr_a_ref[...] = corr_a
            corr_b_ref[...] = correction(theta, hu_b_ref[...], u_b_ref[...], diag_b_ref[...])
            left_matmul(meta_ref, env_ref, env2_ref, corr_a.astype(BF16), left_ref)

        def update_kernel(meta_ref, got_ref, old_theta_ref, u_a_ref, corr_a_ref, hu_a_ref, u_b_ref, corr_b_ref, hu_b_ref, hc_b_ref, diag_ref, diag_b_ref, env_ref, env2_ref, u_a_out, corr_a_out, u_b_out, corr_b_out, hu_b_out, theta_ref, left_ref, *hu_a_out):
            lines = jnp.sum(got_ref[:, shard_rows:].astype(F32), axis=0)
            line = jnp.sum(lines, axis=0, keepdims=True) * scale
            sums = [line[:, k : k + 1] for k in range(6)]
            old, new, theta, _ = projected(old_theta_ref[0:1, 0:1], sums)
            theta_ref[...] = jnp.broadcast_to(theta, theta_ref.shape)
            u_a = old * u_a_ref[...] + new * corr_a_ref[...]
            hu_a = old * hu_a_ref[...] + new * share_of([got_ref[j, :shard_rows].astype(F32) for j in range(n_xy)])
            corr_a = correction(theta, hu_a, u_a, diag_ref[place(meta_ref)[0]])
            u_a_out[...], corr_a_out[...] = u_a, corr_a
            for ref in hu_a_out:
                ref[...] = hu_a
            u_b = old * u_b_ref[...] + new * corr_b_ref[...]
            hu_b = old * hu_b_ref[...] + new * hc_b_ref[...]
            u_b_out[...], hu_b_out[...] = u_b, hu_b
            corr_b_out[...] = correction(theta, hu_b, u_b, diag_b_ref[...])
            left_matmul(meta_ref, env_ref, env2_ref, corr_a.astype(BF16), left_ref)

        def last_kernel(meta_ref, got_ref, theta_ref, u_a_ref, corr_a_ref, u_far_ref, corr_far_ref, out_ref, energy_ref):
            line = jnp.sum(got_ref[...], axis=0, keepdims=True) * scale
            sums = [line[:, k : k + 1] for k in range(6)]
            old, new, _, lowest = projected(theta_ref[0:1, 0:1], sums)
            c = place(meta_ref)[0]
            energy_ref[...] = lowest
            out_ref[c] = old * u_a_ref[...] + new * corr_a_ref[...]
            out_ref[1 - c] = old * u_far_ref[...] + new * corr_far_ref[...]

        def v(*arrays):
            return [(a, VMEM) for a in arrays]

        i_meta = [(meta, SMEM)]
        left_out = ((n_z, 2, cols, cols), BF16)
        tile_out, a_out, b_out = ((8, cols), F32), (share, F32), (shard, F32)
        work = 4 * size * size * cols

        first, psi_a = call(
            start_kernel, [((n_z * one, cols), F32), a_out], i_meta + v(psi), (), START
        )

        def swapped(env, other):
            give = lax.dynamic_slice(
                env, (0, other, 0, 0), (1, 1, size, size), allow_negative_indices=False
            )
            return lax.ppermute(give.reshape(size, size), "core", swap)

        first, left_env, other = lax.optimization_barrier((first, left_env, 1 - core))
        lefts = v(left_env, swapped(left_env, other))
        first = a2a_rows(first, n_z, "sec")
        u_a, u_b, left = call(
            first_kernel, [a_out, b_out, left_out], i_meta + v(first, psi_a) + lefts, (), work
        )
        left, right_env = lax.optimization_barrier((left, right_env))
        rights = v(right_env, swapped(right_env, other))

        def apply_right(left, kind=F32):
            moved = a2a(left, "sec")
            (partial,) = call(
                right_kernel, [((n_xy, sub, size), kind)], i_meta + v(moved) + rights, (), work
            )
            return a2a(partial, XY)

        payload_out = ((2 * n_z * one, cols), F32)
        got = apply_right(left)
        hu_b, payload = call(
            first_image_kernel,
            [b_out, ((2 * n_z * two, cols), F32)],
            i_meta + v(got, u_b, diag),
        )
        payload, diag_b = call(
            first_spread_kernel,
            [((n_xy * (shard_rows + 1), cols), F32), b_out],
            i_meta + v(a2a_rows(payload, 2 * n_z, CZ)),
        )
        got = a2a_rows(payload, n_xy, XY)
        hu_a, corr_a, corr_b, theta, left = call(
            begin_kernel,
            [a_out, a_out, b_out, tile_out, left_out],
            i_meta + v(got, u_a, u_b, hu_b, diag, diag_b) + lefts, (), work,
        )
        for step in range(ITERS - 1):
            got = apply_right(left)
            hc_b, payload = call(
                image_kernel, [b_out, payload_out], i_meta + v(got, u_b, corr_b, hu_b)
            )
            (payload,) = call(
                spread_kernel,
                [((n_xy, shard_rows + BROWS, cols), BF16)],
                i_meta + v(a2a_rows(payload, 2 * n_z, CZ)),
            )
            got = a2a(payload, XY)
            more = [a_out] * (step < ITERS - 2)
            u_a, corr_a, u_b, corr_b, hu_b, theta, left, *more = call(
                update_kernel,
                [a_out, a_out, b_out, b_out, b_out, tile_out, left_out] + more,
                i_meta + v(got, theta, u_a, corr_a, hu_a, u_b, corr_b, hu_b, hc_b, diag, diag_b) + lefts,
                (), work,
            )
            (hu_a,) = more or (None,)
        got = apply_right(left, BF16)
        got, u_send, corr_send = lax.optimization_barrier((got, u_a, corr_a))
        u_far = lax.ppermute(u_send, "core", swap)
        corr_far = lax.ppermute(corr_send, "core", swap)
        (sums,) = call(
            last_image_kernel, [((2 * n_z * n_xy, cols), F32)], i_meta + v(got, u_b, corr_b, hu_b)
        )
        sums = a2a(sums, ALL)
        out, energy = call(
            last_kernel, [(psi.shape, F32), ((1, 1), F32)],
            i_meta + v(sums, theta, u_a, corr_a, u_far, corr_far),
        )
        return out, energy.reshape(())

    return per_device


def solution(mesh):
    n_z = mesh.shape["sec"]
    n_y = n_x = int(round((mesh.shape["term"] // 2) ** 0.5))
    fine = Mesh(mesh.devices.reshape(n_y, n_x, 2, n_z), ("y", "x", "core", "sec"))
    term = ("y", "x", "core")
    in_specs = (
        P(None, None, "sec"),
        P(None, None, "sec"),
        P(),
        P(term, None, None, None),
        P(term, None, None, None),
    )
    out_specs = (P(None, None, "sec"), P())
    return jax.shard_map(
        make(n_y, n_x, n_z), mesh=fine, in_specs=in_specs, out_specs=out_specs, check_vma=False
    )
```

```python
import functools

import jax
import jax.numpy as jnp
from jax import lax
from jax.experimental import pallas as pl
from jax.experimental.pallas import tpu as pltpu
from jax.sharding import Mesh, PartitionSpec as P

ITERS = 2
XY = ("y", "x")
CZ = ("core", "sec")
ALL = ("y", "x", "core", "sec")
LANES = 128
PIECE = 1024
TILE = 16
RANGE = 32000.0
DIGIT = 2.0**14
I16 = jnp.int16
LIMIT = 24
START = 4 * 10**9
F32 = jnp.float32
BF16 = jnp.bfloat16
SMEM = pl.BlockSpec(memory_space=pltpu.SMEM)
VMEM = pl.BlockSpec(memory_space=pltpu.VMEM)


def call(kernel, outs, ins, scratch=(), flops=0):
    moved = sum(int(a.size) * a.dtype.itemsize for a, _ in ins)
    return pl.pallas_call(
        kernel,
        out_shape=[jax.ShapeDtypeStruct(s, d) for s, d in outs],
        in_specs=[s for _, s in ins],
        out_specs=[VMEM] * len(outs),
        scratch_shapes=list(scratch),
        compiler_params=pltpu.CompilerParams(vmem_limit_bytes=LIMIT * 2**20),
        cost_estimate=pl.CostEstimate(flops=flops, bytes_accessed=moved, transcendentals=0),
    )(*[a for a, _ in ins])


def fold(product):
    parts = [product[:, k : k + LANES] for k in range(0, product.shape[1], LANES)]
    return jnp.sum(functools.reduce(lambda a, b: a + b, parts), axis=0, keepdims=True)


def line_of(rows):
    tile = jnp.concatenate(rows + [jnp.zeros((8 - len(rows), LANES), F32)], axis=0)
    sums = jnp.sum(tile, axis=1, keepdims=True)
    row = lax.broadcasted_iota(jnp.int32, tile.shape, 0)
    lane = lax.broadcasted_iota(jnp.int32, tile.shape, 1)
    return jnp.sum(jnp.where(row == lane, sums, 0.0), axis=0, keepdims=True)


def add_rows(ref, start, step, count):
    return functools.reduce(lambda a, b: a + b, [ref[pl.ds(start + step * k, 1)] for k in range(count)])


def powers():
    lane = lax.broadcasted_iota(jnp.int32, (1, LANES), 1)
    up, down = jnp.ones((1, LANES), F32), jnp.ones((1, LANES), F32)
    for bit in range(7):
        chosen = (lane >> bit) % 2 == 1
        up = up * jnp.where(chosen, 2.0 ** (1 << bit), 1.0)
        down = down * jnp.where(chosen & (lane < LANES - 1), 2.0 ** -(1 << bit), 1.0)
    down = jnp.where(lane < LANES - 1, down, 0.0)
    return lane.astype(F32), up, down


def exponent_of(largest):
    _, up, down = powers()
    above = jnp.sum(jnp.where(up < largest, 1.0, 0.0), axis=1, keepdims=True)
    below = jnp.sum(jnp.where((down >= largest) & (down > 0.0), 1.0, 0.0), axis=1, keepdims=True)
    return jnp.clip(jnp.where(largest > 1.0, above, 1.0 - below), -126.0, 126.0)


def power(exponent):
    lane, up, down = powers()
    chosen = jnp.where(lane == exponent, up, 0.0)
    chosen = chosen + jnp.where((lane == -exponent) & (exponent < 0.0), down, 0.0)
    return jnp.sum(chosen, axis=1, keepdims=True)


def whole(values):
    return jnp.floor(values + 0.5)


def encode(block, line):
    largest = jnp.max(jnp.max(jnp.abs(block), axis=0, keepdims=True), axis=1, keepdims=True)
    exponent = exponent_of(largest)
    rows = [jnp.broadcast_to(exponent, line.shape)]
    block = whole(block * power(-exponent) * RANGE)
    exponent = exponent_of(jnp.max(jnp.abs(line), axis=1, keepdims=True))
    rows.append(jnp.broadcast_to(exponent, line.shape))
    rest = line * power(-exponent)
    for _ in range(3):
        rest = rest * DIGIT
        rows.append(whole(rest))
        rest = rest - rows[-1]
    rows.append(jnp.zeros((TILE - len(rows), LANES), F32))
    return jnp.concatenate([block] + rows, axis=0).astype(jnp.int32).astype(I16)


def decode(ref, count):
    size = ref.shape[1] - TILE
    tiles = [ref[j, size:].astype(jnp.int32).astype(F32) for j in range(count)]
    rows = [jnp.concatenate([tile[k : k + 1] for tile in tiles], axis=0) for k in range(5)]
    scales = power(rows[0][:, :1])
    blocks = [
        ref[j, :size].astype(jnp.int32).astype(F32) * (1.0 / RANGE) * scales[j : j + 1]
        for j in range(count)
    ]
    line = ((rows[4] / DIGIT + rows[3]) / DIGIT + rows[2]) / DIGIT * power(rows[1][:, :1])
    return blocks, jnp.sum(line, axis=0, keepdims=True)


def make(n_y, n_x, n_z):
    n_xy = n_y * n_x

    def per_device(psi, diag, block_dims, left_env, right_env):
        sectors, size, cols = psi.shape
        sub = cols // n_xy
        shard_rows = n_z * sub
        one = sub + 1
        scale = 1.0 / (size * size)
        core = lax.axis_index("core")
        swap = [(0, 1), (1, 0)]
        row = lax.broadcasted_iota(jnp.int32, (sectors + 2, 2), 0) - sectors
        col = lax.broadcasted_iota(jnp.int32, (sectors + 2, 2), 1)
        meta = jnp.where(
            row < 0,
            jnp.pad(block_dims, ((0, 2), (0, 0))),
            jnp.where(row > 0, lax.axis_index(XY), jnp.where(col == 0, core, lax.axis_index("sec"))),
        )
        share, shard = (size, cols), (sub, size)

        def a2a(array, axes):
            return lax.all_to_all(array, axes, 0, 0, tiled=True)

        def a2a_rows(array, parts, axes):
            blocks = array.reshape(parts, array.shape[0] // parts, 1, cols)
            return a2a(blocks, axes).reshape(array.shape)

        def dims_of(meta_ref, sector):
            return meta_ref[sector, 0], meta_ref[sector, 1]

        def place(meta_ref):
            return meta_ref[sectors, 0], meta_ref[sectors, 1], meta_ref[sectors + 1, 0]

        def share_mask(meta_ref, sector):
            row = lax.broadcasted_iota(jnp.int32, share, 0)
            col = lax.broadcasted_iota(jnp.int32, share, 1) + place(meta_ref)[1] * cols
            rows, columns = dims_of(meta_ref, sector)
            return (row < rows) & (col < columns)

        def own_rows(meta_ref, k):
            return pl.ds(pl.multiple_of(k * cols + place(meta_ref)[2] * sub, sub), sub)

        def start_kernel(meta_ref, psi_ref, out_ref, psi_a_ref):
            total = jnp.zeros((1, LANES), F32)
            for s in range(sectors):
                own = jnp.where(share_mask(meta_ref, s), psi_ref[s], 0.0)
                total = total + fold(own * own)

                @pl.when(place(meta_ref)[0] == s)
                def _():
                    psi_a_ref[...] = own

            for k in range(n_z):
                out_ref[pl.ds(k * one, sub)] = psi_a_ref[own_rows(meta_ref, k)]
                out_ref[pl.ds(k * one + sub, 1)] = total

        def left_matmul(meta_ref, env_ref, got_ref, field, left_ref):
            core, per = place(meta_ref)[0], PIECE // cols
            for i in range(size // PIECE):
                rows = pl.ds(i * PIECE, PIECE)
                for w in range(2):
                    env = env_ref[0, core, rows] if w == 0 else got_ref[rows]
                    part = jnp.dot(env, field, preferred_element_type=F32)
                    left_ref[i * per : (i + 1) * per, w] = part.astype(BF16).reshape(per, cols, cols)

        def first_kernel(meta_ref, got_ref, psi_a_ref, env_ref, env2_ref, u_a_ref, u_b_ref, left_ref):
            norm = jnp.sum(add_rows(got_ref, sub, one, n_z), axis=1, keepdims=True) * scale
            inverse = 1.0 / jnp.sqrt(norm)
            u_a = psi_a_ref[...] * inverse
            u_a_ref[...] = u_a
            for k in range(n_z):
                lanes = slice(k * cols, (k + 1) * cols)
                u_b_ref[:, lanes] = got_ref[pl.ds(k * one, sub)] * inverse
            left_matmul(meta_ref, env_ref, env2_ref, u_a.astype(BF16), left_ref)

        def right_pieces(meta_ref, moved_ref, env_ref, got_ref):
            core = place(meta_ref)[0]
            fields = [
                jnp.concatenate([moved_ref[k, w] for k in range(n_z)], axis=1) for w in range(2)
            ]
            for i in range(size // PIECE):
                rows = pl.ds(i * PIECE, PIECE)
                total = None
                for w in range(2):
                    env = env_ref[0, core, rows] if w == 0 else got_ref[rows]
                    part = lax.dot_general(
                        fields[w], env, (((1,), (1,)), ((), ())), preferred_element_type=F32
                    )
                    total = part if total is None else total + part
                yield rows, total

        def right_kernel(meta_ref, moved_ref, env_ref, got_ref, out_ref):
            for rows, total in right_pieces(meta_ref, moved_ref, env_ref, got_ref):
                out_ref[:, :, rows] = total.reshape(n_xy, sub, PIECE).astype(out_ref.dtype)

        def image_of(meta_ref, got_ref):
            core, z, q = place(meta_ref)
            image = jnp.sum(got_ref[...].astype(F32), axis=0)
            row = lax.broadcasted_iota(jnp.int32, shard, 0) + (z * cols + q * sub)
            col = lax.broadcasted_iota(jnp.int32, shard, 1)
            rows, columns = dims_of(meta_ref, core)
            return jnp.where((row < rows) & (col < columns), image, 0.0)

        def dots_line(image, u_b_ref, more):
            u = u_b_ref[...]
            if not more:
                return line_of([fold(u * image)])
            corr, hu = more[0][...], more[1][...]
            pairs = [(u, image), (corr, hu), (corr, image), (u, corr), (corr, corr), (u, u)]
            return line_of([fold(a * b) for a, b in pairs])

        def first_image_kernel(meta_ref, got_ref, u_b_ref, diag_ref, image_ref, out_ref):
            image = image_of(meta_ref, got_ref)
            image_ref[...] = image
            line = dots_line(image, u_b_ref, ())
            for k in range(n_z):
                for c in range(2):
                    shard_k = image[:, k * cols : (k + 1) * cols]
                    rows = jnp.where(place(meta_ref)[0] == c, shard_k, diag_ref[c, own_rows(meta_ref, k)])
                    out_ref[pl.ds((c * n_z + k) * one, sub)] = rows
                    out_ref[pl.ds((c * n_z + k) * one + sub, 1)] = line

        def image_kernel(meta_ref, got_ref, u_b_ref, corr_b_ref, hu_b_ref, image_ref, out_ref):
            image = image_of(meta_ref, got_ref)
            image_ref[...] = image
            line = dots_line(image, u_b_ref, (corr_b_ref, hu_b_ref))
            for k in range(2 * n_z):
                out_ref[pl.ds(k * one, sub)] = image[:, (k % n_z) * cols : (k % n_z + 1) * cols]
                out_ref[pl.ds(k * one + sub, 1)] = line

        def last_image_kernel(meta_ref, got_ref, u_b_ref, corr_b_ref, hu_b_ref, out_ref):
            image = image_of(meta_ref, got_ref)
            line = dots_line(image, u_b_ref, (corr_b_ref, hu_b_ref))
            out_ref[...] = jnp.broadcast_to(line, out_ref.shape)

        def from_cores(meta_ref, got_ref, k):
            zero, other = [got_ref[pl.ds((c * n_z + k) * one, sub)] for c in range(2)]
            first = place(meta_ref)[0] == 0
            return jnp.where(first, zero, other), jnp.where(first, other, zero)

        def spread_kernel(meta_ref, got_ref, out_ref, *diag_b_ref):
            line = add_rows(got_ref, sub, one, 2 * n_z)
            shards = []
            for k in range(n_z):
                rows, far = from_cores(meta_ref, got_ref, k)
                shards.append(rows)
                for ref in diag_b_ref:
                    ref[:, k * cols : (k + 1) * cols] = far
            block = encode(jnp.concatenate(shards, axis=0), line)
            out_ref[...] = jnp.broadcast_to(block[None], out_ref.shape)

        def projected(theta, sums):
            u_image, corr_hu, corr_image, project, size_corr, size_u = sums
            inverse = 1.0 / jnp.sqrt(size_corr - project * project * (2.0 - size_u))
            cross = 0.5 * ((u_image - project * theta) + (corr_hu - project * theta)) * inverse
            corner = corr_image - project * (corr_hu + u_image) + project * project * theta
            corner = corner * inverse * inverse
            half = 0.5 * (theta - corner)
            lowest = 0.5 * (theta + corner) - jnp.sqrt(half * half + cross * cross)
            x, y = corner - lowest, -cross
            length = jnp.sqrt(x * x + y * y)
            x, y = x / length, y / length
            theta = x * x * theta + 2.0 * x * y * cross + y * y * corner
            return x - y * project * inverse, y * inverse, theta, lowest

        def correction(theta, image, vector, diagonal):
            return (image - theta * vector) / (1.0 + jnp.abs(diagonal - theta))

        def share_of(parts):
            parts = [part.reshape(n_z, 1, sub, cols) for part in parts]
            return jnp.concatenate(parts, axis=1).reshape(share)

        def begin_kernel(meta_ref, got_ref, u_a_ref, u_b_ref, hu_b_ref, diag_ref, diag_b_ref, env_ref, env2_ref, hu_a_ref, corr_a_ref, corr_b_ref, theta_ref, left_ref):
            blocks, line = decode(got_ref, n_xy)
            theta = line[:, :1] * scale
            theta_ref[...] = jnp.broadcast_to(theta, theta_ref.shape)
            hu_a = share_of(blocks)
            hu_a_ref[...] = hu_a
            corr_a = correction(theta, hu_a, u_a_ref[...], diag_ref[place(meta_ref)[0]])
            corr_a_ref[...] = corr_a
            corr_b_ref[...] = correction(theta, hu_b_ref[...], u_b_ref[...], diag_b_ref[...])
            left_matmul(meta_ref, env_ref, env2_ref, corr_a.astype(BF16), left_ref)

        def update_kernel(meta_ref, got_ref, old_theta_ref, u_a_ref, corr_a_ref, hu_a_ref, u_b_ref, corr_b_ref, hu_b_ref, hc_b_ref, diag_ref, diag_b_ref, env_ref, env2_ref, u_a_out, corr_a_out, u_b_out, corr_b_out, hu_b_out, theta_ref, left_ref, *hu_a_out):
            blocks, line = decode(got_ref, n_xy)
            sums = [line[:, k : k + 1] * scale for k in range(6)]
            old, new, theta, _ = projected(old_theta_ref[0:1, 0:1], sums)
            theta_ref[...] = jnp.broadcast_to(theta, theta_ref.shape)
            u_a = old * u_a_ref[...] + new * corr_a_ref[...]
            hu_a = old * hu_a_ref[...] + new * share_of(blocks)
            corr_a = correction(theta, hu_a, u_a, diag_ref[place(meta_ref)[0]])
            u_a_out[...], corr_a_out[...] = u_a, corr_a
            for ref in hu_a_out:
                ref[...] = hu_a
            u_b = old * u_b_ref[...] + new * corr_b_ref[...]
            hu_b = old * hu_b_ref[...] + new * hc_b_ref[...]
            u_b_out[...], hu_b_out[...] = u_b, hu_b
            corr_b_out[...] = correction(theta, hu_b, u_b, diag_b_ref[...])
            left_matmul(meta_ref, env_ref, env2_ref, corr_a.astype(BF16), left_ref)

        def last_kernel(meta_ref, got_ref, theta_ref, u_a_ref, corr_a_ref, u_far_ref, corr_far_ref, out_ref, energy_ref):
            line = jnp.sum(got_ref[...], axis=0, keepdims=True) * scale
            sums = [line[:, k : k + 1] for k in range(6)]
            old, new, _, lowest = projected(theta_ref[0:1, 0:1], sums)
            c = place(meta_ref)[0]
            energy_ref[...] = lowest
            out_ref[c] = old * u_a_ref[...] + new * corr_a_ref[...]
            out_ref[1 - c] = old * u_far_ref[...] + new * corr_far_ref[...]

        def v(*arrays):
            return [(a, VMEM) for a in arrays]

        i_meta = [(meta, SMEM)]
        left_out = ((n_z, 2, cols, cols), BF16)
        tile_out, a_out, b_out = ((8, cols), F32), (share, F32), (shard, F32)
        work = 4 * size * size * cols

        first, psi_a = call(
            start_kernel, [((n_z * one, cols), F32), a_out], i_meta + v(psi), (), START
        )

        def swapped(env, other):
            give = lax.dynamic_slice(
                env, (0, other, 0, 0), (1, 1, size, size), allow_negative_indices=False
            )
            return lax.ppermute(give.reshape(size, size), "core", swap)

        first, left_env, other = lax.optimization_barrier((first, left_env, 1 - core))
        lefts = v(left_env, swapped(left_env, other))
        first = a2a_rows(first, n_z, "sec")
        u_a, u_b, left = call(
            first_kernel, [a_out, b_out, left_out], i_meta + v(first, psi_a) + lefts, (), work
        )
        left, right_env = lax.optimization_barrier((left, right_env))
        rights = v(right_env, swapped(right_env, other))

        def apply_right(left, kind=F32):
            moved = a2a(left, "sec")
            (partial,) = call(
                right_kernel, [((n_xy, sub, size), kind)], i_meta + v(moved) + rights, (), work
            )
            return a2a(partial, XY)

        payload_out = ((2 * n_z * one, cols), F32)
        got = apply_right(left)
        hu_b, payload = call(
            first_image_kernel,
            [b_out, payload_out],
            i_meta + v(got, u_b, diag),
        )
        gathered = ((n_xy, shard_rows + TILE, cols), I16)
        payload, diag_b = call(
            spread_kernel, [gathered, b_out], i_meta + v(a2a_rows(payload, 2 * n_z, CZ))
        )
        got = a2a(payload, XY)
        hu_a, corr_a, corr_b, theta, left = call(
            begin_kernel,
            [a_out, a_out, b_out, tile_out, left_out],
            i_meta + v(got, u_a, u_b, hu_b, diag, diag_b) + lefts, (), work,
        )
        for step in range(ITERS - 1):
            got = apply_right(left, BF16)
            hc_b, payload = call(
                image_kernel, [b_out, payload_out], i_meta + v(got, u_b, corr_b, hu_b)
            )
            (payload,) = call(
                spread_kernel, [gathered], i_meta + v(a2a_rows(payload, 2 * n_z, CZ))
            )
            got = a2a(payload, XY)
            more = [a_out] * (step < ITERS - 2)
            u_a, corr_a, u_b, corr_b, hu_b, theta, left, *more = call(
                update_kernel,
                [a_out, a_out, b_out, b_out, b_out, tile_out, left_out] + more,
                i_meta + v(got, theta, u_a, corr_a, hu_a, u_b, corr_b, hu_b, hc_b, diag, diag_b) + lefts,
                (), work,
            )
            (hu_a,) = more or (None,)
        got = apply_right(left, BF16)
        got, u_send, corr_send = lax.optimization_barrier((got, u_a, corr_a))
        u_far = lax.ppermute(u_send, "core", swap)
        corr_far = lax.ppermute(corr_send, "core", swap)
        (sums,) = call(
            last_image_kernel, [((2 * n_z * n_xy, cols), F32)], i_meta + v(got, u_b, corr_b, hu_b)
        )
        sums = a2a(sums, ALL)
        out, energy = call(
            last_kernel, [(psi.shape, F32), ((1, 1), F32)],
            i_meta + v(sums, theta, u_a, corr_a, u_far, corr_far),
        )
        return out, energy.reshape(())

    return per_device


def solution(mesh):
    n_z = mesh.shape["sec"]
    n_y = n_x = int(round((mesh.shape["term"] // 2) ** 0.5))
    fine = Mesh(mesh.devices.reshape(n_y, n_x, 2, n_z), ("y", "x", "core", "sec"))
    term = ("y", "x", "core")
    in_specs = (
        P(None, None, "sec"),
        P(None, None, "sec"),
        P(),
        P(term, None, None, None),
        P(term, None, None, None),
    )
    out_specs = (P(None, None, "sec"), P())
    return jax.shard_map(
        make(n_y, n_x, n_z), mesh=fine, in_specs=in_specs, out_specs=out_specs, check_vma=False
    )
```

```python
import functools

import jax
import jax.numpy as jnp
from jax import lax
from jax.experimental import pallas as pl
from jax.experimental.pallas import tpu as pltpu
from jax.sharding import Mesh, PartitionSpec as P

ITERS = 2
XY = ("y", "x")
CZ = ("core", "sec")
ALL = ("y", "x", "core", "sec")
LANES = 128
PIECE = 1024
TILE = 16
RANGE = 32000.0
DIGIT = 2.0**14
I16 = jnp.int16
LIMIT = 24
START = 4 * 10**9
F32 = jnp.float32
BF16 = jnp.bfloat16
SMEM = pl.BlockSpec(memory_space=pltpu.SMEM)
VMEM = pl.BlockSpec(memory_space=pltpu.VMEM)


def call(kernel, outs, ins, scratch=(), flops=0):
    moved = sum(int(a.size) * a.dtype.itemsize for a, _ in ins)
    return pl.pallas_call(
        kernel,
        out_shape=[jax.ShapeDtypeStruct(s, d) for s, d in outs],
        in_specs=[s for _, s in ins],
        out_specs=[VMEM] * len(outs),
        scratch_shapes=list(scratch),
        compiler_params=pltpu.CompilerParams(vmem_limit_bytes=LIMIT * 2**20),
        cost_estimate=pl.CostEstimate(flops=flops, bytes_accessed=moved, transcendentals=0),
    )(*[a for a, _ in ins])


def fold(product):
    parts = [product[:, k : k + LANES] for k in range(0, product.shape[1], LANES)]
    return jnp.sum(functools.reduce(lambda a, b: a + b, parts), axis=0, keepdims=True)


def line_of(rows):
    tile = jnp.concatenate(rows + [jnp.zeros((8 - len(rows), LANES), F32)], axis=0)
    sums = jnp.sum(tile, axis=1, keepdims=True)
    row = lax.broadcasted_iota(jnp.int32, tile.shape, 0)
    lane = lax.broadcasted_iota(jnp.int32, tile.shape, 1)
    return jnp.sum(jnp.where(row == lane, sums, 0.0), axis=0, keepdims=True)


def add_rows(ref, start, step, count):
    return functools.reduce(lambda a, b: a + b, [ref[pl.ds(start + step * k, 1)] for k in range(count)])


def powers():
    lane = lax.broadcasted_iota(jnp.int32, (1, LANES), 1)
    up, down = jnp.ones((1, LANES), F32), jnp.ones((1, LANES), F32)
    for bit in range(7):
        chosen = (lane >> bit) % 2 == 1
        up = up * jnp.where(chosen, 2.0 ** (1 << bit), 1.0)
        down = down * jnp.where(chosen & (lane < LANES - 1), 2.0 ** -(1 << bit), 1.0)
    down = jnp.where(lane < LANES - 1, down, 0.0)
    return lane.astype(F32), up, down


def exponent_of(largest):
    _, up, down = powers()
    above = jnp.sum(jnp.where(up < largest, 1.0, 0.0), axis=1, keepdims=True)
    below = jnp.sum(jnp.where((down >= largest) & (down > 0.0), 1.0, 0.0), axis=1, keepdims=True)
    return jnp.clip(jnp.where(largest > 1.0, above, 1.0 - below), -126.0, 126.0)


def power(exponent):
    lane, up, down = powers()
    chosen = jnp.where(lane == exponent, up, 0.0)
    chosen = chosen + jnp.where((lane == -exponent) & (exponent < 0.0), down, 0.0)
    return jnp.sum(chosen, axis=1, keepdims=True)


def whole(values):
    return jnp.floor(values + 0.5)


def encode(block, line):
    largest = jnp.max(jnp.max(jnp.abs(block), axis=0, keepdims=True), axis=1, keepdims=True)
    exponent = exponent_of(largest)
    rows = [jnp.broadcast_to(exponent, line.shape)]
    block = whole(block * power(-exponent) * RANGE)
    exponent = exponent_of(jnp.max(jnp.abs(line), axis=1, keepdims=True))
    rows.append(jnp.broadcast_to(exponent, line.shape))
    rest = line * power(-exponent)
    for _ in range(3):
        rest = rest * DIGIT
        rows.append(whole(rest))
        rest = rest - rows[-1]
    rows.append(jnp.zeros((TILE - len(rows), LANES), F32))
    return jnp.concatenate([block] + rows, axis=0).astype(jnp.int32).astype(I16)


def decode(ref, count):
    size = ref.shape[1] - TILE
    tiles = [ref[j, size:].astype(jnp.int32).astype(F32) for j in range(count)]
    rows = [jnp.concatenate([tile[k : k + 1] for tile in tiles], axis=0) for k in range(5)]
    scales = power(rows[0][:, :1])
    blocks = [
        ref[j, :size].astype(jnp.int32).astype(F32) * (1.0 / RANGE) * scales[j : j + 1]
        for j in range(count)
    ]
    line = ((rows[4] / DIGIT + rows[3]) / DIGIT + rows[2]) / DIGIT * power(rows[1][:, :1])
    return blocks, jnp.sum(line, axis=0, keepdims=True)


def make(n_y, n_x, n_z):
    n_xy = n_y * n_x

    def per_device(psi, diag, block_dims, left_env, right_env):
        sectors, size, cols = psi.shape
        sub = cols // n_xy
        shard_rows = n_z * sub
        one = sub + 1
        scale = 1.0 / (size * size)
        core = lax.axis_index("core")
        swap = [(0, 1), (1, 0)]
        row = lax.broadcasted_iota(jnp.int32, (sectors + 2, 2), 0) - sectors
        col = lax.broadcasted_iota(jnp.int32, (sectors + 2, 2), 1)
        meta = jnp.where(
            row < 0,
            jnp.pad(block_dims, ((0, 2), (0, 0))),
            jnp.where(row > 0, lax.axis_index(XY), jnp.where(col == 0, core, lax.axis_index("sec"))),
        )
        share, shard = (size, cols), (sub, size)

        def a2a(array, axes):
            return lax.all_to_all(array, axes, 0, 0, tiled=True)

        def a2a_rows(array, parts, axes):
            blocks = array.reshape(parts, array.shape[0] // parts, 1, cols)
            return a2a(blocks, axes).reshape(array.shape)

        def dims_of(meta_ref, sector):
            return meta_ref[sector, 0], meta_ref[sector, 1]

        def place(meta_ref):
            return meta_ref[sectors, 0], meta_ref[sectors, 1], meta_ref[sectors + 1, 0]

        def share_mask(meta_ref, sector):
            row = lax.broadcasted_iota(jnp.int32, share, 0)
            col = lax.broadcasted_iota(jnp.int32, share, 1) + place(meta_ref)[1] * cols
            rows, columns = dims_of(meta_ref, sector)
            return (row < rows) & (col < columns)

        def own_rows(meta_ref, k):
            return pl.ds(pl.multiple_of(k * cols + place(meta_ref)[2] * sub, sub), sub)

        def start_kernel(meta_ref, psi_ref, out_ref, psi_a_ref):
            total = jnp.zeros((1, LANES), F32)
            for s in range(sectors):
                own = jnp.where(share_mask(meta_ref, s), psi_ref[s], 0.0)
                total = total + fold(own * own)

                @pl.when(place(meta_ref)[0] == s)
                def _():
                    psi_a_ref[...] = own

            for k in range(n_z):
                out_ref[pl.ds(k * one, sub)] = psi_a_ref[own_rows(meta_ref, k)]
                out_ref[pl.ds(k * one + sub, 1)] = total

        def left_matmul(meta_ref, env_ref, got_ref, field, left_ref):
            core, per = place(meta_ref)[0], PIECE // cols
            for i in range(size // PIECE):
                rows = pl.ds(i * PIECE, PIECE)
                for w in range(2):
                    env = env_ref[0, core, rows] if w == 0 else got_ref[rows]
                    part = jnp.dot(env, field, preferred_element_type=F32)
                    left_ref[i * per : (i + 1) * per, w] = part.astype(BF16).reshape(per, cols, cols)

        def first_kernel(meta_ref, got_ref, psi_a_ref, env_ref, env2_ref, u_a_ref, u_b_ref, left_ref):
            norm = jnp.sum(add_rows(got_ref, sub, one, n_z), axis=1, keepdims=True) * scale
            inverse = 1.0 / jnp.sqrt(norm)
            u_a = psi_a_ref[...] * inverse
            u_a_ref[...] = u_a
            for k in range(n_z):
                lanes = slice(k * cols, (k + 1) * cols)
                u_b_ref[:, lanes] = got_ref[pl.ds(k * one, sub)] * inverse
            left_matmul(meta_ref, env_ref, env2_ref, u_a.astype(BF16), left_ref)

        def right_pieces(meta_ref, moved_ref, env_ref, got_ref):
            core = place(meta_ref)[0]
            fields = [
                jnp.concatenate([moved_ref[k, w] for k in range(n_z)], axis=1) for w in range(2)
            ]
            for i in range(size // PIECE):
                rows = pl.ds(i * PIECE, PIECE)
                total = None
                for w in range(2):
                    env = env_ref[0, core, rows] if w == 0 else got_ref[rows]
                    part = lax.dot_general(
                        fields[w], env, (((1,), (1,)), ((), ())), preferred_element_type=F32
                    )
                    total = part if total is None else total + part
                yield rows, total

        def right_kernel(meta_ref, moved_ref, env_ref, got_ref, out_ref):
            for rows, total in right_pieces(meta_ref, moved_ref, env_ref, got_ref):
                out_ref[:, :, rows] = total.reshape(n_xy, sub, PIECE).astype(out_ref.dtype)

        def first_right_kernel(meta_ref, moved_ref, env_ref, got_ref, out_ref):
            parts = [total for _, total in right_pieces(meta_ref, moved_ref, env_ref, got_ref)]
            partial = jnp.concatenate(parts, axis=1)
            largest = jnp.max(jnp.max(jnp.abs(partial), axis=0, keepdims=True), axis=1, keepdims=True)
            exponent = exponent_of(largest)
            partial = whole(partial * power(-exponent) * RANGE)
            tile = jnp.broadcast_to(exponent, (TILE, cols)).astype(jnp.int32).astype(I16)
            for j in range(n_xy):
                rows = partial[j * sub : (j + 1) * sub]
                rows = [rows[:, k * cols : (k + 1) * cols] for k in range(n_z)]
                block = jnp.concatenate(rows, axis=0).astype(jnp.int32).astype(I16)
                out_ref[j, :shard_rows] = block
                out_ref[j, shard_rows:] = tile

        def first_sum(got_ref):
            tiles = [got_ref[j, shard_rows:].astype(jnp.int32).astype(F32) for j in range(n_xy)]
            scales = power(jnp.concatenate([tile[:1] for tile in tiles], axis=0)[:, :1])
            total = jnp.zeros((shard_rows, cols), F32)
            for j in range(n_xy):
                block = got_ref[j, :shard_rows].astype(jnp.int32).astype(F32)
                total = total + block * (1.0 / RANGE) * scales[j : j + 1]
            return jnp.concatenate([total[k * sub : (k + 1) * sub] for k in range(n_z)], axis=1)

        def image_of(meta_ref, image):
            core, z, q = place(meta_ref)
            row = lax.broadcasted_iota(jnp.int32, shard, 0) + (z * cols + q * sub)
            col = lax.broadcasted_iota(jnp.int32, shard, 1)
            rows, columns = dims_of(meta_ref, core)
            return jnp.where((row < rows) & (col < columns), image, 0.0)

        def dots_line(image, u_b_ref, more):
            u = u_b_ref[...]
            if not more:
                return line_of([fold(u * image)])
            corr, hu = more[0][...], more[1][...]
            pairs = [(u, image), (corr, hu), (corr, image), (u, corr), (corr, corr), (u, u)]
            return line_of([fold(a * b) for a, b in pairs])

        def first_image_kernel(meta_ref, got_ref, u_b_ref, diag_ref, image_ref, out_ref):
            image = image_of(meta_ref, first_sum(got_ref))
            image_ref[...] = image
            line = dots_line(image, u_b_ref, ())
            for k in range(n_z):
                for c in range(2):
                    shard_k = image[:, k * cols : (k + 1) * cols]
                    rows = jnp.where(place(meta_ref)[0] == c, shard_k, diag_ref[c, own_rows(meta_ref, k)])
                    out_ref[pl.ds((c * n_z + k) * one, sub)] = rows
                    out_ref[pl.ds((c * n_z + k) * one + sub, 1)] = line

        def image_kernel(meta_ref, got_ref, u_b_ref, corr_b_ref, hu_b_ref, image_ref, out_ref):
            image = image_of(meta_ref, jnp.sum(got_ref[...].astype(F32), axis=0))
            image_ref[...] = image
            line = dots_line(image, u_b_ref, (corr_b_ref, hu_b_ref))
            for k in range(2 * n_z):
                out_ref[pl.ds(k * one, sub)] = image[:, (k % n_z) * cols : (k % n_z + 1) * cols]
                out_ref[pl.ds(k * one + sub, 1)] = line

        def last_image_kernel(meta_ref, got_ref, u_b_ref, corr_b_ref, hu_b_ref, out_ref):
            image = image_of(meta_ref, jnp.sum(got_ref[...].astype(F32), axis=0))
            line = dots_line(image, u_b_ref, (corr_b_ref, hu_b_ref))
            out_ref[...] = jnp.broadcast_to(line, out_ref.shape)

        def from_cores(meta_ref, got_ref, k):
            zero, other = [got_ref[pl.ds((c * n_z + k) * one, sub)] for c in range(2)]
            first = place(meta_ref)[0] == 0
            return jnp.where(first, zero, other), jnp.where(first, other, zero)

        def spread_kernel(meta_ref, got_ref, out_ref, *diag_b_ref):
            line = add_rows(got_ref, sub, one, 2 * n_z)
            shards = []
            for k in range(n_z):
                rows, far = from_cores(meta_ref, got_ref, k)
                shards.append(rows)
                for ref in diag_b_ref:
                    ref[:, k * cols : (k + 1) * cols] = far
            block = encode(jnp.concatenate(shards, axis=0), line)
            out_ref[...] = jnp.broadcast_to(block[None], out_ref.shape)

        def projected(theta, sums):
            u_image, corr_hu, corr_image, project, size_corr, size_u = sums
            inverse = 1.0 / jnp.sqrt(size_corr - project * project * (2.0 - size_u))
            cross = 0.5 * ((u_image - project * theta) + (corr_hu - project * theta)) * inverse
            corner = corr_image - project * (corr_hu + u_image) + project * project * theta
            corner = corner * inverse * inverse
            half = 0.5 * (theta - corner)
            lowest = 0.5 * (theta + corner) - jnp.sqrt(half * half + cross * cross)
            x, y = corner - lowest, -cross
            length = jnp.sqrt(x * x + y * y)
            x, y = x / length, y / length
            theta = x * x * theta + 2.0 * x * y * cross + y * y * corner
            return x - y * project * inverse, y * inverse, theta, lowest

        def correction(theta, image, vector, diagonal):
            return (image - theta * vector) / (1.0 + jnp.abs(diagonal - theta))

        def share_of(parts):
            parts = [part.reshape(n_z, 1, sub, cols) for part in parts]
            return jnp.concatenate(parts, axis=1).reshape(share)

        def begin_kernel(meta_ref, got_ref, u_a_ref, u_b_ref, hu_b_ref, diag_ref, diag_b_ref, env_ref, env2_ref, hu_a_ref, corr_a_ref, corr_b_ref, theta_ref, left_ref):
            blocks, line = decode(got_ref, n_xy)
            theta = line[:, :1] * scale
            theta_ref[...] = jnp.broadcast_to(theta, theta_ref.shape)
            hu_a = share_of(blocks)
            hu_a_ref[...] = hu_a
            corr_a = correction(theta, hu_a, u_a_ref[...], diag_ref[place(meta_ref)[0]])
            corr_a_ref[...] = corr_a
            corr_b_ref[...] = correction(theta, hu_b_ref[...], u_b_ref[...], diag_b_ref[...])
            left_matmul(meta_ref, env_ref, env2_ref, corr_a.astype(BF16), left_ref)

        def update_kernel(meta_ref, got_ref, old_theta_ref, u_a_ref, corr_a_ref, hu_a_ref, u_b_ref, corr_b_ref, hu_b_ref, hc_b_ref, diag_ref, diag_b_ref, env_ref, env2_ref, u_a_out, corr_a_out, u_b_out, corr_b_out, hu_b_out, theta_ref, left_ref, *hu_a_out):
            blocks, line = decode(got_ref, n_xy)
            sums = [line[:, k : k + 1] * scale for k in range(6)]
            old, new, theta, _ = projected(old_theta_ref[0:1, 0:1], sums)
            theta_ref[...] = jnp.broadcast_to(theta, theta_ref.shape)
            u_a = old * u_a_ref[...] + new * corr_a_ref[...]
            hu_a = old * hu_a_ref[...] + new * share_of(blocks)
            corr_a = correction(theta, hu_a, u_a, diag_ref[place(meta_ref)[0]])
            u_a_out[...], corr_a_out[...] = u_a, corr_a
            for ref in hu_a_out:
                ref[...] = hu_a
            u_b = old * u_b_ref[...] + new * corr_b_ref[...]
            hu_b = old * hu_b_ref[...] + new * hc_b_ref[...]
            u_b_out[...], hu_b_out[...] = u_b, hu_b
            corr_b_out[...] = correction(theta, hu_b, u_b, diag_b_ref[...])
            left_matmul(meta_ref, env_ref, env2_ref, corr_a.astype(BF16), left_ref)

        def last_kernel(meta_ref, got_ref, theta_ref, u_a_ref, corr_a_ref, u_far_ref, corr_far_ref, out_ref, energy_ref):
            line = jnp.sum(got_ref[...], axis=0, keepdims=True) * scale
            sums = [line[:, k : k + 1] for k in range(6)]
            old, new, _, lowest = projected(theta_ref[0:1, 0:1], sums)
            c = place(meta_ref)[0]
            energy_ref[...] = lowest
            out_ref[c] = old * u_a_ref[...] + new * corr_a_ref[...]
            out_ref[1 - c] = old * u_far_ref[...] + new * corr_far_ref[...]

        def v(*arrays):
            return [(a, VMEM) for a in arrays]

        i_meta = [(meta, SMEM)]
        left_out = ((n_z, 2, cols, cols), BF16)
        tile_out, a_out, b_out = ((8, cols), F32), (share, F32), (shard, F32)
        work = 4 * size * size * cols

        first, psi_a = call(
            start_kernel, [((n_z * one, cols), F32), a_out], i_meta + v(psi), (), START
        )

        def swapped(env, other):
            give = lax.dynamic_slice(
                env, (0, other, 0, 0), (1, 1, size, size), allow_negative_indices=False
            )
            return lax.ppermute(give.reshape(size, size), "core", swap)

        first, left_env, other = lax.optimization_barrier((first, left_env, 1 - core))
        lefts = v(left_env, swapped(left_env, other))
        first = a2a_rows(first, n_z, "sec")
        u_a, u_b, left = call(
            first_kernel, [a_out, b_out, left_out], i_meta + v(first, psi_a) + lefts, (), work
        )
        left, right_env = lax.optimization_barrier((left, right_env))
        rights = v(right_env, swapped(right_env, other))

        gathered = ((n_xy, shard_rows + TILE, cols), I16)

        def apply_right(left, kernel, out):
            moved = a2a(left, "sec")
            (partial,) = call(kernel, [out], i_meta + v(moved) + rights, (), work)
            return a2a(partial, XY)

        summed = ((n_xy, sub, size), BF16)
        payload_out = ((2 * n_z * one, cols), F32)
        got = apply_right(left, first_right_kernel, gathered)
        hu_b, payload = call(
            first_image_kernel,
            [b_out, payload_out],
            i_meta + v(got, u_b, diag),
        )
        payload, diag_b = call(
            spread_kernel, [gathered, b_out], i_meta + v(a2a_rows(payload, 2 * n_z, CZ))
        )
        got = a2a(payload, XY)
        hu_a, corr_a, corr_b, theta, left = call(
            begin_kernel,
            [a_out, a_out, b_out, tile_out, left_out],
            i_meta + v(got, u_a, u_b, hu_b, diag, diag_b) + lefts, (), work,
        )
        for step in range(ITERS - 1):
            got = apply_right(left, right_kernel, summed)
            hc_b, payload = call(
                image_kernel, [b_out, payload_out], i_meta + v(got, u_b, corr_b, hu_b)
            )
            (payload,) = call(
                spread_kernel, [gathered], i_meta + v(a2a_rows(payload, 2 * n_z, CZ))
            )
            got = a2a(payload, XY)
            more = [a_out] * (step < ITERS - 2)
            u_a, corr_a, u_b, corr_b, hu_b, theta, left, *more = call(
                update_kernel,
                [a_out, a_out, b_out, b_out, b_out, tile_out, left_out] + more,
                i_meta + v(got, theta, u_a, corr_a, hu_a, u_b, corr_b, hu_b, hc_b, diag, diag_b) + lefts,
                (), work,
            )
            (hu_a,) = more or (None,)
        got = apply_right(left, right_kernel, summed)
        got, u_send, corr_send = lax.optimization_barrier((got, u_a, corr_a))
        u_far = lax.ppermute(u_send, "core", swap)
        corr_far = lax.ppermute(corr_send, "core", swap)
        (sums,) = call(
            last_image_kernel, [((2 * n_z * n_xy, cols), F32)], i_meta + v(got, u_b, corr_b, hu_b)
        )
        sums = a2a(sums, ALL)
        out, energy = call(
            last_kernel, [(psi.shape, F32), ((1, 1), F32)],
            i_meta + v(sums, theta, u_a, corr_a, u_far, corr_far),
        )
        return out, energy.reshape(())

    return per_device


def solution(mesh):
    n_z = mesh.shape["sec"]
    n_y = n_x = int(round((mesh.shape["term"] // 2) ** 0.5))
    fine = Mesh(mesh.devices.reshape(n_y, n_x, 2, n_z), ("y", "x", "core", "sec"))
    term = ("y", "x", "core")
    in_specs = (
        P(None, None, "sec"),
        P(None, None, "sec"),
        P(),
        P(term, None, None, None),
        P(term, None, None, None),
    )
    out_specs = (P(None, None, "sec"), P())
    return jax.shard_map(
        make(n_y, n_x, n_z), mesh=fine, in_specs=in_specs, out_specs=out_specs, check_vma=False
    )
```

```python
import functools

import jax
import jax.numpy as jnp
from jax import lax
from jax.experimental import pallas as pl
from jax.experimental.pallas import tpu as pltpu
from jax.sharding import Mesh, PartitionSpec as P

ITERS = 2
XY = ("y", "x")
CZ = ("core", "sec")
ALL = ("y", "x", "core", "sec")
LANES = 128
PIECE = 1024
TILE = 16
RANGE = 32000.0
DIGIT = 2.0**14
I16 = jnp.int16
LIMIT = 24
START = 4 * 10**9
F32 = jnp.float32
BF16 = jnp.bfloat16
SMEM = pl.BlockSpec(memory_space=pltpu.SMEM)
VMEM = pl.BlockSpec(memory_space=pltpu.VMEM)


def call(kernel, outs, ins, scratch=(), flops=0):
    moved = sum(int(a.size) * a.dtype.itemsize for a, _ in ins)
    return pl.pallas_call(
        kernel,
        out_shape=[jax.ShapeDtypeStruct(s, d) for s, d in outs],
        in_specs=[s for _, s in ins],
        out_specs=[VMEM] * len(outs),
        scratch_shapes=list(scratch),
        compiler_params=pltpu.CompilerParams(vmem_limit_bytes=LIMIT * 2**20),
        cost_estimate=pl.CostEstimate(flops=flops, bytes_accessed=moved, transcendentals=0),
    )(*[a for a, _ in ins])


def fold(product):
    parts = [product[:, k : k + LANES] for k in range(0, product.shape[1], LANES)]
    return jnp.sum(functools.reduce(lambda a, b: a + b, parts), axis=0, keepdims=True)


def line_of(rows):
    tile = jnp.concatenate(rows + [jnp.zeros((8 - len(rows), LANES), F32)], axis=0)
    sums = jnp.sum(tile, axis=1, keepdims=True)
    row = lax.broadcasted_iota(jnp.int32, tile.shape, 0)
    lane = lax.broadcasted_iota(jnp.int32, tile.shape, 1)
    return jnp.sum(jnp.where(row == lane, sums, 0.0), axis=0, keepdims=True)


def add_rows(ref, start, step, count):
    return functools.reduce(lambda a, b: a + b, [ref[pl.ds(start + step * k, 1)] for k in range(count)])


def powers():
    lane = lax.broadcasted_iota(jnp.int32, (1, LANES), 1)
    up, down = jnp.ones((1, LANES), F32), jnp.ones((1, LANES), F32)
    for bit in range(7):
        chosen = (lane >> bit) % 2 == 1
        up = up * jnp.where(chosen, 2.0 ** (1 << bit), 1.0)
        down = down * jnp.where(chosen & (lane < LANES - 1), 2.0 ** -(1 << bit), 1.0)
    down = jnp.where(lane < LANES - 1, down, 0.0)
    return lane.astype(F32), up, down


def exponent_of(largest):
    _, up, down = powers()
    above = jnp.sum(jnp.where(up < largest, 1.0, 0.0), axis=1, keepdims=True)
    below = jnp.sum(jnp.where((down >= largest) & (down > 0.0), 1.0, 0.0), axis=1, keepdims=True)
    return jnp.clip(jnp.where(largest > 1.0, above, 1.0 - below), -126.0, 126.0)


def power(exponent):
    lane, up, down = powers()
    chosen = jnp.where(lane == exponent, up, 0.0)
    chosen = chosen + jnp.where((lane == -exponent) & (exponent < 0.0), down, 0.0)
    return jnp.sum(chosen, axis=1, keepdims=True)


def whole(values):
    return jnp.floor(values + 0.5)


def encode(block, line):
    largest = jnp.max(jnp.max(jnp.abs(block), axis=0, keepdims=True), axis=1, keepdims=True)
    exponent = exponent_of(largest)
    rows = [jnp.broadcast_to(exponent, line.shape)]
    block = whole(block * power(-exponent) * RANGE)
    exponent = exponent_of(jnp.max(jnp.abs(line), axis=1, keepdims=True))
    rows.append(jnp.broadcast_to(exponent, line.shape))
    rest = line * power(-exponent)
    for _ in range(3):
        rest = rest * DIGIT
        rows.append(whole(rest))
        rest = rest - rows[-1]
    rows.append(jnp.zeros((TILE - len(rows), LANES), F32))
    return jnp.concatenate([block] + rows, axis=0).astype(jnp.int32).astype(I16)


def decode(ref, count):
    size = ref.shape[1] - TILE
    tiles = [ref[j, size:].astype(jnp.int32).astype(F32) for j in range(count)]
    rows = [jnp.concatenate([tile[k : k + 1] for tile in tiles], axis=0) for k in range(5)]
    scales = power(rows[0][:, :1])
    blocks = [
        ref[j, :size].astype(jnp.int32).astype(F32) * (1.0 / RANGE) * scales[j : j + 1]
        for j in range(count)
    ]
    line = ((rows[4] / DIGIT + rows[3]) / DIGIT + rows[2]) / DIGIT * power(rows[1][:, :1])
    return blocks, jnp.sum(line, axis=0, keepdims=True)


def make(n_y, n_x, n_z):
    n_xy = n_y * n_x

    def per_device(psi, diag, block_dims, left_env, right_env):
        sectors, size, cols = psi.shape
        sub = cols // n_xy
        shard_rows = n_z * sub
        one = sub + 1
        scale = 1.0 / (size * size)
        core = lax.axis_index("core")
        swap = [(0, 1), (1, 0)]
        row = lax.broadcasted_iota(jnp.int32, (sectors + 2, 2), 0) - sectors
        col = lax.broadcasted_iota(jnp.int32, (sectors + 2, 2), 1)
        meta = jnp.where(
            row < 0,
            jnp.pad(block_dims, ((0, 2), (0, 0))),
            jnp.where(row > 0, lax.axis_index(XY), jnp.where(col == 0, core, lax.axis_index("sec"))),
        )
        share, shard = (size, cols), (sub, size)

        def a2a(array, axes):
            return lax.all_to_all(array, axes, 0, 0, tiled=True)

        def a2a_rows(array, parts, axes):
            blocks = array.reshape(parts, array.shape[0] // parts, 1, cols)
            return a2a(blocks, axes).reshape(array.shape)

        def dims_of(meta_ref, sector):
            return meta_ref[sector, 0], meta_ref[sector, 1]

        def place(meta_ref):
            return meta_ref[sectors, 0], meta_ref[sectors, 1], meta_ref[sectors + 1, 0]

        def share_mask(meta_ref, sector):
            row = lax.broadcasted_iota(jnp.int32, share, 0)
            col = lax.broadcasted_iota(jnp.int32, share, 1) + place(meta_ref)[1] * cols
            rows, columns = dims_of(meta_ref, sector)
            return (row < rows) & (col < columns)

        def own_rows(meta_ref, k):
            return pl.ds(pl.multiple_of(k * cols + place(meta_ref)[2] * sub, sub), sub)

        def start_kernel(meta_ref, psi_ref, out_ref, psi_a_ref):
            total = jnp.zeros((1, LANES), F32)
            for s in range(sectors):
                own = jnp.where(share_mask(meta_ref, s), psi_ref[s], 0.0)
                total = total + fold(own * own)

                @pl.when(place(meta_ref)[0] == s)
                def _():
                    psi_a_ref[...] = own

            for k in range(n_z):
                out_ref[pl.ds(k * one, sub)] = psi_a_ref[own_rows(meta_ref, k)]
                out_ref[pl.ds(k * one + sub, 1)] = total

        def left_matmul(meta_ref, env_ref, got_ref, field, left_ref):
            core, per = place(meta_ref)[0], PIECE // cols
            for i in range(size // PIECE):
                rows = pl.ds(i * PIECE, PIECE)
                for w in range(2):
                    env = env_ref[0, core, rows] if w == 0 else got_ref[rows]
                    part = jnp.dot(env, field, preferred_element_type=F32)
                    left_ref[i * per : (i + 1) * per, w] = part.astype(BF16).reshape(per, cols, cols)

        def first_kernel(meta_ref, got_ref, psi_a_ref, env_ref, env2_ref, u_a_ref, u_b_ref, left_ref):
            norm = jnp.sum(add_rows(got_ref, sub, one, n_z), axis=1, keepdims=True) * scale
            inverse = 1.0 / jnp.sqrt(norm)
            u_a = psi_a_ref[...] * inverse
            u_a_ref[...] = u_a
            for k in range(n_z):
                lanes = slice(k * cols, (k + 1) * cols)
                u_b_ref[:, lanes] = got_ref[pl.ds(k * one, sub)] * inverse
            left_matmul(meta_ref, env_ref, env2_ref, u_a.astype(BF16), left_ref)

        def right_pieces(meta_ref, moved_ref, env_ref, got_ref):
            core = place(meta_ref)[0]
            fields = [
                jnp.concatenate([moved_ref[k, w] for k in range(n_z)], axis=1) for w in range(2)
            ]
            for i in range(size // PIECE):
                rows = pl.ds(i * PIECE, PIECE)
                total = None
                for w in range(2):
                    env = env_ref[0, core, rows] if w == 0 else got_ref[rows]
                    part = lax.dot_general(
                        fields[w], env, (((1,), (1,)), ((), ())), preferred_element_type=F32
                    )
                    total = part if total is None else total + part
                yield rows, total

        def right_kernel(meta_ref, moved_ref, env_ref, got_ref, out_ref):
            for rows, total in right_pieces(meta_ref, moved_ref, env_ref, got_ref):
                out_ref[:, :, rows] = total.reshape(n_xy, sub, PIECE).astype(out_ref.dtype)

        def first_right_kernel(meta_ref, moved_ref, env_ref, got_ref, out_ref):
            parts = [total for _, total in right_pieces(meta_ref, moved_ref, env_ref, got_ref)]
            partial = jnp.concatenate(parts, axis=1)
            sizes = jnp.abs(partial)
            rows = [
                jnp.max(sizes[j * sub : (j + 1) * sub], axis=0, keepdims=True) for j in range(n_xy)
            ]
            exponents = exponent_of(jnp.max(jnp.concatenate(rows, axis=0), axis=1, keepdims=True))
            scales = power(-exponents)
            tiles = jnp.broadcast_to(exponents, (n_xy, cols))
            for j in range(n_xy):
                rows = partial[j * sub : (j + 1) * sub] * scales[j : j + 1] * RANGE
                rows = [rows[:, k * cols : (k + 1) * cols] for k in range(n_z)]
                tile = jnp.broadcast_to(tiles[j : j + 1], (TILE, cols))
                block = jnp.concatenate([whole(jnp.concatenate(rows, axis=0)), tile], axis=0)
                out_ref[j] = block.astype(jnp.int32).astype(I16)

        def first_sum(got_ref):
            tiles = [got_ref[j, shard_rows:].astype(jnp.int32).astype(F32) for j in range(n_xy)]
            scales = power(jnp.concatenate([tile[:1] for tile in tiles], axis=0)[:, :1])
            total = jnp.zeros((shard_rows, cols), F32)
            for j in range(n_xy):
                block = got_ref[j, :shard_rows].astype(jnp.int32).astype(F32)
                total = total + block * (1.0 / RANGE) * scales[j : j + 1]
            return jnp.concatenate([total[k * sub : (k + 1) * sub] for k in range(n_z)], axis=1)

        def image_of(meta_ref, image):
            core, z, q = place(meta_ref)
            row = lax.broadcasted_iota(jnp.int32, shard, 0) + (z * cols + q * sub)
            col = lax.broadcasted_iota(jnp.int32, shard, 1)
            rows, columns = dims_of(meta_ref, core)
            return jnp.where((row < rows) & (col < columns), image, 0.0)

        def dots_line(image, u_b_ref, more):
            u = u_b_ref[...]
            if not more:
                return line_of([fold(u * image)])
            corr, hu = more[0][...], more[1][...]
            pairs = [(u, image), (corr, hu), (corr, image), (u, corr), (corr, corr), (u, u)]
            return line_of([fold(a * b) for a, b in pairs])

        def first_image_kernel(meta_ref, got_ref, u_b_ref, diag_ref, image_ref, out_ref):
            image = image_of(meta_ref, first_sum(got_ref))
            image_ref[...] = image
            line = dots_line(image, u_b_ref, ())
            for k in range(n_z):
                for c in range(2):
                    shard_k = image[:, k * cols : (k + 1) * cols]
                    rows = jnp.where(place(meta_ref)[0] == c, shard_k, diag_ref[c, own_rows(meta_ref, k)])
                    out_ref[pl.ds((c * n_z + k) * one, sub)] = rows
                    out_ref[pl.ds((c * n_z + k) * one + sub, 1)] = line

        def image_kernel(meta_ref, got_ref, u_b_ref, corr_b_ref, hu_b_ref, image_ref, out_ref):
            image = image_of(meta_ref, jnp.sum(got_ref[...].astype(F32), axis=0))
            image_ref[...] = image
            line = dots_line(image, u_b_ref, (corr_b_ref, hu_b_ref))
            for k in range(2 * n_z):
                out_ref[pl.ds(k * one, sub)] = image[:, (k % n_z) * cols : (k % n_z + 1) * cols]
                out_ref[pl.ds(k * one + sub, 1)] = line

        def last_image_kernel(meta_ref, got_ref, u_b_ref, corr_b_ref, hu_b_ref, out_ref):
            image = image_of(meta_ref, jnp.sum(got_ref[...].astype(F32), axis=0))
            line = dots_line(image, u_b_ref, (corr_b_ref, hu_b_ref))
            out_ref[...] = jnp.broadcast_to(line, out_ref.shape)

        def from_cores(meta_ref, got_ref, k):
            zero, other = [got_ref[pl.ds((c * n_z + k) * one, sub)] for c in range(2)]
            first = place(meta_ref)[0] == 0
            return jnp.where(first, zero, other), jnp.where(first, other, zero)

        def spread_kernel(meta_ref, got_ref, out_ref, *diag_b_ref):
            line = add_rows(got_ref, sub, one, 2 * n_z)
            shards = []
            for k in range(n_z):
                rows, far = from_cores(meta_ref, got_ref, k)
                shards.append(rows)
                for ref in diag_b_ref:
                    ref[:, k * cols : (k + 1) * cols] = far
            block = encode(jnp.concatenate(shards, axis=0), line)
            out_ref[...] = jnp.broadcast_to(block[None], out_ref.shape)

        def projected(theta, sums):
            u_image, corr_hu, corr_image, project, size_corr, size_u = sums
            inverse = 1.0 / jnp.sqrt(size_corr - project * project * (2.0 - size_u))
            cross = 0.5 * ((u_image - project * theta) + (corr_hu - project * theta)) * inverse
            corner = corr_image - project * (corr_hu + u_image) + project * project * theta
            corner = corner * inverse * inverse
            half = 0.5 * (theta - corner)
            lowest = 0.5 * (theta + corner) - jnp.sqrt(half * half + cross * cross)
            x, y = corner - lowest, -cross
            length = jnp.sqrt(x * x + y * y)
            x, y = x / length, y / length
            theta = x * x * theta + 2.0 * x * y * cross + y * y * corner
            return x - y * project * inverse, y * inverse, theta, lowest

        def correction(theta, image, vector, diagonal):
            return (image - theta * vector) / (1.0 + jnp.abs(diagonal - theta))

        def share_of(parts):
            parts = [part.reshape(n_z, 1, sub, cols) for part in parts]
            return jnp.concatenate(parts, axis=1).reshape(share)

        def begin_kernel(meta_ref, got_ref, u_a_ref, u_b_ref, hu_b_ref, diag_ref, diag_b_ref, env_ref, env2_ref, hu_a_ref, corr_a_ref, corr_b_ref, theta_ref, left_ref):
            blocks, line = decode(got_ref, n_xy)
            theta = line[:, :1] * scale
            theta_ref[...] = jnp.broadcast_to(theta, theta_ref.shape)
            hu_a = share_of(blocks)
            hu_a_ref[...] = hu_a
            corr_a = correction(theta, hu_a, u_a_ref[...], diag_ref[place(meta_ref)[0]])
            corr_a_ref[...] = corr_a
            corr_b_ref[...] = correction(theta, hu_b_ref[...], u_b_ref[...], diag_b_ref[...])
            left_matmul(meta_ref, env_ref, env2_ref, corr_a.astype(BF16), left_ref)

        def update_kernel(meta_ref, got_ref, old_theta_ref, u_a_ref, corr_a_ref, hu_a_ref, u_b_ref, corr_b_ref, hu_b_ref, hc_b_ref, diag_ref, diag_b_ref, env_ref, env2_ref, u_a_out, corr_a_out, u_b_out, corr_b_out, hu_b_out, theta_ref, left_ref, *hu_a_out):
            blocks, line = decode(got_ref, n_xy)
            sums = [line[:, k : k + 1] * scale for k in range(6)]
            old, new, theta, _ = projected(old_theta_ref[0:1, 0:1], sums)
            theta_ref[...] = jnp.broadcast_to(theta, theta_ref.shape)
            u_a = old * u_a_ref[...] + new * corr_a_ref[...]
            hu_a = old * hu_a_ref[...] + new * share_of(blocks)
            corr_a = correction(theta, hu_a, u_a, diag_ref[place(meta_ref)[0]])
            u_a_out[...], corr_a_out[...] = u_a, corr_a
            for ref in hu_a_out:
                ref[...] = hu_a
            u_b = old * u_b_ref[...] + new * corr_b_ref[...]
            hu_b = old * hu_b_ref[...] + new * hc_b_ref[...]
            u_b_out[...], hu_b_out[...] = u_b, hu_b
            corr_b_out[...] = correction(theta, hu_b, u_b, diag_b_ref[...])
            left_matmul(meta_ref, env_ref, env2_ref, corr_a.astype(BF16), left_ref)

        def last_kernel(meta_ref, got_ref, theta_ref, u_a_ref, corr_a_ref, u_far_ref, corr_far_ref, out_ref, energy_ref):
            line = jnp.sum(got_ref[...], axis=0, keepdims=True) * scale
            sums = [line[:, k : k + 1] for k in range(6)]
            old, new, _, lowest = projected(theta_ref[0:1, 0:1], sums)
            c = place(meta_ref)[0]
            energy_ref[...] = lowest
            out_ref[c] = old * u_a_ref[...] + new * corr_a_ref[...]
            out_ref[1 - c] = old * u_far_ref[...] + new * corr_far_ref[...]

        def v(*arrays):
            return [(a, VMEM) for a in arrays]

        i_meta = [(meta, SMEM)]
        left_out = ((n_z, 2, cols, cols), BF16)
        tile_out, a_out, b_out = ((8, cols), F32), (share, F32), (shard, F32)
        work = 4 * size * size * cols

        first, psi_a = call(
            start_kernel, [((n_z * one, cols), F32), a_out], i_meta + v(psi), (), START
        )

        def swapped(env, other):
            give = lax.dynamic_slice(
                env, (0, other, 0, 0), (1, 1, size, size), allow_negative_indices=False
            )
            return lax.ppermute(give.reshape(size, size), "core", swap)

        first, left_env, other = lax.optimization_barrier((first, left_env, 1 - core))
        lefts = v(left_env, swapped(left_env, other))
        first = a2a_rows(first, n_z, "sec")
        u_a, u_b, left = call(
            first_kernel, [a_out, b_out, left_out], i_meta + v(first, psi_a) + lefts, (), work
        )
        left, right_env = lax.optimization_barrier((left, right_env))
        rights = v(right_env, swapped(right_env, other))

        gathered = ((n_xy, shard_rows + TILE, cols), I16)

        def apply_right(left, kernel, out):
            moved = a2a(left, "sec")
            (partial,) = call(kernel, [out], i_meta + v(moved) + rights, (), work)
            return a2a(partial, XY)

        summed = ((n_xy, sub, size), BF16)
        payload_out = ((2 * n_z * one, cols), F32)
        got = apply_right(left, first_right_kernel, gathered)
        hu_b, payload = call(
            first_image_kernel,
            [b_out, payload_out],
            i_meta + v(got, u_b, diag),
        )
        payload, diag_b = call(
            spread_kernel, [gathered, b_out], i_meta + v(a2a_rows(payload, 2 * n_z, CZ))
        )
        got = a2a(payload, XY)
        hu_a, corr_a, corr_b, theta, left = call(
            begin_kernel,
            [a_out, a_out, b_out, tile_out, left_out],
            i_meta + v(got, u_a, u_b, hu_b, diag, diag_b) + lefts, (), work,
        )
        for step in range(ITERS - 1):
            got = apply_right(left, right_kernel, summed)
            hc_b, payload = call(
                image_kernel, [b_out, payload_out], i_meta + v(got, u_b, corr_b, hu_b)
            )
            (payload,) = call(
                spread_kernel, [gathered], i_meta + v(a2a_rows(payload, 2 * n_z, CZ))
            )
            got = a2a(payload, XY)
            more = [a_out] * (step < ITERS - 2)
            u_a, corr_a, u_b, corr_b, hu_b, theta, left, *more = call(
                update_kernel,
                [a_out, a_out, b_out, b_out, b_out, tile_out, left_out] + more,
                i_meta + v(got, theta, u_a, corr_a, hu_a, u_b, corr_b, hu_b, hc_b, diag, diag_b) + lefts,
                (), work,
            )
            (hu_a,) = more or (None,)
        got = apply_right(left, right_kernel, summed)
        got, u_send, corr_send = lax.optimization_barrier((got, u_a, corr_a))
        u_far = lax.ppermute(u_send, "core", swap)
        corr_far = lax.ppermute(corr_send, "core", swap)
        (sums,) = call(
            last_image_kernel, [((2 * n_z * n_xy, cols), F32)], i_meta + v(got, u_b, corr_b, hu_b)
        )
        sums = a2a(sums, ALL)
        out, energy = call(
            last_kernel, [(psi.shape, F32), ((1, 1), F32)],
            i_meta + v(sums, theta, u_a, corr_a, u_far, corr_far),
        )
        return out, energy.reshape(())

    return per_device


def solution(mesh):
    n_z = mesh.shape["sec"]
    n_y = n_x = int(round((mesh.shape["term"] // 2) ** 0.5))
    fine = Mesh(mesh.devices.reshape(n_y, n_x, 2, n_z), ("y", "x", "core", "sec"))
    term = ("y", "x", "core")
    in_specs = (
        P(None, None, "sec"),
        P(None, None, "sec"),
        P(),
        P(term, None, None, None),
        P(term, None, None, None),
    )
    out_specs = (P(None, None, "sec"), P())
    return jax.shard_map(
        make(n_y, n_x, n_z), mesh=fine, in_specs=in_specs, out_specs=out_specs, check_vma=False
    )
```

```python
import functools

import jax
import jax.numpy as jnp
from jax import lax
from jax.experimental import pallas as pl
from jax.experimental.pallas import tpu as pltpu
from jax.sharding import Mesh, PartitionSpec as P

ITERS = 2
XY = ("y", "x")
CZ = ("core", "sec")
ALL = ("core", "sec", "y", "x")
LANES = 128
PIECE = 1024
TILE = 16
RANGE = 32000.0
DIGIT = 2.0**14
I16 = jnp.int16
LIMIT = 24
START = 4 * 10**9
F32 = jnp.float32
BF16 = jnp.bfloat16
SMEM = pl.BlockSpec(memory_space=pltpu.SMEM)
VMEM = pl.BlockSpec(memory_space=pltpu.VMEM)


def call(kernel, outs, ins, scratch=(), flops=0):
    moved = sum(int(a.size) * a.dtype.itemsize for a, _ in ins)
    return pl.pallas_call(
        kernel,
        out_shape=[jax.ShapeDtypeStruct(s, d) for s, d in outs],
        in_specs=[s for _, s in ins],
        out_specs=[VMEM] * len(outs),
        scratch_shapes=list(scratch),
        compiler_params=pltpu.CompilerParams(vmem_limit_bytes=LIMIT * 2**20),
        cost_estimate=pl.CostEstimate(flops=flops, bytes_accessed=moved, transcendentals=0),
    )(*[a for a, _ in ins])


def fold(product):
    parts = [product[:, k : k + LANES] for k in range(0, product.shape[1], LANES)]
    return jnp.sum(functools.reduce(lambda a, b: a + b, parts), axis=0, keepdims=True)


def line_of(rows):
    tile = jnp.concatenate(rows + [jnp.zeros((8 - len(rows), LANES), F32)], axis=0)
    sums = jnp.sum(tile, axis=1, keepdims=True)
    row = lax.broadcasted_iota(jnp.int32, tile.shape, 0)
    lane = lax.broadcasted_iota(jnp.int32, tile.shape, 1)
    return jnp.sum(jnp.where(row == lane, sums, 0.0), axis=0, keepdims=True)


def add_rows(ref, start, step, count):
    return functools.reduce(lambda a, b: a + b, [ref[pl.ds(start + step * k, 1)] for k in range(count)])


def powers():
    lane = lax.broadcasted_iota(jnp.int32, (1, LANES), 1)
    up, down = jnp.ones((1, LANES), F32), jnp.ones((1, LANES), F32)
    for bit in range(7):
        chosen = (lane >> bit) % 2 == 1
        up = up * jnp.where(chosen, 2.0 ** (1 << bit), 1.0)
        down = down * jnp.where(chosen & (lane < LANES - 1), 2.0 ** -(1 << bit), 1.0)
    down = jnp.where(lane < LANES - 1, down, 0.0)
    return lane.astype(F32), up, down


def exponent_of(largest):
    _, up, down = powers()
    above = jnp.sum(jnp.where(up < largest, 1.0, 0.0), axis=1, keepdims=True)
    below = jnp.sum(jnp.where((down >= largest) & (down > 0.0), 1.0, 0.0), axis=1, keepdims=True)
    return jnp.clip(jnp.where(largest > 1.0, above, 1.0 - below), -126.0, 126.0)


def power(exponent):
    lane, up, down = powers()
    chosen = jnp.where(lane == exponent, up, 0.0)
    chosen = chosen + jnp.where((lane == -exponent) & (exponent < 0.0), down, 0.0)
    return jnp.sum(chosen, axis=1, keepdims=True)


def whole(values):
    return jnp.floor(values + 0.5)


def encode(block, line):
    largest = jnp.max(jnp.max(jnp.abs(block), axis=0, keepdims=True), axis=1, keepdims=True)
    exponent = exponent_of(largest)
    rows = [jnp.broadcast_to(exponent, line.shape)]
    block = whole(block * power(-exponent) * RANGE)
    exponent = exponent_of(jnp.max(jnp.abs(line), axis=1, keepdims=True))
    rows.append(jnp.broadcast_to(exponent, line.shape))
    rest = line * power(-exponent)
    for _ in range(3):
        rest = rest * DIGIT
        rows.append(whole(rest))
        rest = rest - rows[-1]
    rows.append(jnp.zeros((TILE - len(rows), LANES), F32))
    return jnp.concatenate([block] + rows, axis=0).astype(jnp.int32).astype(I16)


def decode(ref, count):
    size = ref.shape[1] - TILE
    tiles = [ref[j, size:].astype(jnp.int32).astype(F32) for j in range(count)]
    rows = [jnp.concatenate([tile[k : k + 1] for tile in tiles], axis=0) for k in range(5)]
    scales = power(rows[0][:, :1])
    blocks = [
        ref[j, :size].astype(jnp.int32).astype(F32) * (1.0 / RANGE) * scales[j : j + 1]
        for j in range(count)
    ]
    line = ((rows[4] / DIGIT + rows[3]) / DIGIT + rows[2]) / DIGIT * power(rows[1][:, :1])
    return blocks, jnp.sum(line, axis=0, keepdims=True)


def make(n_y, n_x, n_z):
    n_xy = n_y * n_x

    def per_device(psi, diag, block_dims, left_env, right_env):
        sectors, size, cols = psi.shape
        sub = cols // n_xy
        shard_rows = n_z * sub
        one = sub + 1
        scale = 1.0 / (size * size)
        core = lax.axis_index("core")
        swap = [(0, 1), (1, 0)]
        row = lax.broadcasted_iota(jnp.int32, (sectors + 2, 2), 0) - sectors
        col = lax.broadcasted_iota(jnp.int32, (sectors + 2, 2), 1)
        meta = jnp.where(
            row < 0,
            jnp.pad(block_dims, ((0, 2), (0, 0))),
            jnp.where(row > 0, lax.axis_index(XY), jnp.where(col == 0, core, lax.axis_index("sec"))),
        )
        share, shard = (size, cols), (sub, size)

        def a2a(array, axes):
            return lax.all_to_all(array, axes, 0, 0, tiled=True)

        def a2a_rows(array, parts, axes):
            blocks = array.reshape(parts, array.shape[0] // parts, 1, cols)
            return a2a(blocks, axes).reshape(array.shape)

        def dims_of(meta_ref, sector):
            return meta_ref[sector, 0], meta_ref[sector, 1]

        def place(meta_ref):
            return meta_ref[sectors, 0], meta_ref[sectors, 1], meta_ref[sectors + 1, 0]

        def share_mask(meta_ref, sector):
            row = lax.broadcasted_iota(jnp.int32, share, 0)
            col = lax.broadcasted_iota(jnp.int32, share, 1) + place(meta_ref)[1] * cols
            rows, columns = dims_of(meta_ref, sector)
            return (row < rows) & (col < columns)

        def own_rows(meta_ref, k):
            return pl.ds(pl.multiple_of(k * cols + place(meta_ref)[2] * sub, sub), sub)

        def start_kernel(meta_ref, psi_ref, out_ref, psi_a_ref):
            total = jnp.zeros((1, LANES), F32)
            for s in range(sectors):
                own = jnp.where(share_mask(meta_ref, s), psi_ref[s], 0.0)
                total = total + fold(own * own)

                @pl.when(place(meta_ref)[0] == s)
                def _():
                    psi_a_ref[...] = own

            for k in range(n_z):
                out_ref[pl.ds(k * one, sub)] = psi_a_ref[own_rows(meta_ref, k)]
                out_ref[pl.ds(k * one + sub, 1)] = total

        def left_matmul(meta_ref, env_ref, got_ref, field, left_ref):
            core, per = place(meta_ref)[0], PIECE // cols
            for i in range(size // PIECE):
                rows = pl.ds(i * PIECE, PIECE)
                for w in range(2):
                    env = env_ref[0, core, rows] if w == 0 else got_ref[rows]
                    part = jnp.dot(env, field, preferred_element_type=F32)
                    left_ref[i * per : (i + 1) * per, w] = part.astype(BF16).reshape(per, cols, cols)

        def first_kernel(meta_ref, got_ref, psi_a_ref, env_ref, env2_ref, u_a_ref, u_b_ref, left_ref):
            norm = jnp.sum(add_rows(got_ref, sub, one, n_z), axis=1, keepdims=True) * scale
            inverse = 1.0 / jnp.sqrt(norm)
            u_a = psi_a_ref[...] * inverse
            u_a_ref[...] = u_a
            for k in range(n_z):
                lanes = slice(k * cols, (k + 1) * cols)
                u_b_ref[:, lanes] = got_ref[pl.ds(k * one, sub)] * inverse
            left_matmul(meta_ref, env_ref, env2_ref, u_a.astype(BF16), left_ref)

        def right_pieces(meta_ref, moved_ref, env_ref, got_ref):
            core = place(meta_ref)[0]
            fields = [
                jnp.concatenate([moved_ref[k, w] for k in range(n_z)], axis=1) for w in range(2)
            ]
            for i in range(size // PIECE):
                rows = pl.ds(i * PIECE, PIECE)
                total = None
                for w in range(2):
                    env = env_ref[0, core, rows] if w == 0 else got_ref[rows]
                    part = lax.dot_general(
                        fields[w], env, (((1,), (1,)), ((), ())), preferred_element_type=F32
                    )
                    total = part if total is None else total + part
                yield rows, total

        def right_kernel(meta_ref, moved_ref, env_ref, got_ref, out_ref):
            for rows, total in right_pieces(meta_ref, moved_ref, env_ref, got_ref):
                out_ref[:, :, rows] = total.reshape(n_xy, sub, PIECE).astype(out_ref.dtype)

        def first_right_kernel(meta_ref, moved_ref, env_ref, got_ref, out_ref):
            parts = [total for _, total in right_pieces(meta_ref, moved_ref, env_ref, got_ref)]
            partial = jnp.concatenate(parts, axis=1)
            sizes = jnp.abs(partial)
            rows = [
                jnp.max(sizes[j * sub : (j + 1) * sub], axis=0, keepdims=True) for j in range(n_xy)
            ]
            exponents = exponent_of(jnp.max(jnp.concatenate(rows, axis=0), axis=1, keepdims=True))
            scales = power(-exponents)
            tiles = jnp.broadcast_to(exponents, (n_xy, cols))
            for j in range(n_xy):
                rows = partial[j * sub : (j + 1) * sub] * scales[j : j + 1] * RANGE
                rows = [rows[:, k * cols : (k + 1) * cols] for k in range(n_z)]
                tile = jnp.broadcast_to(tiles[j : j + 1], (TILE, cols))
                block = jnp.concatenate([whole(jnp.concatenate(rows, axis=0)), tile], axis=0)
                out_ref[j] = block.astype(jnp.int32).astype(I16)

        def first_sum(got_ref):
            tiles = [got_ref[j, shard_rows:].astype(jnp.int32).astype(F32) for j in range(n_xy)]
            scales = power(jnp.concatenate([tile[:1] for tile in tiles], axis=0)[:, :1])
            total = jnp.zeros((shard_rows, cols), F32)
            for j in range(n_xy):
                block = got_ref[j, :shard_rows].astype(jnp.int32).astype(F32)
                total = total + block * (1.0 / RANGE) * scales[j : j + 1]
            return jnp.concatenate([total[k * sub : (k + 1) * sub] for k in range(n_z)], axis=1)

        def image_of(meta_ref, image):
            core, z, q = place(meta_ref)
            row = lax.broadcasted_iota(jnp.int32, shard, 0) + (z * cols + q * sub)
            col = lax.broadcasted_iota(jnp.int32, shard, 1)
            rows, columns = dims_of(meta_ref, core)
            return jnp.where((row < rows) & (col < columns), image, 0.0)

        def dots_line(image, u_b_ref, more):
            u = u_b_ref[...]
            if not more:
                return line_of([fold(u * image)])
            corr, hu = more[0][...], more[1][...]
            pairs = [(u, image), (corr, hu), (corr, image), (u, corr), (corr, corr), (u, u)]
            return line_of([fold(a * b) for a, b in pairs])

        def first_image_kernel(meta_ref, got_ref, u_b_ref, diag_ref, image_ref, out_ref):
            image = image_of(meta_ref, first_sum(got_ref))
            image_ref[...] = image
            line = dots_line(image, u_b_ref, ())
            for k in range(n_z):
                for c in range(2):
                    shard_k = image[:, k * cols : (k + 1) * cols]
                    rows = jnp.where(place(meta_ref)[0] == c, shard_k, diag_ref[c, own_rows(meta_ref, k)])
                    out_ref[pl.ds((c * n_z + k) * one, sub)] = rows
                    out_ref[pl.ds((c * n_z + k) * one + sub, 1)] = line

        def image_kernel(meta_ref, got_ref, u_b_ref, corr_b_ref, hu_b_ref, image_ref, out_ref):
            image = image_of(meta_ref, jnp.sum(got_ref[...].astype(F32), axis=0))
            image_ref[...] = image
            line = dots_line(image, u_b_ref, (corr_b_ref, hu_b_ref))
            for k in range(2 * n_z):
                out_ref[pl.ds(k * one, sub)] = image[:, (k % n_z) * cols : (k % n_z + 1) * cols]
                out_ref[pl.ds(k * one + sub, 1)] = line

        def last_image_kernel(meta_ref, got_ref, u_b_ref, corr_b_ref, hu_b_ref, out_ref):
            image = image_of(meta_ref, jnp.sum(got_ref[...].astype(F32), axis=0))
            line = dots_line(image, u_b_ref, (corr_b_ref, hu_b_ref))
            out_ref[...] = jnp.broadcast_to(line, out_ref.shape)

        def from_cores(meta_ref, got_ref, k):
            zero, other = [got_ref[pl.ds((c * n_z + k) * one, sub)] for c in range(2)]
            first = place(meta_ref)[0] == 0
            return jnp.where(first, zero, other), jnp.where(first, other, zero)

        def spread_kernel(meta_ref, got_ref, out_ref, *diag_b_ref):
            line = add_rows(got_ref, sub, one, 2 * n_z)
            shards = []
            for k in range(n_z):
                rows, far = from_cores(meta_ref, got_ref, k)
                shards.append(rows)
                for ref in diag_b_ref:
                    ref[:, k * cols : (k + 1) * cols] = far
            block = encode(jnp.concatenate(shards, axis=0), line)
            out_ref[...] = jnp.broadcast_to(block[None], out_ref.shape)

        def projected(theta, sums):
            u_image, corr_hu, corr_image, project, size_corr, size_u = sums
            inverse = 1.0 / jnp.sqrt(size_corr - project * project * (2.0 - size_u))
            cross = 0.5 * ((u_image - project * theta) + (corr_hu - project * theta)) * inverse
            corner = corr_image - project * (corr_hu + u_image) + project * project * theta
            corner = corner * inverse * inverse
            half = 0.5 * (theta - corner)
            lowest = 0.5 * (theta + corner) - jnp.sqrt(half * half + cross * cross)
            x, y = corner - lowest, -cross
            length = jnp.sqrt(x * x + y * y)
            x, y = x / length, y / length
            theta = x * x * theta + 2.0 * x * y * cross + y * y * corner
            return x - y * project * inverse, y * inverse, theta, lowest

        def correction(theta, image, vector, diagonal):
            return (image - theta * vector) / (1.0 + jnp.abs(diagonal - theta))

        def share_of(parts):
            parts = [part.reshape(n_z, 1, sub, cols) for part in parts]
            return jnp.concatenate(parts, axis=1).reshape(share)

        def begin_kernel(meta_ref, got_ref, u_a_ref, u_b_ref, hu_b_ref, diag_ref, diag_b_ref, env_ref, env2_ref, hu_a_ref, corr_a_ref, corr_b_ref, theta_ref, left_ref):
            blocks, line = decode(got_ref, n_xy)
            theta = line[:, :1] * scale
            theta_ref[...] = jnp.broadcast_to(theta, theta_ref.shape)
            hu_a = share_of(blocks)
            hu_a_ref[...] = hu_a
            corr_a = correction(theta, hu_a, u_a_ref[...], diag_ref[place(meta_ref)[0]])
            corr_a_ref[...] = corr_a
            corr_b_ref[...] = correction(theta, hu_b_ref[...], u_b_ref[...], diag_b_ref[...])
            left_matmul(meta_ref, env_ref, env2_ref, corr_a.astype(BF16), left_ref)

        def update_kernel(meta_ref, got_ref, old_theta_ref, u_a_ref, corr_a_ref, hu_a_ref, u_b_ref, corr_b_ref, hu_b_ref, hc_b_ref, diag_ref, diag_b_ref, env_ref, env2_ref, pair_out, u_b_out, corr_b_out, hu_b_out, theta_ref, left_ref, *hu_a_out):
            blocks, line = decode(got_ref, n_xy)
            sums = [line[:, k : k + 1] * scale for k in range(6)]
            old, new, theta, _ = projected(old_theta_ref[0:1, 0:1], sums)
            theta_ref[...] = jnp.broadcast_to(theta, theta_ref.shape)
            u_a = old * u_a_ref[...] + new * corr_a_ref[...]
            hu_a = old * hu_a_ref[...] + new * share_of(blocks)
            corr_a = correction(theta, hu_a, u_a, diag_ref[place(meta_ref)[0]])
            pair_out[0], pair_out[1] = u_a, corr_a
            for ref in hu_a_out:
                ref[...] = hu_a
            u_b = old * u_b_ref[...] + new * corr_b_ref[...]
            hu_b = old * hu_b_ref[...] + new * hc_b_ref[...]
            u_b_out[...], hu_b_out[...] = u_b, hu_b
            corr_b_out[...] = correction(theta, hu_b, u_b, diag_b_ref[...])
            left_matmul(meta_ref, env_ref, env2_ref, corr_a.astype(BF16), left_ref)

        def last_kernel(meta_ref, got_ref, theta_ref, pair_ref, far_ref, out_ref, energy_ref):
            line = jnp.sum(got_ref[...], axis=0, keepdims=True) * scale
            sums = [line[:, k : k + 1] for k in range(6)]
            old, new, _, lowest = projected(theta_ref[0:1, 0:1], sums)
            c = place(meta_ref)[0]
            energy_ref[...] = lowest
            out_ref[c] = old * pair_ref[0] + new * pair_ref[1]
            out_ref[1 - c] = old * far_ref[0] + new * far_ref[1]

        def v(*arrays):
            return [(a, VMEM) for a in arrays]

        i_meta = [(meta, SMEM)]
        left_out = ((n_z, 2, cols, cols), BF16)
        tile_out, a_out, b_out = ((8, cols), F32), (share, F32), (shard, F32)
        work = 4 * size * size * cols

        first, psi_a = call(
            start_kernel, [((n_z * one, cols), F32), a_out], i_meta + v(psi), (), START
        )

        def swapped(env, other):
            give = lax.dynamic_slice(
                env, (0, other, 0, 0), (1, 1, size, size), allow_negative_indices=False
            )
            return lax.ppermute(give.reshape(size, size), "core", swap)

        first, left_env, other = lax.optimization_barrier((first, left_env, 1 - core))
        lefts = v(left_env, swapped(left_env, other))
        first = a2a_rows(first, n_z, "sec")
        u_a, u_b, left = call(
            first_kernel, [a_out, b_out, left_out], i_meta + v(first, psi_a) + lefts, (), work
        )
        left, right_env = lax.optimization_barrier((left, right_env))
        rights = v(right_env, swapped(right_env, other))

        gathered = ((n_xy, shard_rows + TILE, cols), I16)

        def apply_right(left, kernel, out):
            moved = a2a(left, "sec")
            (partial,) = call(kernel, [out], i_meta + v(moved) + rights, (), work)
            return a2a(partial, XY)

        summed = ((n_xy, sub, size), BF16)
        payload_out = ((2 * n_z * one, cols), F32)
        got = apply_right(left, first_right_kernel, gathered)
        hu_b, payload = call(
            first_image_kernel,
            [b_out, payload_out],
            i_meta + v(got, u_b, diag),
        )
        payload, diag_b = call(
            spread_kernel, [gathered, b_out], i_meta + v(a2a_rows(payload, 2 * n_z, CZ))
        )
        got = a2a(payload, XY)
        hu_a, corr_a, corr_b, theta, left = call(
            begin_kernel,
            [a_out, a_out, b_out, tile_out, left_out],
            i_meta + v(got, u_a, u_b, hu_b, diag, diag_b) + lefts, (), work,
        )
        for step in range(ITERS - 1):
            got = apply_right(left, right_kernel, summed)
            hc_b, payload = call(
                image_kernel, [b_out, payload_out], i_meta + v(got, u_b, corr_b, hu_b)
            )
            (payload,) = call(
                spread_kernel, [gathered], i_meta + v(a2a_rows(payload, 2 * n_z, CZ))
            )
            got = a2a(payload, XY)
            more = [a_out] * (step < ITERS - 2)
            pair, u_b, corr_b, hu_b, theta, left, *more = call(
                update_kernel,
                [((2, *share), F32), b_out, b_out, b_out, tile_out, left_out] + more,
                i_meta + v(got, theta, u_a, corr_a, hu_a, u_b, corr_b, hu_b, hc_b, diag, diag_b) + lefts,
                (), work,
            )
            (hu_a,) = more or (None,)
            u_a, corr_a = pair[0], pair[1]
        got = apply_right(left, right_kernel, summed)
        got, pair = lax.optimization_barrier((got, pair))
        far = lax.ppermute(pair, "core", swap)
        (sums,) = call(
            last_image_kernel, [((2 * n_z * n_xy, cols), F32)], i_meta + v(got, u_b, corr_b, hu_b)
        )
        sums = a2a(sums, ALL)
        out, energy = call(
            last_kernel, [(psi.shape, F32), ((1, 1), F32)],
            i_meta + v(sums, theta, pair, far),
        )
        return out, energy.reshape(())

    return per_device


def solution(mesh):
    n_z = mesh.shape["sec"]
    n_y = n_x = int(round((mesh.shape["term"] // 2) ** 0.5))
    fine = Mesh(mesh.devices.reshape(n_y, n_x, 2, n_z), ("y", "x", "core", "sec"))
    term = ("y", "x", "core")
    in_specs = (
        P(None, None, "sec"),
        P(None, None, "sec"),
        P(),
        P(term, None, None, None),
        P(term, None, None, None),
    )
    out_specs = (P(None, None, "sec"), P())
    return jax.shard_map(
        make(n_y, n_x, n_z), mesh=fine, in_specs=in_specs, out_specs=out_specs, check_vma=False
    )
```

```python
import functools

import jax
import jax.numpy as jnp
from jax import lax
from jax.experimental import pallas as pl
from jax.experimental.pallas import tpu as pltpu
from jax.sharding import Mesh, PartitionSpec as P

ITERS = 2
XY = ("y", "x")
CZ = ("core", "sec")
ALL = ("core", "sec", "y", "x")
LANES = 128
PIECE = 1024
TILE = 16
RANGE = 32000.0
DIGIT = 2.0**14
I16 = jnp.int16
LIMIT = 24
START = 4 * 10**9
F32 = jnp.float32
BF16 = jnp.bfloat16
SMEM = pl.BlockSpec(memory_space=pltpu.SMEM)
VMEM = pl.BlockSpec(memory_space=pltpu.VMEM)


def call(kernel, outs, ins, scratch=(), flops=0):
    moved = sum(int(a.size) * a.dtype.itemsize for a, _ in ins)
    return pl.pallas_call(
        kernel,
        out_shape=[jax.ShapeDtypeStruct(s, d) for s, d in outs],
        in_specs=[s for _, s in ins],
        out_specs=[VMEM] * len(outs),
        scratch_shapes=list(scratch),
        compiler_params=pltpu.CompilerParams(vmem_limit_bytes=LIMIT * 2**20),
        cost_estimate=pl.CostEstimate(flops=flops, bytes_accessed=moved, transcendentals=0),
    )(*[a for a, _ in ins])


def fold(product):
    parts = [product[:, k : k + LANES] for k in range(0, product.shape[1], LANES)]
    return jnp.sum(functools.reduce(lambda a, b: a + b, parts), axis=0, keepdims=True)


def line_of(rows):
    tile = jnp.concatenate(rows + [jnp.zeros((8 - len(rows), LANES), F32)], axis=0)
    sums = jnp.sum(tile, axis=1, keepdims=True)
    row = lax.broadcasted_iota(jnp.int32, tile.shape, 0)
    lane = lax.broadcasted_iota(jnp.int32, tile.shape, 1)
    return jnp.sum(jnp.where(row == lane, sums, 0.0), axis=0, keepdims=True)


def add_rows(ref, start, step, count):
    return functools.reduce(lambda a, b: a + b, [ref[pl.ds(start + step * k, 1)] for k in range(count)])


def powers():
    lane = lax.broadcasted_iota(jnp.int32, (1, LANES), 1)
    up, down = jnp.ones((1, LANES), F32), jnp.ones((1, LANES), F32)
    for bit in range(7):
        chosen = (lane >> bit) % 2 == 1
        up = up * jnp.where(chosen, 2.0 ** (1 << bit), 1.0)
        down = down * jnp.where(chosen & (lane < LANES - 1), 2.0 ** -(1 << bit), 1.0)
    down = jnp.where(lane < LANES - 1, down, 0.0)
    return lane.astype(F32), up, down


def exponent_of(largest):
    _, up, down = powers()
    above = jnp.sum(jnp.where(up < largest, 1.0, 0.0), axis=1, keepdims=True)
    below = jnp.sum(jnp.where((down >= largest) & (down > 0.0), 1.0, 0.0), axis=1, keepdims=True)
    return jnp.clip(jnp.where(largest > 1.0, above, 1.0 - below), -126.0, 126.0)


def power(exponent):
    lane, up, down = powers()
    chosen = jnp.where(lane == exponent, up, 0.0)
    chosen = chosen + jnp.where((lane == -exponent) & (exponent < 0.0), down, 0.0)
    return jnp.sum(chosen, axis=1, keepdims=True)


def whole(values):
    return jnp.floor(values + 0.5)


def encode(block, line):
    largest = jnp.max(jnp.max(jnp.abs(block), axis=0, keepdims=True), axis=1, keepdims=True)
    exponent = exponent_of(largest)
    rows = [jnp.broadcast_to(exponent, line.shape)]
    block = whole(block * power(-exponent) * RANGE)
    exponent = exponent_of(jnp.max(jnp.abs(line), axis=1, keepdims=True))
    rows.append(jnp.broadcast_to(exponent, line.shape))
    rest = line * power(-exponent)
    for _ in range(3):
        rest = rest * DIGIT
        rows.append(whole(rest))
        rest = rest - rows[-1]
    rows.append(jnp.zeros((TILE - len(rows), LANES), F32))
    return jnp.concatenate([block] + rows, axis=0).astype(I16)


def decode(ref, count):
    size = ref.shape[1] - TILE
    tiles = [ref[j, size:].astype(F32) for j in range(count)]
    rows = [jnp.concatenate([tile[k : k + 1] for tile in tiles], axis=0) for k in range(5)]
    scales = power(rows[0][:, :1])
    blocks = [
        ref[j, :size].astype(F32) * (1.0 / RANGE) * scales[j : j + 1]
        for j in range(count)
    ]
    line = ((rows[4] / DIGIT + rows[3]) / DIGIT + rows[2]) / DIGIT * power(rows[1][:, :1])
    return blocks, jnp.sum(line, axis=0, keepdims=True)


def make(n_y, n_x, n_z):
    n_xy = n_y * n_x

    def per_device(psi, diag, block_dims, left_env, right_env):
        sectors, size, cols = psi.shape
        sub = cols // n_xy
        shard_rows = n_z * sub
        one = sub + 1
        scale = 1.0 / (size * size)
        core = lax.axis_index("core")
        swap = [(0, 1), (1, 0)]
        row = lax.broadcasted_iota(jnp.int32, (sectors + 2, 2), 0) - sectors
        col = lax.broadcasted_iota(jnp.int32, (sectors + 2, 2), 1)
        meta = jnp.where(
            row < 0,
            jnp.pad(block_dims, ((0, 2), (0, 0))),
            jnp.where(row > 0, lax.axis_index(XY), jnp.where(col == 0, core, lax.axis_index("sec"))),
        )
        share, shard = (size, cols), (sub, size)

        def a2a(array, axes):
            return lax.all_to_all(array, axes, 0, 0, tiled=True)

        def a2a_rows(array, parts, axes):
            blocks = array.reshape(parts, array.shape[0] // parts, 1, cols)
            return a2a(blocks, axes).reshape(array.shape)

        def dims_of(meta_ref, sector):
            return meta_ref[sector, 0], meta_ref[sector, 1]

        def place(meta_ref):
            return meta_ref[sectors, 0], meta_ref[sectors, 1], meta_ref[sectors + 1, 0]

        def share_mask(meta_ref, sector):
            row = lax.broadcasted_iota(jnp.int32, share, 0)
            col = lax.broadcasted_iota(jnp.int32, share, 1) + place(meta_ref)[1] * cols
            rows, columns = dims_of(meta_ref, sector)
            return (row < rows) & (col < columns)

        def own_rows(meta_ref, k):
            return pl.ds(pl.multiple_of(k * cols + place(meta_ref)[2] * sub, sub), sub)

        def start_kernel(meta_ref, psi_ref, out_ref, psi_a_ref):
            total = jnp.zeros((1, LANES), F32)
            for s in range(sectors):
                own = jnp.where(share_mask(meta_ref, s), psi_ref[s], 0.0)
                total = total + fold(own * own)

                @pl.when(place(meta_ref)[0] == s)
                def _():
                    psi_a_ref[...] = own

            for k in range(n_z):
                out_ref[pl.ds(k * one, sub)] = psi_a_ref[own_rows(meta_ref, k)]
                out_ref[pl.ds(k * one + sub, 1)] = total

        def left_matmul(meta_ref, env_ref, got_ref, field, left_ref):
            core, per = place(meta_ref)[0], PIECE // cols
            for i in range(size // PIECE):
                rows = pl.ds(i * PIECE, PIECE)
                for w in range(2):
                    env = env_ref[0, core, rows] if w == 0 else got_ref[rows]
                    part = jnp.dot(env, field, preferred_element_type=F32)
                    left_ref[i * per : (i + 1) * per, w] = part.astype(BF16).reshape(per, cols, cols)

        def first_kernel(meta_ref, got_ref, psi_a_ref, env_ref, env2_ref, u_a_ref, u_b_ref, left_ref):
            norm = jnp.sum(add_rows(got_ref, sub, one, n_z), axis=1, keepdims=True) * scale
            inverse = 1.0 / jnp.sqrt(norm)
            u_a = psi_a_ref[...] * inverse
            u_a_ref[...] = u_a
            for k in range(n_z):
                lanes = slice(k * cols, (k + 1) * cols)
                u_b_ref[:, lanes] = got_ref[pl.ds(k * one, sub)] * inverse
            left_matmul(meta_ref, env_ref, env2_ref, u_a.astype(BF16), left_ref)

        def right_pieces(meta_ref, moved_ref, env_ref, got_ref):
            core = place(meta_ref)[0]
            fields = [
                jnp.concatenate([moved_ref[k, w] for k in range(n_z)], axis=1) for w in range(2)
            ]
            for i in range(size // PIECE):
                rows = pl.ds(i * PIECE, PIECE)
                total = None
                for w in range(2):
                    env = env_ref[0, core, rows] if w == 0 else got_ref[rows]
                    part = lax.dot_general(
                        fields[w], env, (((1,), (1,)), ((), ())), preferred_element_type=F32
                    )
                    total = part if total is None else total + part
                yield rows, total

        def right_kernel(meta_ref, moved_ref, env_ref, got_ref, out_ref):
            for rows, total in right_pieces(meta_ref, moved_ref, env_ref, got_ref):
                out_ref[:, :, rows] = total.reshape(n_xy, sub, PIECE).astype(out_ref.dtype)

        def first_right_kernel(meta_ref, moved_ref, env_ref, got_ref, out_ref):
            parts = [total for _, total in right_pieces(meta_ref, moved_ref, env_ref, got_ref)]
            partial = jnp.concatenate(parts, axis=1)
            sizes = jnp.abs(partial)
            rows = [
                jnp.max(sizes[j * sub : (j + 1) * sub], axis=0, keepdims=True) for j in range(n_xy)
            ]
            exponents = exponent_of(jnp.max(jnp.concatenate(rows, axis=0), axis=1, keepdims=True))
            scales = power(-exponents)
            tiles = jnp.broadcast_to(exponents, (n_xy, cols))
            for j in range(n_xy):
                rows = partial[j * sub : (j + 1) * sub] * scales[j : j + 1] * RANGE
                rows = [rows[:, k * cols : (k + 1) * cols] for k in range(n_z)]
                tile = jnp.broadcast_to(tiles[j : j + 1], (TILE, cols))
                block = jnp.concatenate([whole(jnp.concatenate(rows, axis=0)), tile], axis=0)
                out_ref[j] = block.astype(I16)

        def first_sum(got_ref):
            tiles = [got_ref[j, shard_rows:].astype(F32) for j in range(n_xy)]
            scales = power(jnp.concatenate([tile[:1] for tile in tiles], axis=0)[:, :1])
            total = jnp.zeros((shard_rows, cols), F32)
            for j in range(n_xy):
                block = got_ref[j, :shard_rows].astype(F32)
                total = total + block * (1.0 / RANGE) * scales[j : j + 1]
            return jnp.concatenate([total[k * sub : (k + 1) * sub] for k in range(n_z)], axis=1)

        def image_of(meta_ref, image):
            core, z, q = place(meta_ref)
            row = lax.broadcasted_iota(jnp.int32, shard, 0) + (z * cols + q * sub)
            col = lax.broadcasted_iota(jnp.int32, shard, 1)
            rows, columns = dims_of(meta_ref, core)
            return jnp.where((row < rows) & (col < columns), image, 0.0)

        def dots_line(image, u_b_ref, more):
            u = u_b_ref[...]
            if not more:
                return line_of([fold(u * image)])
            corr, hu = more[0][...], more[1][...]
            pairs = [(u, image), (corr, hu), (corr, image), (u, corr), (corr, corr), (u, u)]
            return line_of([fold(a * b) for a, b in pairs])

        def first_image_kernel(meta_ref, got_ref, u_b_ref, diag_ref, image_ref, out_ref):
            image = image_of(meta_ref, first_sum(got_ref))
            image_ref[...] = image
            line = dots_line(image, u_b_ref, ())
            for k in range(n_z):
                for c in range(2):
                    shard_k = image[:, k * cols : (k + 1) * cols]
                    rows = jnp.where(place(meta_ref)[0] == c, shard_k, diag_ref[c, own_rows(meta_ref, k)])
                    out_ref[pl.ds((c * n_z + k) * one, sub)] = rows
                    out_ref[pl.ds((c * n_z + k) * one + sub, 1)] = line

        def image_kernel(meta_ref, got_ref, u_b_ref, corr_b_ref, hu_b_ref, image_ref, out_ref):
            image = image_of(meta_ref, jnp.sum(got_ref[...].astype(F32), axis=0))
            image_ref[...] = image
            line = dots_line(image, u_b_ref, (corr_b_ref, hu_b_ref))
            for k in range(2 * n_z):
                out_ref[pl.ds(k * one, sub)] = image[:, (k % n_z) * cols : (k % n_z + 1) * cols]
                out_ref[pl.ds(k * one + sub, 1)] = line

        def last_image_kernel(meta_ref, got_ref, u_b_ref, corr_b_ref, hu_b_ref, out_ref):
            image = image_of(meta_ref, jnp.sum(got_ref[...].astype(F32), axis=0))
            line = dots_line(image, u_b_ref, (corr_b_ref, hu_b_ref))
            out_ref[...] = jnp.broadcast_to(line, out_ref.shape)

        def from_cores(meta_ref, got_ref, k):
            zero, other = [got_ref[pl.ds((c * n_z + k) * one, sub)] for c in range(2)]
            first = place(meta_ref)[0] == 0
            return jnp.where(first, zero, other), jnp.where(first, other, zero)

        def spread_kernel(meta_ref, got_ref, out_ref, *diag_b_ref):
            line = add_rows(got_ref, sub, one, 2 * n_z)
            shards = []
            for k in range(n_z):
                rows, far = from_cores(meta_ref, got_ref, k)
                shards.append(rows)
                for ref in diag_b_ref:
                    ref[:, k * cols : (k + 1) * cols] = far
            block = encode(jnp.concatenate(shards, axis=0), line)
            out_ref[...] = jnp.broadcast_to(block[None], out_ref.shape)

        def projected(theta, sums):
            u_image, corr_hu, corr_image, project, size_corr, size_u = sums
            inverse = 1.0 / jnp.sqrt(size_corr - project * project * (2.0 - size_u))
            cross = 0.5 * ((u_image - project * theta) + (corr_hu - project * theta)) * inverse
            corner = corr_image - project * (corr_hu + u_image) + project * project * theta
            corner = corner * inverse * inverse
            half = 0.5 * (theta - corner)
            lowest = 0.5 * (theta + corner) - jnp.sqrt(half * half + cross * cross)
            x, y = corner - lowest, -cross
            length = jnp.sqrt(x * x + y * y)
            x, y = x / length, y / length
            theta = x * x * theta + 2.0 * x * y * cross + y * y * corner
            return x - y * project * inverse, y * inverse, theta, lowest

        def correction(theta, image, vector, diagonal):
            return (image - theta * vector) / (1.0 + jnp.abs(diagonal - theta))

        def share_of(parts):
            parts = [part.reshape(n_z, 1, sub, cols) for part in parts]
            return jnp.concatenate(parts, axis=1).reshape(share)

        def begin_kernel(meta_ref, got_ref, u_a_ref, u_b_ref, hu_b_ref, diag_ref, diag_b_ref, env_ref, env2_ref, hu_a_ref, corr_a_ref, corr_b_ref, theta_ref, left_ref):
            blocks, line = decode(got_ref, n_xy)
            theta = line[:, :1] * scale
            theta_ref[...] = jnp.broadcast_to(theta, theta_ref.shape)
            hu_a = share_of(blocks)
            hu_a_ref[...] = hu_a
            corr_a = correction(theta, hu_a, u_a_ref[...], diag_ref[place(meta_ref)[0]])
            corr_a_ref[...] = corr_a
            corr_b_ref[...] = correction(theta, hu_b_ref[...], u_b_ref[...], diag_b_ref[...])
            left_matmul(meta_ref, env_ref, env2_ref, corr_a.astype(BF16), left_ref)

        def update_kernel(meta_ref, got_ref, old_theta_ref, u_a_ref, corr_a_ref, hu_a_ref, u_b_ref, corr_b_ref, hu_b_ref, hc_b_ref, diag_ref, diag_b_ref, env_ref, env2_ref, pair_out, u_b_out, corr_b_out, hu_b_out, theta_ref, left_ref, *hu_a_out):
            blocks, line = decode(got_ref, n_xy)
            sums = [line[:, k : k + 1] * scale for k in range(6)]
            old, new, theta, _ = projected(old_theta_ref[0:1, 0:1], sums)
            theta_ref[...] = jnp.broadcast_to(theta, theta_ref.shape)
            u_a = old * u_a_ref[...] + new * corr_a_ref[...]
            hu_a = old * hu_a_ref[...] + new * share_of(blocks)
            corr_a = correction(theta, hu_a, u_a, diag_ref[place(meta_ref)[0]])
            pair_out[0], pair_out[1] = u_a, corr_a
            for ref in hu_a_out:
                ref[...] = hu_a
            u_b = old * u_b_ref[...] + new * corr_b_ref[...]
            hu_b = old * hu_b_ref[...] + new * hc_b_ref[...]
            u_b_out[...], hu_b_out[...] = u_b, hu_b
            corr_b_out[...] = correction(theta, hu_b, u_b, diag_b_ref[...])
            left_matmul(meta_ref, env_ref, env2_ref, corr_a.astype(BF16), left_ref)

        def last_kernel(meta_ref, got_ref, theta_ref, pair_ref, far_ref, out_ref, energy_ref):
            line = jnp.sum(got_ref[...], axis=0, keepdims=True) * scale
            sums = [line[:, k : k + 1] for k in range(6)]
            old, new, _, lowest = projected(theta_ref[0:1, 0:1], sums)
            c = place(meta_ref)[0]
            energy_ref[...] = lowest
            out_ref[c] = old * pair_ref[0] + new * pair_ref[1]
            out_ref[1 - c] = old * far_ref[0] + new * far_ref[1]

        def v(*arrays):
            return [(a, VMEM) for a in arrays]

        i_meta = [(meta, SMEM)]
        left_out = ((n_z, 2, cols, cols), BF16)
        tile_out, a_out, b_out = ((8, cols), F32), (share, F32), (shard, F32)
        work = 4 * size * size * cols

        first, psi_a = call(
            start_kernel, [((n_z * one, cols), F32), a_out], i_meta + v(psi), (), START
        )

        def swapped(env, other):
            give = lax.dynamic_slice(
                env, (0, other, 0, 0), (1, 1, size, size), allow_negative_indices=False
            )
            return lax.ppermute(give.reshape(size, size), "core", swap)

        first, left_env, other = lax.optimization_barrier((first, left_env, 1 - core))
        lefts = v(left_env, swapped(left_env, other))
        first = a2a_rows(first, n_z, "sec")
        u_a, u_b, left = call(
            first_kernel, [a_out, b_out, left_out], i_meta + v(first, psi_a) + lefts, (), work
        )
        left, right_env = lax.optimization_barrier((left, right_env))
        rights = v(right_env, swapped(right_env, other))

        gathered = ((n_xy, shard_rows + TILE, cols), I16)

        def apply_right(left, kernel, out):
            moved = a2a(left, "sec")
            (partial,) = call(kernel, [out], i_meta + v(moved) + rights, (), work)
            return a2a(partial, XY)

        summed = ((n_xy, sub, size), BF16)
        payload_out = ((2 * n_z * one, cols), F32)
        got = apply_right(left, first_right_kernel, gathered)
        hu_b, payload = call(
            first_image_kernel,
            [b_out, payload_out],
            i_meta + v(got, u_b, diag),
        )
        payload, diag_b = call(
            spread_kernel, [gathered, b_out], i_meta + v(a2a_rows(payload, 2 * n_z, CZ))
        )
        got = a2a(payload, XY)
        hu_a, corr_a, corr_b, theta, left = call(
            begin_kernel,
            [a_out, a_out, b_out, tile_out, left_out],
            i_meta + v(got, u_a, u_b, hu_b, diag, diag_b) + lefts, (), work,
        )
        for step in range(ITERS - 1):
            got = apply_right(left, right_kernel, summed)
            hc_b, payload = call(
                image_kernel, [b_out, payload_out], i_meta + v(got, u_b, corr_b, hu_b)
            )
            (payload,) = call(
                spread_kernel, [gathered], i_meta + v(a2a_rows(payload, 2 * n_z, CZ))
            )
            got = a2a(payload, XY)
            more = [a_out] * (step < ITERS - 2)
            pair, u_b, corr_b, hu_b, theta, left, *more = call(
                update_kernel,
                [((2, *share), F32), b_out, b_out, b_out, tile_out, left_out] + more,
                i_meta + v(got, theta, u_a, corr_a, hu_a, u_b, corr_b, hu_b, hc_b, diag, diag_b) + lefts,
                (), work,
            )
            (hu_a,) = more or (None,)
            u_a, corr_a = pair[0], pair[1]
        got = apply_right(left, right_kernel, summed)
        got, pair = lax.optimization_barrier((got, pair))
        far = lax.ppermute(pair, "core", swap)
        (sums,) = call(
            last_image_kernel, [((2 * n_z * n_xy, cols), F32)], i_meta + v(got, u_b, corr_b, hu_b)
        )
        sums = a2a(sums, ALL)
        out, energy = call(
            last_kernel, [(psi.shape, F32), ((1, 1), F32)],
            i_meta + v(sums, theta, pair, far),
        )
        return out, energy.reshape(())

    return per_device


def solution(mesh):
    n_z = mesh.shape["sec"]
    n_y = n_x = int(round((mesh.shape["term"] // 2) ** 0.5))
    fine = Mesh(mesh.devices.reshape(n_y, n_x, 2, n_z), ("y", "x", "core", "sec"))
    term = ("y", "x", "core")
    in_specs = (
        P(None, None, "sec"),
        P(None, None, "sec"),
        P(),
        P(term, None, None, None),
        P(term, None, None, None),
    )
    out_specs = (P(None, None, "sec"), P())
    return jax.shard_map(
        make(n_y, n_x, n_z), mesh=fine, in_specs=in_specs, out_specs=out_specs, check_vma=False
    )
```
